32 devices in a mesh: slab: 8 (over y, x, core), grp: 4 (over z).
Axes of the slice: x: 2, y: 2, z: 4, core: 2. Of those that a mesh axis runs over, the one named last changes fastest.
Arguments:
- source: float32 [3, 256, 2048], P(None, 'slab', 'grp'), may hold values from -8 to 8
- conductivity: float32 [3, 256, 2048], P(None, 'slab', 'grp'), may hold values from 0.1 to 10
- leakance: float32 [2, 256, 2048], P(None, 'slab', 'grp'), may hold values from 0.05 to 5
- storage: float32 [3, 256, 2048], P(None, 'slab', 'grp'), may hold values from 0.1 to 1
- et_rate: float32 [256, 2048], P('slab', 'grp'), may hold values from 0.05 to 1
- zone_of_block: int32 [32, 256], P('slab', 'grp'), may hold values from 0 to 255
- zone_recharge: float32 [256], replicated, may hold values from -4 to 4
- zone_weight: float32 [256], replicated, may hold values from 0.25 to 4
- pair_zones: int32 [512, 2], replicated, may hold values from 0 to 255, as said below
- pair_weight: float32 [512], replicated, may hold values from 0.25 to 4
Outputs:
- solution: float32 [3, 256, 2048], P(None, 'slab', 'grp')
- residual: float32 [3, 256, 2048], P(None, 'slab', 'grp')
The draws below stay inside these ranges and needn't reach their ends.
Inputs may be any that keep to these rules, and one draw needn't show every extreme that they name: `pair_zones`: each row names two different zones; every zone is the first entry of some row.
All inputs are finite; a program needn't handle non-finite values.
Results may differ from the reference program's by a relative error of at most 0.00017.
Values sent between devices are 32-bit elements; how exact they have to be, the bound alone decides.
No kernel may reach another device: no remote copies, remote signals or barrier semaphores. Data moves between devices by JAX's collectives and lax.ppermute only.
A program may use at most 64 MiB of HBM per device.

```python
import math
import jax
import jax.numpy as jnp
from jax import lax

LAYERS = 3
ITERS = 3
ZONES = 256
PAIRS = 512
NX = 256
NY = 2048


def draw_source(key, part):
    key = jax.random.fold_in(key, 5)
    ramp_scale = 1.0 + 2.0 * lax.broadcasted_iota(jnp.float32, (LAYERS, NX, NY), 1) / NX
    noise_part = jax.random.normal(key, (LAYERS, NX, NY), jnp.float32)
    values = noise_part * ramp_scale
    return jnp.clip(values, -8.0, 8.0)


def draw_pair_zones(key, part):
    key = jax.random.fold_in(key, 7)
    first_key, second_key = jax.random.split(key)
    leading = jax.random.permutation(first_key, jnp.arange(PAIRS, dtype=jnp.int32) % ZONES)
    offsets = jax.random.randint(second_key, (PAIRS,), 1, ZONES, dtype=jnp.int32)
    partner = (leading + offsets) % ZONES
    return jnp.stack([leading, partner], axis=1).astype(jnp.int32)


def with_ends(drawn, key, smallest, high):
    spot = [jax.random.randint(jax.random.fold_in(key, axis), (), 0, length) for axis, length in enumerate(drawn.shape)]
    widest = drawn.shape.index(max(drawn.shape))
    next_to = spot[:widest] + [(spot[widest] + 1) % drawn.shape[widest]] + spot[widest + 1:]
    return drawn.at[tuple(spot)].set(smallest).at[tuple(next_to)].set(high)


def steps_of(own_key, extent, shards, smallest, largest):
    level, own = 1.0, jax.random.fold_in(own_key, 6)
    for dim, blocks in shards:
        draws = jnp.exp(jax.random.uniform(jax.random.fold_in(own, dim), (blocks,), jnp.float32, smallest / len(shards), largest / len(shards)))
        level = level * jnp.repeat(draws, extent[dim] // blocks).reshape([-1 if axis == dim else 1 for axis in range(len(extent))])
    return level


def noise(own_key, extent, deviation, most, kind=jnp.bfloat16):
    return jnp.clip(deviation * jax.random.normal(own_key, extent, jnp.float32), -most, most).astype(kind)


def setup_inputs(seed: int = 0) -> dict:
    key_list = jax.random.split(jax.random.key(seed), 11)
    source = draw_source(jax.random.fold_in(key_list[10], 71), 0)
    conductivity = jnp.clip(jnp.exp(math.log(10.0) - 4.6051702 * jax.random.uniform(key_list[1], (LAYERS, NX, NY), jnp.float32) ** steps_of(key_list[1], (LAYERS, NX, NY), ((1, 8), (2, 4)), -0.2, 0.2)), 0.1, 10.0)
    leakance = jnp.clip(jnp.exp(math.log(5.0) - 4.6051702 * jax.random.uniform(key_list[2], (LAYERS - 1, NX, NY), jnp.float32) ** steps_of(key_list[2], (LAYERS - 1, NX, NY), ((1, 8), (2, 4)), -0.2, 0.2)), 0.05, 5.0)
    storage = jnp.clip(jnp.exp(math.log(1.0) - 2.3025851 * jax.random.uniform(key_list[3], (LAYERS, NX, NY), jnp.float32) ** steps_of(key_list[3], (LAYERS, NX, NY), ((1, 8), (2, 4)), -0.2, 0.2)), 0.1, 1.0)
    et_rate = jnp.clip(jnp.exp(math.log(1.0) - 2.9957323 * jax.random.uniform(key_list[4], (NX, NY), jnp.float32) ** steps_of(key_list[4], (NX, NY), ((0, 8), (1, 4)), -0.2, 0.2)), 0.05, 1.0)
    zone_of_block = with_ends(jax.random.randint(key_list[5], (NX // 8, NY // 8), 0, ZONES), jax.random.fold_in(key_list[5], 1), 0, ZONES - 1).astype(jnp.int32)
    zone_recharge = noise(key_list[6], (ZONES,), 1.0, 4.0, jnp.float32)
    zone_weight = jnp.clip(jnp.exp(jax.random.uniform(key_list[7], (ZONES,), jnp.float32, math.log(0.25), math.log(4.0))), 0.25, 4.0)
    pair_zones = draw_pair_zones(jax.random.fold_in(key_list[10], 71), 0)
    pair_weight = jnp.clip(jnp.exp(jax.random.uniform(key_list[9], (PAIRS,), jnp.float32, math.log(0.25), math.log(4.0))), 0.25, 4.0)
    return dict(source=source, conductivity=conductivity, leakance=leakance, storage=storage, et_rate=et_rate, zone_of_block=zone_of_block, zone_recharge=zone_recharge, zone_weight=zone_weight, pair_zones=pair_zones, pair_weight=pair_weight)


COUPLE = 4.0
PRECOND_T = 2.0
PRECOND_SHIFT = 3.0


def spectral_weight(wave_rows, wave_cols, rows_total, cols_total):
    half_rows = jnp.sin(wave_rows.astype(jnp.float32) * (math.pi / rows_total))
    half_cols = jnp.sin(wave_cols.astype(jnp.float32) * (math.pi / cols_total))
    return 1.0 / (PRECOND_T * 4.0 * (half_rows * half_rows + half_cols * half_cols) + PRECOND_SHIFT)


def reference(source, conductivity, leakance, storage, et_rate, zone_of_block, zone_recharge, zone_weight, pair_zones, pair_weight):
    padded_cond = jnp.pad(conductivity, ((0, 0), (1, 1), (1, 1)))
    north_face = 0.5 * (conductivity + padded_cond[:, :-2, 1:-1])
    south_face = 0.5 * (conductivity + padded_cond[:, 2:, 1:-1])
    west_face = 0.5 * (conductivity + padded_cond[:, 1:-1, :-2])
    east_face = 0.5 * (conductivity + padded_cond[:, 1:-1, 2:])
    empty_layer = jnp.zeros_like(leakance[:1])
    below_link = jnp.concatenate([leakance, empty_layer], axis=0)
    above_link = jnp.concatenate([empty_layer, leakance], axis=0)
    surface_loss = jnp.concatenate([et_rate[None], jnp.zeros_like(storage[1:])], axis=0)
    diagonal = storage + north_face + south_face + west_face + east_face + below_link + above_link + surface_loss

    def spread_zones(values):
        per_block = values[zone_of_block]
        return jnp.repeat(jnp.repeat(per_block, 8, axis=0), 8, axis=1)

    def gather_zones(surface):
        block_sums = surface.reshape(NX // 8, 8, NY // 8, 8).sum(axis=(1, 3))
        return jax.ops.segment_sum(block_sums.reshape(-1), zone_of_block.reshape(-1), num_segments=ZONES)

    def coupling(totals):
        scaled = totals * (ZONES / (NX * NY))
        contrast = pair_weight * (scaled[pair_zones[:, 0]] - scaled[pair_zones[:, 1]])
        gained = jax.ops.segment_sum(contrast, pair_zones[:, 0], num_segments=ZONES)
        lost = jax.ops.segment_sum(contrast, pair_zones[:, 1], num_segments=ZONES)
        return zone_weight * scaled + (gained - lost)

    def operator_apply(values_in):
        padded = jnp.pad(values_in, ((0, 0), (1, 1), (1, 1)))
        deeper = jnp.concatenate([values_in[1:], jnp.zeros_like(values_in[:1])], axis=0)
        higher = jnp.concatenate([jnp.zeros_like(values_in[:1]), values_in[:-1]], axis=0)
        partial_image = (diagonal * values_in - north_face * padded[:, :-2, 1:-1] - south_face * padded[:, 2:, 1:-1]
                         - west_face * padded[:, 1:-1, :-2] - east_face * padded[:, 1:-1, 2:]
                         - below_link * deeper - above_link * higher)
        couple_values = coupling(gather_zones(values_in[0]))
        surface = partial_image[0] + COUPLE * spread_zones(couple_values)
        return jnp.concatenate([surface[None], partial_image[1:]], axis=0)

    def precondition(residual_in):
        depth_sum = jnp.sum(residual_in, axis=0)
        waves = spectral_weight(jnp.arange(NX, dtype=jnp.int32)[:, None], jnp.arange(NY, dtype=jnp.int32)[None, :], NX, NY)
        smooth = jnp.real(jnp.fft.ifft2(jnp.fft.fft2(depth_sum) * waves)).astype(residual_in.dtype)
        return residual_in / diagonal + smooth[None]

    right_side = jnp.concatenate([(source[0] + spread_zones(zone_recharge))[None], source[1:]], axis=0)
    solution = jnp.zeros_like(source)
    residual = right_side
    preconditioned = precondition(residual)
    direction = preconditioned
    gamma_now = jnp.sum(residual * preconditioned)
    for sweep_index in range(ITERS):
        applied = operator_apply(direction)
        step_length = gamma_now / jnp.sum(direction * applied)
        solution = solution + step_length * direction
        residual = residual - step_length * applied
        if sweep_index + 1 < ITERS:
            preconditioned = precondition(residual)
            gamma_next = jnp.sum(residual * preconditioned)
            direction = preconditioned + (gamma_next / gamma_now) * direction
            gamma_now = gamma_next
    return solution, residual
```

```python
import math

import jax
import jax.numpy as jnp
import numpy as np
from jax import lax
from jax.experimental import pallas as pl
from jax.experimental.pallas import tpu as pltpu
from jax.sharding import PartitionSpec as P

COUPLE = 4.0
PRECOND_T = 2.0
PRECOND_SHIFT = 3.0
HIGHEST = lax.Precision.HIGHEST
BOTH = ("slab", "grp")
VMEM_LIMIT = 48 * 1024 * 1024


def sine_basis(count):
    index = np.arange(1, count + 1)
    basis = math.sqrt(2.0 / (count + 1)) * np.sin(np.pi * np.outer(index, index) / (count + 1))
    return basis, 4.0 * np.sin(np.pi * index / (2.0 * (count + 1))) ** 2


def fourier_basis(count):
    cells = np.arange(count)[:, None]
    waves = np.concatenate([np.arange(count // 2 + 1), np.arange(1, count // 2)])[None, :]
    turned = 2.0 * np.pi * ((cells * waves) % count) / count
    is_sine = np.arange(count)[None, :] > count // 2
    basis = np.where(is_sine, np.sin(turned), np.cos(turned)) * math.sqrt(2.0 / count)
    basis[:, 0] /= math.sqrt(2.0)
    basis[:, count // 2] /= math.sqrt(2.0)
    return basis, 4.0 * np.sin(np.pi * waves[0] / count) ** 2


def chain_tables(cross, total, block):
    half = (PRECOND_SHIFT / PRECOND_T + cross) / 2.0 + 1.0
    decay = 1.0 / (half + np.sqrt(half * half - 1.0))
    scale = 1.0 / ((1.0 - decay**total) * PRECOND_T * (1.0 / decay - decay))

    def green(distance):
        distance = distance % total
        return PRECOND_T * scale * (decay**distance + decay ** (total - distance))

    count = total // block
    tables = np.zeros((4, count, len(cross)))
    for back in range(count):
        tables[0, back] = green(block * back)
        tables[1, back] = green(block * (back - 1) - 1) + (1.0 if back == 1 % count else 0.0)
        tables[2, back] = green(block * (back + 1) + 1) + (1.0 if back == count - 1 else 0.0)
        tables[3, back] = green(block * back)
    return tables


def grid_tables(slabs, groups, rows, cols):
    rows_total, cols_total = slabs * rows, groups * cols
    sine_rows, cross_rows = sine_basis(rows)
    sine_cols, cross_cols = sine_basis(cols)
    waves, cross_waves = fourier_basis(rows_total)
    weight = 1.0 / (PRECOND_SHIFT + PRECOND_T * (cross_rows[:, None] + cross_cols[None, :]))
    wave_weight = 1.0 / (PRECOND_SHIFT + PRECOND_T * (cross_waves[:, None] + cross_cols[None, :]))
    first, last = sine_cols[0], sine_cols[-1]
    lanes = 1024 + 128
    answer = np.zeros((2, cols, 128))
    for end, row in enumerate((0, rows - 1)):
        inside = PRECOND_T * np.einsum("ri,ij,i->jr", sine_rows, weight, sine_rows[:, row])
        answer[end, :, :rows] = first[:, None] * inside
        answer[end, :, rows : 2 * rows] = last[:, None] * inside
    spread_rows = np.repeat(np.eye(rows // 8), 8, axis=0)
    spread_cols = np.repeat(np.eye(cols // 8), 8, axis=0)
    mode_rows, mode_cols = sine_rows @ spread_rows, sine_cols @ spread_cols
    mixed = np.einsum("ri,ij,ib->rbj", sine_rows, weight, mode_rows)
    coarse = np.zeros((rows // 8, cols // 8, 2 * cols + 128))
    coarse[:, :, :cols] = np.einsum("bj,jc->bcj", mixed[0], mode_cols)
    coarse[:, :, cols : 2 * cols] = np.einsum("bj,jc->bcj", mixed[-1], mode_cols)
    coarse[:, :, 2 * cols : 2 * cols + rows] = np.einsum("rbj,j,jc->bcr", mixed, first, mode_cols)
    coarse[:, :, 2 * cols + rows : 2 * cols + 2 * rows] = np.einsum(
        "rbj,j,jc->bcr", mixed, last, mode_cols
    )
    to_waves = np.zeros((slabs, 2, rows, 2, rows_total))
    for side in range(2):
        to_waves[:, side, :, side, :] = waves.reshape(slabs, rows, rows_total)
    column_chain = chain_tables(cross_waves, cols_total, cols)
    tile = max(8, groups)
    own_columns = np.zeros((groups, 4, tile, rows_total))
    for group in range(groups):
        for other in range(groups):
            own_columns[group, :, other] = column_chain[:, (group - other) % groups]
    around = np.zeros((slabs, 8, rows_total))
    for slab in range(slabs):
        around[slab, 0] = waves[(rows * slab - 1) % rows_total]
        around[slab, 1] = waves[(rows * slab + rows) % rows_total]
    ends = np.zeros((8, cols))
    ends[0], ends[1] = first, last
    up = np.zeros((128, cols))
    up[1 : 1 + cols // 8] = spread_cols.T
    blocks = (rows // 8) * (cols // 8)
    down = np.tile(spread_cols, (1, rows // 8))
    tables = dict(
        sine_rows=sine_rows,
        sine_cols=sine_cols,
        weight=weight,
        row_chain=chain_tables(cross_cols, rows_total, rows).reshape(4 * slabs, cols),
        answer=answer.reshape(2 * cols, 128),
        coarse=coarse.reshape(blocks, 2 * cols + 128),
        to_waves=to_waves.reshape(slabs * 2 * rows, 2 * rows_total),
        own_columns=own_columns.reshape(groups, 4 * tile, rows_total),
        own_waves=waves.reshape(slabs, rows, rows_total),
        around=around,
        wave_weight=wave_weight,
        ends=ends,
        up=up,
        up_modes=up @ sine_cols,
        down=down,
    )
    return {name: np.asarray(table, np.float32) for name, table in tables.items()}


def mm(left, right):
    return jnp.dot(left, right, precision=HIGHEST, preferred_element_type=jnp.float32)


def mm_t(left, right):
    return lax.dot_general(
        left, right, (((1,), (1,)), ((), ())), precision=HIGHEST, preferred_element_type=jnp.float32
    )


def iota(shape, dim):
    return lax.broadcasted_iota(jnp.int32, shape, dim)


def lookup(values, index):
    rows, lanes = index.shape
    zones = values.shape[1]
    within, which = index % 128, index // 128
    pieces = []
    for start in range(0, lanes, 128):
        part = jnp.zeros((rows, 128), jnp.float32)
        for half in range(zones // 128):
            table = jnp.broadcast_to(values[:, 128 * half : 128 * (half + 1)], (rows, 128))
            found = jnp.take_along_axis(table, within[:, start : start + 128], axis=1)
            part = jnp.where(which[:, start : start + 128] == half, found, part)
        pieces.append(part)
    return jnp.concatenate(pieces, axis=1) if len(pieces) > 1 else pieces[0]


def columns_to_lanes(parts, selector):
    stacked = jnp.concatenate(parts, axis=0)
    return mm_t(selector, stacked)


def rings(q_mixed, t):
    inside = mm(t["sine_rows"], mm(t["sine_rows"], q_mixed) * t["weight"])
    rows = inside.shape[0]
    picked = columns_to_lanes([inside] * (128 // rows), t["ends"])
    place = iota((8, 128), 1) // rows == iota((8, 128), 0)
    edges = jnp.sum(jnp.where(place, picked, 0.0), axis=0, keepdims=True)
    return inside[0:1], inside[rows - 1 : rows], edges


def stencil(values, before, after, left, right):
    rows, cols = values.shape
    row, col = iota(values.shape, 0), iota(values.shape, 1)
    up = jnp.where(row == 0, before, pltpu.roll(values, 1, 0))
    down = jnp.where(row == rows - 1, after, pltpu.roll(values, rows - 1, 0))
    west = jnp.where(col == 0, left, pltpu.roll(values, 1, 1))
    east = jnp.where(col == cols - 1, right, pltpu.roll(values, cols - 1, 1))
    return (up + down) + (west + east)


def zone_totals(surface, zone_column, down, zones):
    rows = surface.shape[0]
    sums = jnp.concatenate(
        [jnp.sum(surface[8 * i : 8 * i + 8], axis=0, keepdims=True) for i in range(rows // 8)], axis=0
    )
    spread = mm(sums, down)
    blocks = down.shape[1]
    width = blocks // (rows // 8)
    own = iota(spread.shape, 1) // width == iota(spread.shape, 0)
    line = jnp.sum(jnp.where(own, spread, 0.0), axis=0, keepdims=True)
    hot = (zone_column == iota((blocks, zones), 1)).astype(jnp.float32)
    return mm(line, hot)


def spread_rows8(lines, rows):
    return jnp.concatenate(
        [jnp.broadcast_to(lines[i : i + 1], (8, lines.shape[1])) for i in range(rows // 8)], axis=0
    )


def smooth(rings_all, edges_all, q_mixed, slab, group, groups, t):
    devices = rings_all.shape[0]
    slabs = devices // groups
    rows, cols = q_mixed.shape
    first_rows, last_rows = rings_all[:, :cols], rings_all[:, cols:]
    before = jnp.zeros_like(first_rows)
    after = jnp.zeros_like(first_rows)
    chain = t["row_chain"]
    for back in range(slabs):
        turned_first = pltpu.roll(first_rows, groups * back, 0) if back else first_rows
        turned_last = pltpu.roll(last_rows, groups * back, 0) if back else last_rows
        line = [chain[slabs * kind + back : slabs * kind + back + 1] for kind in range(4)]
        before = before + (line[0] * turned_first + line[1] * turned_last)
        after = after + (line[2] * turned_first + line[3] * turned_last)
    mine = iota(before.shape, 0) == slab * groups + group
    own_before = jnp.sum(jnp.where(mine, before, 0.0), axis=0, keepdims=True)
    own_after = jnp.sum(jnp.where(mine, after, 0.0), axis=0, keepdims=True)
    edges = edges_all + mm(before, t["answer"][:cols]) + mm(after, t["answer"][cols:])
    half = 2 * rows
    other = pltpu.roll(pltpu.roll(edges, half, 1), devices - groups, 0)
    paired = jnp.where(iota(edges.shape, 1) < half, edges, other)
    tile = max(8, groups)
    lines = jnp.concatenate(
        [paired[2 * groups * p : 2 * groups * p + tile] for p in range(slabs // 2)], axis=1
    )
    waved = mm(lines, t["to_waves"])
    count = waved.shape[1] // 2
    firsts, lasts = waved[:, :count], waved[:, count:]
    chain = t["own_columns"]
    table = [chain[tile * kind : tile * (kind + 1)] for kind in range(4)]
    left = jnp.sum(table[0] * firsts + table[1] * lasts, axis=0, keepdims=True)
    right = jnp.sum(table[2] * firsts + table[3] * lasts, axis=0, keepdims=True)
    row = iota((8, count), 0)
    sides = jnp.where(row == 0, left, jnp.where(row == 1, right, 0.0))
    columns = mm_t(t["own_waves"], sides)
    left_col, right_col = columns[:, 0:1], columns[:, 1:2]
    around = t["around"]
    north, south = around[0:1], around[1:2]
    four = jnp.where(
        row == 0,
        north * left,
        jnp.where(row == 1, north * right, jnp.where(row == 2, south * left, jnp.where(row == 3, south * right, 0.0))),
    )
    four = mm(four, t["wave_weight"])
    first, last = t["ends"][0:1], t["ends"][1:2]
    north_row = own_before + PRECOND_T * (first * four[0:1] + last * four[1:2])
    south_row = own_after + PRECOND_T * (first * four[2:3] + last * four[3:4])
    place = iota((rows, cols), 0)
    loaded = q_mixed + PRECOND_T * (
        jnp.where(place == 0, north_row, 0.0)
        + jnp.where(place == rows - 1, south_row, 0.0)
        + left_col * first
        + right_col * last
    )
    inside = mm(t["sine_rows"], mm(t["sine_rows"], loaded) * t["weight"])
    pad = jnp.zeros((6, cols), jnp.float32)
    whole = mm(jnp.concatenate([inside, north_row, south_row, pad], axis=0), t["sine_cols"])
    return whole[:rows], whole[rows : rows + 1], whole[rows + 1 : rows + 2], left_col, right_col


SMOOTH_TABLES = (
    "sine_rows", "sine_cols", "weight", "row_chain", "answer", "coarse", "to_waves", "own_columns", "own_waves",
    "around", "wave_weight", "ends", "up", "up_modes", "down",
)
PER_SLAB = ("own_waves", "around")


def call(body, outs, scratch=()):
    return pl.pallas_call(
        body,
        out_shape=[jax.ShapeDtypeStruct(shape, jnp.float32) for shape in outs],
        scratch_shapes=list(scratch),
        compiler_params=pltpu.CompilerParams(vmem_limit_bytes=VMEM_LIMIT),
    )


def shards(
    source,
    conductivity,
    leakance,
    storage,
    et_rate,
    zone_of_block,
    zone_recharge,
    zone_weight,
    pair_zones,
    pair_weight,
):
    slabs, groups = lax.axis_size("slab"), lax.axis_size("grp")
    layers, rows, cols = source.shape
    devices = slabs * groups
    zones = zone_weight.shape[0]
    slab, group = lax.axis_index("slab"), lax.axis_index("grp")
    here = jnp.stack([slab, group]).astype(jnp.int32)
    tables = grid_tables(slabs, groups, rows, cols)
    block_rows, block_cols = rows // 8, cols // 8
    width = 2 * cols + 128 + zones + 256
    at_edges, at_zones, at_sides = 2 * cols, 2 * cols + 128, 2 * cols + 128 + zones
    area = (layers, rows, cols)

    def neighbours(first, last):
        return (
            lax.ppermute(last, "slab", [(i, i + 1) for i in range(slabs - 1)]),
            lax.ppermute(first, "slab", [(i + 1, i) for i in range(slabs - 1)]),
        )

    def exchange(chunk):
        return lax.all_to_all(chunk, BOTH, split_axis=0, concat_axis=0, tiled=True)

    t = {name: jnp.asarray(table) for name, table in tables.items()}
    for name in PER_SLAB:
        t[name] = lax.dynamic_index_in_dim(t[name], slab, keepdims=False)
    t["own_columns"] = lax.dynamic_index_in_dim(t["own_columns"], group, keepdims=False)
    picks = np.zeros((8, 128), np.float32)
    picks[0, 0], picks[1, 127] = 1.0, 1.0
    picks = jnp.asarray(picks)

    cond_north, cond_south = neighbours(conductivity[:, 0], conductivity[:, rows - 1])
    cond_west = lax.ppermute(conductivity[:, :, cols - 1], "grp", [(i, i + 1) for i in range(groups - 1)])
    cond_east = lax.ppermute(conductivity[:, :, 0], "grp", [(i + 1, i) for i in range(groups - 1)])
    cond_sides = jnp.pad(jnp.stack([cond_west, cond_east], axis=-1), ((0, 0), (0, 0), (0, 126)))

    zone_column = zone_of_block.reshape(-1, 1)
    zone_lane = zone_of_block.reshape(1, -1).astype(jnp.float32)
    own_ext = jnp.pad(zone_of_block, ((1, 8 - block_rows - 1), (1, 128 - block_cols - 1)))

    zone_ids = lax.broadcasted_iota(jnp.int32, (1, zones), 1)
    pair_table = (pair_zones[:, 0:1] == zone_ids).astype(jnp.float32) - (
        pair_zones[:, 1:2] == zone_ids
    ).astype(jnp.float32)
    couple = (COUPLE * zones / (slabs * rows * groups * cols)) * (
        jnp.dot(pair_table.T, pair_weight[:, None] * pair_table, precision=HIGHEST)
        + jnp.where(zone_ids == zone_ids.T, zone_weight[None, :], 0.0)
    )

    def start_body(source_ref, ext_ref, recharge_ref, up_ref, sr, sc, wt, ends, rhs_ref, q_ref, ring_ref):
        tt = dict(sine_rows=sr[...], weight=wt[...], ends=ends[...])
        field = mm(lookup(recharge_ref[...], ext_ref[...]), up_ref[...])
        rhs_ref[0] = source_ref[0] + spread_rows8(field[1 : 1 + block_rows], rows)
        for layer in range(1, layers):
            rhs_ref[layer] = source_ref[layer]
        total = rhs_ref[0]
        for layer in range(1, layers):
            total = total + rhs_ref[layer]
        q_mixed = mm(total, sc[...])
        q_ref[...] = q_mixed
        first, last, edges = rings(q_mixed, tt)
        ring_ref[:, :cols] = first
        ring_ref[:, cols : 2 * cols] = last
        ring_ref[:, 2 * cols :] = edges

    rhs, q_mixed, ring = call(start_body, [area, (rows, cols), (1, 2 * cols + 128)])(
        source, own_ext, zone_recharge[None], t["up"], t["sine_rows"], t["sine_cols"], t["weight"], t["ends"]
    )

    def side_lanes(parts, picks_value):
        pad = [jnp.zeros((128 - rows * len(parts), 128), jnp.float32)] if rows * len(parts) < 128 else []
        west = columns_to_lanes([p[:, :128] for p in parts] + pad, picks_value)
        east = columns_to_lanes([p[:, cols - 128 :] for p in parts] + pad, picks_value)
        return west[0:1], east[1:2]

    def write_chunk(chunk_ref, line_ref):
        chunk_ref[...] = jnp.broadcast_to(line_ref[...][None], chunk_ref.shape)

    def diagonal_body(
        cond, cn, cs, sides, leak, store, et, rhs_ref, ring_ref, zone_ref, picks_ref,
        inv_ref, rows_ref, chunk_ref, line_ref,
    ):
        scaled = []
        for layer in range(layers):
            own = cond[layer]
            around = stencil(
                own, cn[layer : layer + 1], cs[layer : layer + 1], sides[layer, :, 0:1], sides[layer, :, 1:2]
            )
            diagonal = store[layer] + 0.5 * (4.0 * own + around)
            if layer < layers - 1:
                diagonal = diagonal + leak[layer]
            if layer > 0:
                diagonal = diagonal + leak[layer - 1]
            if layer == 0:
                diagonal = diagonal + et[...]
            inverse = 1.0 / diagonal
            inv_ref[layer] = inverse
            scaled.append(rhs_ref[layer] * inverse)
        top = inv_ref[0]
        for layer in range(layers):
            rows_ref[0, layer : layer + 1] = scaled[layer][0:1]
            rows_ref[1, layer : layer + 1] = scaled[layer][rows - 1 : rows]
        rows_ref[0, layers : layers + 1] = top[0:1]
        rows_ref[1, layers : layers + 1] = top[rows - 1 : rows]
        west, east = side_lanes(scaled + [top], picks_ref[...])
        line_ref[:, : 2 * cols + 128] = ring_ref[...]
        line_ref[:, at_zones : at_zones + zones] = zone_ref[...]
        line_ref[:, at_sides : at_sides + 128] = west
        line_ref[:, at_sides + 128 :] = east
        write_chunk(chunk_ref, line_ref)

    line_scratch = pltpu.VMEM((1, width), jnp.float32)
    inverse, halo_rows, chunk = call(
        diagonal_body, [area, (2, layers + 1, cols), (devices, 1, width)], [line_scratch]
    )(
        conductivity, cond_north, cond_south, cond_sides, leakance, storage, et_rate, rhs, ring, zone_lane, picks
    )
    received = exchange(chunk)
    halo_north, halo_south = neighbours(halo_rows[0], halo_rows[1])
    inv_north, inv_south = halo_north[layers:], halo_south[layers:]

    zone_map = received[:, 0, at_zones : at_zones + zones].astype(jnp.int32)
    whole = zone_map.reshape(slabs, groups, block_rows, block_cols).transpose(0, 2, 1, 3)
    whole = jnp.pad(whole.reshape(slabs * block_rows, groups * block_cols), 1)
    zone_ext = lax.dynamic_slice(
        whole, (slab * block_rows, group * block_cols), (block_rows + 2, block_cols + 2)
    )
    zone_ext = jnp.pad(zone_ext, ((0, 6 - block_rows), (0, 126 - block_cols)))
    first_sides = received[:, :, at_sides:]

    def step_body(coupled, last, names, *refs):
        refs = list(refs)
        take = lambda count: [refs.pop(0) for _ in range(count)]
        (here_ref,) = take(1)
        (recv_ref, q_ref, w_ref, hn, hs, inv_ref, inv_n, inv_s, first_sides_ref) = take(9)
        (cond, cn, cs, sides, leak, zone_col, picks_ref, eye_ref) = take(8)
        (map_ref, ext_ref, couple_ref) = take(3)
        if last:
            rhs_ref, v0_ref, v1_ref, w0_ref = take(4)
        table_refs = take(len(names))
        tt = dict(zip(names, table_refs))
        tt = {
            name: (ref if name in ("row_chain", "answer", "own_columns") else ref[...])
            for name, ref in tt.items()
        }
        if last:
            v_out, wl_out, w_out, chunk_ref, line_ref = refs
        else:
            v_out, wl_out, w_out, q_out, rows_out, chunk_ref, line_ref = refs
        slab_i, group_i = here_ref[0], here_ref[1]
        own = slab_i * groups + group_i
        message = recv_ref[:, 0, :]
        rings_all = message[:, : 2 * cols]
        edges_all = message[:, 2 * cols : 2 * cols + 128]
        q_in = q_ref[...]
        surface = w_ref[0]
        if coupled:
            totals = jnp.sum(message[:, at_zones : at_zones + zones], axis=0, keepdims=True)
            reply = mm(totals, couple_ref[...])
            coarse = mm(lookup(reply, map_ref[...]), tt["coarse"])
            rings_all = rings_all + coarse[:, : 2 * cols]
            edges_all = edges_all + coarse[:, 2 * cols :]
            ext = lookup(reply, ext_ref[...])
            field = mm(ext, tt["up"])
            modes = mm(ext, tt["up_modes"])
            q_in = q_in + spread_rows8(modes[1 : 1 + block_rows], rows)
            surface = surface + spread_rows8(field[1 : 1 + block_rows], rows)
        for layer in range(layers):
            w_out[layer] = surface if layer == 0 else w_ref[layer]
        edges_all = jnp.where(iota(edges_all.shape, 1) < 2 * rows, edges_all, 0.0)
        s, s_north, s_south, s_west, s_east = smooth(
            rings_all, edges_all, q_in, slab_i, group_i, groups, tt
        )
        west_of = jnp.maximum(own - 1, 0)
        east_of = jnp.minimum(own + 1, devices - 1)
        lanes = jnp.concatenate(
            [
                recv_ref[pl.ds(west_of, 1), 0, at_sides + 128 :],
                recv_ref[pl.ds(east_of, 1), 0, at_sides : at_sides + 128],
                first_sides_ref[pl.ds(west_of, 1), 0, 128:],
                first_sides_ref[pl.ds(east_of, 1), 0, :128],
                jnp.zeros((4, 128), jnp.float32),
            ],
            axis=0,
        )
        stood = mm_t(eye_ref[...], lanes)
        has_north = (slab_i > 0).astype(jnp.float32)
        has_south = (slab_i < slabs - 1).astype(jnp.float32)
        has_west = (group_i > 0).astype(jnp.float32)
        has_east = (group_i < groups - 1).astype(jnp.float32)
        fields = []
        outside = []
        for layer in range(layers):
            value = (surface if layer == 0 else w_ref[layer]) * inv_ref[layer] + s
            v_out[layer] = value
            fields.append(value)
            north = hn[layer : layer + 1] + s_north
            south = hs[layer : layer + 1] + s_south
            west = stood[rows * layer : rows * (layer + 1), 0:1] + s_west
            east = stood[rows * layer : rows * (layer + 1), 1:2] + s_east
            if coupled and layer == 0:
                north = north + inv_n[...] * field[0:1]
                south = south + inv_s[...] * field[1 + block_rows : 2 + block_rows]
                beside = spread_rows8(ext[1 : 1 + block_rows], rows)
                west = west + stood[rows * layers : rows * (layers + 1), 2:3] * beside[:, 0:1]
                east = east + stood[rows * layers : rows * (layers + 1), 3:4] * (
                    beside[:, 1 + block_cols : 2 + block_cols]
                )
            outside.append((north * has_north, south * has_south, west * has_west, east * has_east))
        images = []
        for layer in range(layers):
            value, own_cond = fields[layer], cond[layer]
            north, south, west, east = outside[layer]
            plain = stencil(value, north, south, west, east)
            carried = stencil(
                value * own_cond,
                north * cn[layer : layer + 1],
                south * cs[layer : layer + 1],
                west * sides[layer, :, 0:1],
                east * sides[layer, :, 1:2],
            )
            image = value / inv_ref[layer] - 0.5 * (own_cond * plain + carried)
            if layer < layers - 1:
                image = image - leak[layer] * fields[layer + 1]
            if layer > 0:
                image = image - leak[layer - 1] * fields[layer - 1]
            wl_out[layer] = image
            images.append(image)
        line_ref[...] = jnp.zeros(line_ref.shape, jnp.float32)
        totals = zone_totals(fields[0], zone_col[...], tt["down"], zones)
        if last:
            def dot(left, right):
                total = jnp.sum(left[0] * right[0], axis=0, keepdims=True)
                for layer in range(1, layers):
                    total = total + jnp.sum(left[layer] * right[layer], axis=0, keepdims=True)
                return jnp.sum(total, axis=1, keepdims=True)

            w1 = [surface] + [w_ref[layer] for layer in range(1, layers)]
            products = [
                dot(v0_ref, w0_ref), dot(v0_ref, w1), dot(v1_ref, w1), dot(fields, w0_ref), dot(fields, w1),
                dot(fields, images), dot(v0_ref, rhs_ref), dot(v1_ref, rhs_ref), dot(fields, rhs_ref),
            ]
            lane = iota((1, 128), 1)
            packed = jnp.zeros((1, 128), jnp.float32)
            for place, product in enumerate(products):
                packed = jnp.where(lane == place, product, packed)
            line_ref[:, :zones] = totals
            line_ref[:, zones:] = packed
            write_chunk(chunk_ref, line_ref)
            return
        depth = images[0]
        for layer in range(1, layers):
            depth = depth + images[layer]
        q_next = mm(depth, tt["sine_cols"])
        q_out[...] = q_next
        first, final, edges = rings(q_next, tt)
        scaled = [images[layer] * inv_ref[layer] for layer in range(layers)]
        for layer in range(layers):
            rows_out[0, layer : layer + 1] = scaled[layer][0:1]
            rows_out[1, layer : layer + 1] = scaled[layer][rows - 1 : rows]
        west, east = side_lanes(scaled, picks_ref[...])
        line_ref[:, :cols] = first
        line_ref[:, cols : 2 * cols] = final
        line_ref[:, 2 * cols : 2 * cols + 128] = edges
        line_ref[:, at_zones : at_zones + zones] = totals
        line_ref[:, at_sides : at_sides + 128] = west
        line_ref[:, at_sides + 128 :] = east
        write_chunk(chunk_ref, line_ref)

    names = SMOOTH_TABLES
    eye = jnp.eye(128, dtype=jnp.float32)
    tail_width = zones + 128

    def step(coupled, last, received, q_in, w_in, north, south, more=()):
        outs = [area, area, area]
        if last:
            outs += [(devices, 1, tail_width)]
        else:
            outs += [(rows, cols), (2, layers, cols), (devices, 1, width)]
        operands = (
            [here, received, q_in, w_in, north, south, inverse, inv_north, inv_south, first_sides]
            + [conductivity, cond_north, cond_south, cond_sides, leakance, zone_column, picks, eye]
            + [zone_map, zone_ext, couple]
            + list(more)
            + [t[name] for name in names]
        )
        specs = [pl.BlockSpec(memory_space=pltpu.SMEM)] + [
            pl.BlockSpec(memory_space=pltpu.VMEM) for _ in operands[1:]
        ]

        def body(*refs):
            step_body(coupled, last, names, *refs)

        return pl.pallas_call(
            body,
            out_shape=[jax.ShapeDtypeStruct(shape, jnp.float32) for shape in outs],
            in_specs=specs,
            scratch_shapes=[pltpu.VMEM((1, tail_width if last else width), jnp.float32)],
            compiler_params=pltpu.CompilerParams(vmem_limit_bytes=VMEM_LIMIT),
        )(*operands)

    v0, wl0, _, q_mixed, halo_rows, chunk = step(
        False, False, received, q_mixed, rhs, halo_north, halo_south
    )
    received = exchange(chunk)
    halo_north, halo_south = neighbours(halo_rows[0], halo_rows[1])
    v1, wl1, w0, q_mixed, halo_rows, chunk = step(
        True, False, received, q_mixed, wl0, halo_north, halo_south
    )
    received = exchange(chunk)
    halo_north, halo_south = neighbours(halo_rows[0], halo_rows[1])
    v2, wl2, w1, chunk = step(
        True, True, received, q_mixed, wl1, halo_north, halo_south, (rhs, v0, v1, w0)
    )
    received = exchange(chunk)

    def finish_body(recv_ref, ext_ref, couple_ref, up_ref, rhs_ref, v0r, v1r, v2r, w0r, w1r, w2r, sol_ref, res_ref):
        sums = jnp.sum(recv_ref[:, 0, :], axis=0, keepdims=True)
        totals = sums[:, :zones]
        reply = mm(totals, couple_ref[...])
        field = mm(lookup(reply, ext_ref[...]), up_ref[...])
        coupled = spread_rows8(field[1 : 1 + block_rows], rows)
        g = [sums[:, zones + i : zones + i + 1] for i in range(9)]
        a00, a01, a11, a02, a12, a22, h0, h1, h2 = g
        a22 = a22 + jnp.sum(totals * reply, axis=1, keepdims=True)
        l10, l20 = a01 / a00, a02 / a00
        d1 = a11 - l10 * a01
        e12 = a12 - l10 * a02
        l21 = e12 / d1
        d2 = a22 - l20 * a02 - l21 * e12
        y1 = h1 - l10 * h0
        y2 = h2 - l20 * h0 - l21 * y1
        c2 = y2 / d2
        c1 = y1 / d1 - l21 * c2
        c0 = h0 / a00 - l10 * c1 - l20 * c2
        for layer in range(layers):
            w2 = w2r[layer]
            if layer == 0:
                w2 = w2 + coupled
            sol_ref[layer] = c0 * v0r[layer] + c1 * v1r[layer] + c2 * v2r[layer]
            res_ref[layer] = rhs_ref[layer] - c0 * w0r[layer] - c1 * w1r[layer] - c2 * w2

    answer, residual = call(finish_body, [area, area])(
        received, zone_ext, couple, t["up"], rhs, v0, v1, v2, w0, w1, wl2
    )
    return answer, residual


def solution(mesh):
    placed = (
        P(None, "slab", "grp"),
        P(None, "slab", "grp"),
        P(None, "slab", "grp"),
        P(None, "slab", "grp"),
        P("slab", "grp"),
        P("slab", "grp"),
        P(),
        P(),
        P(),
        P(),
    )
    return jax.shard_map(
        shards,
        mesh=mesh,
        in_specs=placed,
        out_specs=(P(None, "slab", "grp"), P(None, "slab", "grp")),
        check_vma=False,
    )
```

```python
import math
from types import SimpleNamespace

import jax
import jax.numpy as jnp
import numpy as np
from jax import lax
from jax.experimental import pallas as pl
from jax.experimental.pallas import tpu as pltpu
from jax.sharding import PartitionSpec as P

COUPLE = 4.0
PRECOND_T = 2.0
PRECOND_SHIFT = 3.0
HIGHEST = lax.Precision.HIGHEST
BOTH = ("slab", "grp")
VMEM_LIMIT = 64 * 1024 * 1024
F32, BF16 = jnp.float32, jnp.bfloat16


def sine_basis(count):
    index = np.arange(1, count + 1)
    basis = math.sqrt(2.0 / (count + 1)) * np.sin(np.pi * np.outer(index, index) / (count + 1))
    return basis, 4.0 * np.sin(np.pi * index / (2.0 * (count + 1))) ** 2


def fourier_basis(count):
    cells = np.arange(count)[:, None]
    waves = np.concatenate([np.arange(count // 2 + 1), np.arange(1, count // 2)])[None, :]
    turned = 2.0 * np.pi * ((cells * waves) % count) / count
    is_sine = np.arange(count)[None, :] > count // 2
    basis = np.where(is_sine, np.sin(turned), np.cos(turned)) * math.sqrt(2.0 / count)
    basis[:, 0] /= math.sqrt(2.0)
    basis[:, count // 2] /= math.sqrt(2.0)
    return basis, 4.0 * np.sin(np.pi * waves[0] / count) ** 2


def chain_tables(cross, total, block):
    half = (PRECOND_SHIFT / PRECOND_T + cross) / 2.0 + 1.0
    decay = 1.0 / (half + np.sqrt(half * half - 1.0))
    scale = 1.0 / ((1.0 - decay**total) * PRECOND_T * (1.0 / decay - decay))

    def green(distance):
        distance = distance % total
        return PRECOND_T * scale * (decay**distance + decay ** (total - distance))

    count = total // block
    tables = np.zeros((4, count, len(cross)))
    for back in range(count):
        tables[0, back] = green(block * back)
        tables[1, back] = green(block * (back - 1) - 1) + (1.0 if back == 1 % count else 0.0)
        tables[2, back] = green(block * (back + 1) + 1) + (1.0 if back == count - 1 else 0.0)
        tables[3, back] = green(block * back)
    return tables


def grid_tables(slabs, groups, rows, cols):
    rows_total, cols_total = slabs * rows, groups * cols
    sine_rows, cross_rows = sine_basis(rows)
    sine_cols, cross_cols = sine_basis(cols)
    waves, cross_waves = fourier_basis(rows_total)
    weight = 1.0 / (PRECOND_SHIFT + PRECOND_T * (cross_rows[:, None] + cross_cols[None, :]))
    wave_weight = 1.0 / (PRECOND_SHIFT + PRECOND_T * (cross_waves[:, None] + cross_cols[None, :]))
    first, last = sine_cols[0], sine_cols[-1]
    answer = np.zeros((2, cols, 128))
    for end, row in enumerate((0, rows - 1)):
        inside = PRECOND_T * np.einsum("ri,ij,i->jr", sine_rows, weight, sine_rows[:, row])
        answer[end, :, :rows] = first[:, None] * inside
        answer[end, :, rows : 2 * rows] = last[:, None] * inside
    spread_rows = np.repeat(np.eye(rows // 8), 8, axis=0)
    spread_cols = np.repeat(np.eye(cols // 8), 8, axis=0)
    mode_rows, mode_cols = sine_rows @ spread_rows, sine_cols @ spread_cols
    mixed = np.einsum("ri,ij,ib->rbj", sine_rows, weight, mode_rows)
    coarse = np.zeros((rows // 8, cols // 8, 2 * cols + 128))
    coarse[:, :, :cols] = np.einsum("bj,jc->bcj", mixed[0], mode_cols)
    coarse[:, :, cols : 2 * cols] = np.einsum("bj,jc->bcj", mixed[-1], mode_cols)
    coarse[:, :, 2 * cols : 2 * cols + rows] = np.einsum("rbj,j,jc->bcr", mixed, first, mode_cols)
    coarse[:, :, 2 * cols + rows : 2 * cols + 2 * rows] = np.einsum(
        "rbj,j,jc->bcr", mixed, last, mode_cols
    )
    column_chain = chain_tables(cross_waves, cols_total, cols)
    tile = max(8, groups)
    own_columns = np.zeros((groups, 4, tile, rows_total))
    for group in range(groups):
        for other in range(groups):
            own_columns[group, :, other] = column_chain[:, (group - other) % groups]
    around = np.zeros((slabs, 8, rows_total))
    for slab in range(slabs):
        around[slab, 0] = waves[(rows * slab - 1) % rows_total]
        around[slab, 1] = waves[(rows * slab + rows) % rows_total]
    ends = np.zeros((8, cols))
    ends[0], ends[1] = first, last
    blocks = (rows // 8) * (cols // 8)
    down = np.tile(spread_cols, (1, rows // 8))
    exact = dict(
        weight=weight,
        row_chain=chain_tables(cross_cols, rows_total, rows).reshape(4 * slabs, cols),
        own_columns=own_columns.reshape(groups, 4 * tile, rows_total),
        around=around,
        ends=ends,
        place=np.tile(np.eye(cols // 8), (1, rows // 8)),
    )
    split = dict(
        sine_rows=sine_rows,
        sine_cols=sine_cols,
        answer=answer.reshape(2 * cols, 128),
        coarse=coarse.reshape(blocks, 2 * cols + 128),
        waves=waves,
        wave_weight=wave_weight,
        up_modes=down.T @ sine_cols,
    )
    tables = {name: np.asarray(table, np.float32) for name, table in exact.items()}
    for name, table in split.items():
        high = table.astype(jnp.bfloat16)
        tables[name] = np.stack([high, (table - high.astype(np.float64)).astype(jnp.bfloat16)])
    tables["down"] = down.astype(jnp.bfloat16)
    return tables


def terms(value, count):
    parts = []
    for _ in range(count):
        part = value.astype(BF16).astype(F32)
        parts.append(part)
        value = value - part
    return parts


DIMS = (((1,), (0,)), ((), ()))
DIMS_T = (((1,), (1,)), ((), ()))


def product(left, right, dims):
    return lax.dot_general(left, right, dims, preferred_element_type=F32)


def mm(value, table, dims=DIMS):
    rows = value.shape[0]
    high, low = terms(value, 2)
    both = product(jnp.concatenate([high, low], axis=0).astype(BF16), table[0], dims)
    return both[:rows] + both[rows:] + product(high.astype(BF16), table[1], dims)


def mm_left(table, value, dims=DIMS):
    rows = table[0].shape[0]
    high, low = terms(value, 2)
    both = product(jnp.concatenate([table[0], table[1]], axis=0), high.astype(BF16), dims)
    return both[:rows] + both[rows:] + product(table[0], low.astype(BF16), dims)


def mm_exact(value, table, dims=DIMS):
    rows = value.shape[0]
    every = product(jnp.concatenate(terms(value, 3), axis=0).astype(BF16), table, dims)
    return every[:rows] + every[rows : 2 * rows] + every[2 * rows :]


def mm_f32(left, right, dims=DIMS):
    return lax.dot_general(left, right, dims, precision=HIGHEST, preferred_element_type=F32)


def iota(shape, dim):
    return lax.broadcasted_iota(jnp.int32, shape, dim)


def lookup(values, index):
    rows, lanes = index.shape
    zones = values.shape[1]
    within, which = index & 127, index >> 7
    pieces = []
    for start in range(0, lanes, 128):
        part = jnp.zeros((rows, 128), F32)
        for half in range(zones // 128):
            table = jnp.broadcast_to(values[:, 128 * half : 128 * (half + 1)], (rows, 128))
            found = jnp.take_along_axis(table, within[:, start : start + 128], axis=1)
            part = jnp.where(which[:, start : start + 128] == half, found, part)
        pieces.append(part)
    return jnp.concatenate(pieces, axis=1) if len(pieces) > 1 else pieces[0]


def rings(q_mixed, t):
    sine_rows = t.sine_rows
    inside = mm_left(sine_rows, mm_left(sine_rows, q_mixed) * t.weight[...])
    rows = inside.shape[0]
    ends = t.ends
    left = jnp.sum(inside * ends[0:1], axis=1, keepdims=True)
    right = jnp.sum(inside * ends[1:2], axis=1, keepdims=True)
    return inside[0:1], inside[rows - 1 : rows], left, right


def side_lanes(parts, last=None):
    rows, cols = parts[0].shape
    lane = iota((rows, 128), 1)
    tall = [jnp.where(lane == 127, p[:, cols - 128 :], p[:, :128]) for p in parts]
    if last is not None:
        tall.append(jnp.where(lane == 127, last[1], last[0]))
    while len(tall) < 4:
        tall.append(jnp.zeros((rows, 128), F32))
    turned = jnp.concatenate(tall, axis=0).T
    return turned[0:1], turned[127:128]


def stencil(values, before, after, left, right):
    rows, cols = values.shape
    row, col = iota(values.shape, 0), iota(values.shape, 1)
    up = jnp.where(row == 0, before, pltpu.roll(values, 1, 0))
    down = jnp.where(row == rows - 1, after, pltpu.roll(values, rows - 1, 0))
    west = jnp.where(col == 0, left, pltpu.roll(values, 1, 1))
    east = jnp.where(col == cols - 1, right, pltpu.roll(values, cols - 1, 1))
    return (up + down) + (west + east)


def to_line(spread, block_cols):
    own = iota(spread.shape, 1) // block_cols == iota(spread.shape, 0)
    return jnp.sum(jnp.where(own, spread, 0.0), axis=0, keepdims=True)


def zone_totals(surface, zone_line, down, zones):
    rows, cols = surface.shape
    sums = [jnp.sum(surface[8 * i : 8 * i + 8], axis=0, keepdims=True) for i in range(rows // 8)]
    sums = jnp.concatenate(sums + [jnp.zeros((8 - rows // 8, cols), F32)], axis=0)
    line = to_line(mm_exact(sums, down), cols // 8)
    blocks = zone_line.shape[1]
    hot = (iota((zones, blocks), 0) == zone_line.astype(jnp.int32)).astype(F32).astype(BF16)
    line = jnp.broadcast_to(line, (8, blocks))
    return mm_exact(line, hot, DIMS_T)[0:1]


def field_rows(lines, down, block_rows, block_cols):
    row, place = iota((8, lines[0][0].shape[1]), 0), iota((8, lines[0][0].shape[1]), 1) // block_cols
    picked = jnp.zeros(row.shape, F32)
    for index, (line, wanted) in enumerate(lines):
        picked = jnp.where((row == index) & (place == wanted), line, picked)
    return mm_exact(picked, down, DIMS_T), picked


def spread_rows8(lines, rows):
    return jnp.concatenate(
        [jnp.broadcast_to(lines[i : i + 1], (8, lines.shape[1])) for i in range(rows // 8)], axis=0
    )


def smooth(first_rows, last_rows, edges, q_mixed, slab, group, groups, t):
    devices = first_rows.shape[0]
    slabs = devices // groups
    rows, cols = q_mixed.shape
    before = jnp.zeros_like(first_rows)
    after = jnp.zeros_like(first_rows)
    chain = t.row_chain
    for back in range(slabs):
        turned_first = pltpu.roll(first_rows, groups * back, 0) if back else first_rows
        turned_last = pltpu.roll(last_rows, groups * back, 0) if back else last_rows
        line = [chain[slabs * kind + back : slabs * kind + back + 1] for kind in range(4)]
        before = before + (line[0] * turned_first + line[1] * turned_last)
        after = after + (line[2] * turned_first + line[3] * turned_last)
    mine = iota(before.shape, 0) == slab * groups + group
    own_before = jnp.sum(jnp.where(mine, before, 0.0), axis=0, keepdims=True)
    own_after = jnp.sum(jnp.where(mine, after, 0.0), axis=0, keepdims=True)
    answer = t.answer
    edges = edges + mm(jnp.concatenate([before, after], axis=1), answer)
    tile, per = max(8, groups), 128 // rows
    lane = iota(edges.shape, 1) // rows
    lines = []
    for side in range(2):
        joined = jnp.zeros_like(edges)
        for i in range(per):
            moved = pltpu.roll(edges, rows * (i - side) % 128, 1) if i != side else edges
            moved = pltpu.roll(moved, devices - groups * i, 0) if i else moved
            joined = jnp.where(lane == i, moved, joined)
        step = per * groups
        lines.append(jnp.concatenate([joined[step * p : step * p + tile] for p in range(slabs // per)], axis=1))
    waves = t.waves
    waved = mm(jnp.concatenate(lines, axis=0), waves)
    count = waved.shape[1]
    firsts, lasts = waved[:tile], waved[tile:]
    chain = t.own_columns
    table = [chain[tile * kind : tile * (kind + 1)] for kind in range(4)]
    left = jnp.sum(table[0] * firsts + table[1] * lasts, axis=0, keepdims=True)
    right = jnp.sum(table[2] * firsts + table[3] * lasts, axis=0, keepdims=True)
    row = iota((8, count), 0)
    sides = jnp.where(row == 0, left, jnp.where(row == 1, right, 0.0))
    own_rows = pl.ds(pl.multiple_of(slab * rows, rows), rows)
    columns = mm_left([waves[0, own_rows, :], waves[1, own_rows, :]], sides, DIMS_T)
    left_col, right_col = columns[:, 0:1], columns[:, 1:2]
    around = t.around
    north, south = around[0:1], around[1:2]
    four = jnp.where(
        row == 0,
        north * left,
        jnp.where(row == 1, north * right, jnp.where(row == 2, south * left, jnp.where(row == 3, south * right, 0.0))),
    )
    four = mm(four, t.wave_weight)
    ends = t.ends
    first, last = ends[0:1], ends[1:2]
    north_row = own_before + PRECOND_T * (first * four[0:1] + last * four[1:2])
    south_row = own_after + PRECOND_T * (first * four[2:3] + last * four[3:4])
    place = iota((rows, cols), 0)
    loaded = q_mixed + PRECOND_T * (
        jnp.where(place == 0, north_row, 0.0)
        + jnp.where(place == rows - 1, south_row, 0.0)
        + left_col * first
        + right_col * last
    )
    sine_rows = t.sine_rows
    inside = mm_left(sine_rows, mm_left(sine_rows, loaded) * t.weight[...])
    pad = jnp.zeros((6, cols), F32)
    whole = mm(jnp.concatenate([inside, north_row, south_row, pad], axis=0), t.sine_cols)
    return whole[:rows], whole[rows : rows + 1], whole[rows + 1 : rows + 2], left_col, right_col


class Operands:
    def __init__(self, copies, buffers):
        self._copies, self._buffers = copies, buffers

    def __getattr__(self, name):
        if name in self._copies:
            self._copies.pop(name).wait()
        return self._buffers[name]


def call(body, ins, outs):
    names, results = list(ins), list(outs)
    pairs = [value if isinstance(value, tuple) else (value, ()) for value in ins.values()]
    arrays = [array for array, _ in pairs]
    copied = [place for place, (_, part) in enumerate(pairs) if part is not None]

    def shape_of(array, part):
        if isinstance(part, str):
            return array.shape[1:]
        return tuple(len(range(*cut.indices(size))) for cut, size in zip(part, array.shape)) + array.shape[len(part) :]

    def kernel(*refs):
        given, refs = refs[: len(names)], refs[len(names) :]
        made, refs = refs[: len(results)], refs[len(results) :]
        held, refs = refs[: len(copied)], refs[len(copied) :]
        built, (in_sems, out_sems) = refs[: len(results)], refs[len(results) :]
        copies = {}
        for slot, place in enumerate(copied):
            part = pairs[place][1]
            origin = given[place].at[lax.axis_index(part) if isinstance(part, str) else part] if part else given[place]
            copies[names[place]] = pltpu.make_async_copy(origin, held[slot], in_sems.at[slot])
            copies[names[place]].start()
        sent = []

        def done(*buffers):
            for buffer in buffers:
                place = [other is buffer for other in built].index(True)
                sent.append(pltpu.make_async_copy(buffer, made[place], out_sems.at[place]))
                sent[-1].start()

        get = Operands(copies, {names[place]: buffer for place, buffer in zip(copied, held)})
        body(get, SimpleNamespace(**dict(zip(results, built))), done)
        for place in copied:
            getattr(get, names[place])
        assert len(sent) == len(results)
        for copy in sent:
            copy.wait()

    buffers = [pltpu.VMEM(shape_of(*pairs[place]), arrays[place].dtype) for place in copied]
    made = pl.pallas_call(
        kernel,
        out_shape=[jax.ShapeDtypeStruct(outs[name], F32) for name in results],
        in_specs=[pl.BlockSpec(memory_space=pl.ANY)] * len(names),
        out_specs=[pl.BlockSpec(memory_space=pl.ANY)] * len(results),
        scratch_shapes=buffers
        + [pltpu.VMEM(outs[name], F32) for name in results]
        + [pltpu.SemaphoreType.DMA((len(copied),)), pltpu.SemaphoreType.DMA((len(results),))],
        compiler_params=pltpu.CompilerParams(vmem_limit_bytes=VMEM_LIMIT),
    )(*arrays)
    return SimpleNamespace(**dict(zip(results, made)))


def shards(
    source,
    conductivity,
    leakance,
    storage,
    et_rate,
    zone_of_block,
    zone_recharge,
    zone_weight,
    pair_zones,
    pair_weight,
):
    slabs, groups = lax.axis_size("slab"), lax.axis_size("grp")
    layers, rows, cols = source.shape
    devices = slabs * groups
    zones = zone_weight.shape[0]
    tables = {name: jnp.asarray(table) for name, table in grid_tables(slabs, groups, rows, cols).items()}
    t = SimpleNamespace(**tables)
    t.own_columns, t.around = (t.own_columns, "grp"), (t.around, "slab")
    block_rows, block_cols = rows // 8, cols // 8
    blocks = block_rows * block_cols
    at_zones = 2 * cols
    at_sides = at_zones + blocks
    widths = (at_sides + 5 * 128, at_zones + zones + 2 * 128)
    area = (layers, rows, cols)

    def neighbours(first, last):
        return (
            lax.ppermute(last, "slab", [(i, i + 1) for i in range(slabs - 1)]),
            lax.ppermute(first, "slab", [(i + 1, i) for i in range(slabs - 1)]),
        )

    def exchange(chunk):
        return lax.all_to_all(chunk, BOTH, split_axis=0, concat_axis=0, tiled=True)

    def start_body(get, out, done):
        ids = get.zone_of_block[...].astype(F32)
        ids = jnp.concatenate([ids, jnp.zeros((8 - block_rows, block_cols), F32)], axis=0)
        zone_line = to_line(mm_f32(ids, get.place[...]), block_cols)
        index = jnp.broadcast_to(zone_line, (8, blocks)).astype(jnp.int32)
        found = lookup(get.zone_recharge[...], index)[0:1]
        field, _ = field_rows([(found, i) for i in range(block_rows)], get.down[...], block_rows, block_cols)
        source_ref, rhs = get.source, out.rhs
        rhs[0] = source_ref[0] + spread_rows8(field, rows)
        for layer in range(1, layers):
            rhs[layer] = source_ref[layer]
        done(out.rhs)
        total = rhs[0]
        for layer in range(1, layers):
            total = total + rhs[layer]
        q_mixed = mm(total, get.sine_cols)
        out.q_mixed[...] = q_mixed
        done(out.q_mixed)
        cond, store, leak = get.conductivity, get.storage, get.leakance
        partial, halo = out.partial, (out.first, out.last)
        for layer in range(layers):
            own = cond[layer]
            diagonal = store[layer] + 0.5 * (4.0 * own + stencil(own, 0.0, 0.0, 0.0, 0.0))
            if layer < layers - 1:
                diagonal = diagonal + leak[layer]
            if layer > 0:
                diagonal = diagonal + leak[layer - 1]
            if layer == 0:
                diagonal = diagonal + get.et_rate[...]
            partial[layer] = diagonal
            for end, row in enumerate((0, rows - 1)):
                halo[end][layer : layer + 1] = own[row : row + 1]
                halo[end][layers + layer : layers + layer + 1] = diagonal[row : row + 1]
                halo[end][2 * layers + layer : 2 * layers + layer + 1] = rhs[layer, row : row + 1]
        done(out.partial, out.first, out.last)
        first, last, left, right = rings(q_mixed, get)
        line, chunk = out.line, out.chunk
        line[:, :cols] = first
        line[:, cols : 2 * cols] = last
        line[:, at_zones:at_sides] = zone_line
        west, east = side_lanes([rhs[layer] for layer in range(layers)], (left, right))
        line[:, at_sides : at_sides + 128] = west
        line[:, at_sides + 128 : at_sides + 256] = east
        west, east = side_lanes(
            [cond[layer] for layer in range(layers)], (partial[0, :, 0:1], partial[0, :, cols - 1 : cols])
        )
        line[:, at_sides + 256 : at_sides + 384] = west
        line[:, at_sides + 384 : at_sides + 512] = east
        west, east = side_lanes([partial[layer] for layer in range(1, layers)])
        line[:, at_sides + 512 :] = jnp.where(iota((1, 128), 1) < 64, west, pltpu.roll(east, 64, 1))
        chunk[...] = jnp.broadcast_to(line[...][None], chunk.shape)
        done(out.chunk, out.line)

    started = call(
        start_body,
        dict(
            zone_of_block=zone_of_block,
            zone_recharge=zone_recharge[None],
            place=t.place,
            down=t.down,
            source=source,
            sine_cols=t.sine_cols,
            conductivity=conductivity,
            storage=storage,
            leakance=leakance,
            et_rate=et_rate,
            sine_rows=t.sine_rows,
            weight=t.weight,
            ends=t.ends,
        ),
        dict(
            rhs=area,
            q_mixed=(rows, cols),
            partial=area,
            first=(3 * layers, cols),
            last=(3 * layers, cols),
            line=(1, widths[0]),
            chunk=(devices, 1, widths[0]),
        ),
    )
    rhs = started.rhs
    received = first_received = exchange(started.chunk)
    halo_north, halo_south = neighbours(started.first, started.last)
    first_north, first_south = halo_north, halo_south

    def couple_body(get, out, done):
        ids, weights = get.pair_zones, get.pair_weight
        place = iota((zones, ids.shape[1]), 0)
        table = (place == ids[0:1]).astype(F32) - (place == ids[1:2]).astype(F32)
        matrix = mm_f32(table * weights[...], table, DIMS_T)
        own = iota((zones, zones), 0) == iota((zones, zones), 1)
        matrix = matrix + jnp.where(own, get.zone_weight[...], 0.0)
        out.couple[...] = (COUPLE * zones / (slabs * rows * groups * cols)) * matrix
        done(out.couple)

    couple = call(
        couple_body,
        dict(pair_zones=pair_zones.T, pair_weight=pair_weight[None], zone_weight=zone_weight[None]),
        dict(couple=(zones, zones)),
    ).couple

    def step_body(number, get, out, done):
        coupled, final = number > 0, number == 2
        slab, group = lax.axis_index("slab"), lax.axis_index("grp")
        own = slab * groups + group
        has_north = (slab > 0).astype(F32)
        has_south = (slab < slabs - 1).astype(F32)
        has_west = (group > 0).astype(F32)
        has_east = (group < groups - 1).astype(F32)
        recv = get.received

        def of(shift, start):
            return recv[pl.ds(jnp.clip(own + shift, 0, devices - 1), 1), 0, start : start + 128]

        first_rows, last_rows = recv[:, 0, :cols], recv[:, 0, cols : 2 * cols]
        sides_at = at_sides if not coupled else at_zones + zones
        lane = iota((devices, 128), 1)
        edges = jnp.where(
            lane < rows,
            pltpu.roll(recv[:, 0, sides_at : sides_at + 128], rows, 1),
            pltpu.roll(recv[:, 0, sides_at + 128 : sides_at + 256], 2 * rows, 1),
        )
        edges = jnp.where(lane < 2 * rows, edges, 0.0)
        q_in = get.q_mixed[...]
        w_ref = get.w
        surface = w_ref[0]
        if coupled:
            totals = jnp.sum(recv[:, 0, at_zones : at_zones + zones], axis=0, keepdims=True)
            reply = mm_f32(jnp.broadcast_to(totals, (8, zones)), get.couple[...])[0:1]
            every = lookup(reply, get.zone_map[:, 0, :].astype(jnp.int32))
            coarse = mm(every, get.coarse)
            first_rows = first_rows + coarse[:, :cols]
            last_rows = last_rows + coarse[:, cols : 2 * cols]
            edges = edges + coarse[:, 2 * cols :]
            device = iota(every.shape, 0)
            line_of = lambda shift: jnp.sum(
                jnp.where(device == own + shift, every, 0.0), axis=0, keepdims=True
            )
            mine = line_of(0)
            wanted = [(mine, i) for i in range(block_rows)]
            wanted += [(line_of(-groups), block_rows - 1), (line_of(groups), 0)]
            field, picked = field_rows(wanted, get.down[...], block_rows, block_cols)
            modes = mm(picked, get.up_modes)
            q_in = q_in + spread_rows8(modes, rows)
            surface = surface + spread_rows8(field, rows)
            column = iota((rows, blocks), 1)
            base = block_cols * (iota((rows, blocks), 0) // 8)
            west_value = jnp.sum(
                jnp.where(column == base + block_cols - 1, line_of(-1), 0.0), axis=1, keepdims=True
            )
            east_value = jnp.sum(jnp.where(column == base, line_of(1), 0.0), axis=1, keepdims=True)
        if final:
            out.w[0] = surface
            for layer in range(1, layers):
                out.w[layer] = w_ref[layer]
            done(out.w)
        elif coupled:
            out.w[0] = surface
            for layer in range(1, layers):
                out.w[layer] = w_ref[layer]
            done(out.w)
        s, s_north, s_south, s_west, s_east = smooth(
            first_rows, last_rows, edges, q_in, slab, group, groups, get
        )
        cond, leak = get.conductivity, get.leakance
        north_ref, south_ref = get.north, get.south
        row, col = iota((rows, cols), 0), iota((rows, cols), 1)
        if coupled:
            cond_north, cond_south = get.first_north, get.first_south
            sides = get.sides
            lanes = [of(-1, sides_at + 128), of(1, sides_at)]
            diagonal_ref, inverse_ref = get.diagonal, get.inverse
            beside = get.beside
        else:
            cond_north, cond_south = north_ref, south_ref
            lanes = [of(-1, sides_at + 128), of(1, sides_at)]
            lanes += [of(-1, sides_at + 384) * has_west, of(1, sides_at + 256) * has_east]
            lanes += [of(-1, sides_at + 512), of(1, sides_at + 512)]
            diagonal_ref, inverse_ref, sides, beside = out.diagonal, out.inverse, out.sides, out.beside
        turned = jnp.concatenate(lanes + [jnp.zeros((128 - len(lanes), 128), F32)], axis=0).T
        if not coupled:
            corner = [
                of(-groups - 1, sides_at + 384) * (has_north * has_west),
                of(-groups + 1, sides_at + 256) * (has_north * has_east),
                of(groups - 1, sides_at + 384) * (has_south * has_west),
                of(groups + 1, sides_at + 256) * (has_south * has_east),
            ]
            ghosts = []
            partial = get.partial
            line_col, line_row = iota((1, cols), 1), iota((rows, 1), 0)
            for layer in range(layers):
                c_north, c_south = north_ref[layer : layer + 1], south_ref[layer : layer + 1]
                c_west = turned[rows * layer : rows * (layer + 1), 2:3]
                c_east = turned[rows * layer : rows * (layer + 1), 3:4]
                both = jnp.where(lane[:rows] == 0, c_west, jnp.where(lane[:rows] == 1, c_east, 0.0))
                sides[layer] = both
                diagonal = partial[layer] + 0.5 * (
                    jnp.where(row == 0, c_north, 0.0)
                    + jnp.where(row == rows - 1, c_south, 0.0)
                    + jnp.where(col == 0, c_west, 0.0)
                    + jnp.where(col == cols - 1, c_east, 0.0)
                )
                diagonal_ref[layer] = diagonal
                inverse_ref[layer] = 1.0 / diagonal
                start, end = rows * layer, rows * layer + rows - 1
                nw, ne = corner[0][:, end : end + 1], corner[1][:, end : end + 1]
                sw, se = corner[2][:, start : start + 1], corner[3][:, start : start + 1]
                own_cond = cond[layer]
                d_north = north_ref[layers + layer : layers + layer + 1] + 0.5 * (
                    own_cond[0:1] + jnp.where(line_col == 0, nw, jnp.where(line_col == cols - 1, ne, 0.0))
                )
                d_south = south_ref[layers + layer : layers + layer + 1] + 0.5 * (
                    own_cond[rows - 1 : rows]
                    + jnp.where(line_col == 0, sw, jnp.where(line_col == cols - 1, se, 0.0))
                )
                if layer == 0:
                    west, east = turned[3 * rows : 4 * rows, 2:3], turned[3 * rows : 4 * rows, 3:4]
                else:
                    west = turned[64 + rows * (layer - 1) : 64 + rows * layer, 4:5]
                    east = turned[rows * (layer - 1) : rows * layer, 5:6]
                d_west = west + 0.5 * (
                    own_cond[:, 0:1] + jnp.where(line_row == 0, nw, jnp.where(line_row == rows - 1, sw, 0.0))
                )
                d_east = east + 0.5 * (
                    own_cond[:, cols - 1 : cols]
                    + jnp.where(line_row == 0, ne, jnp.where(line_row == rows - 1, se, 0.0))
                )
                ghosts.append((1.0 / d_north, 1.0 / d_south, 1.0 / d_west, 1.0 / d_east))
            sides[layers] = jnp.where(lane[:rows] == 0, ghosts[0][2], jnp.where(lane[:rows] == 1, ghosts[0][3], 0.0))
            beside[0:1] = ghosts[0][0]
            beside[1:2] = ghosts[0][1]
            done(out.diagonal, out.inverse, out.sides, out.beside)
        v_out, image_out = out.v, out.image
        fields, outside = [], []
        for layer in range(layers):
            value = (surface if layer == 0 else w_ref[layer]) * inverse_ref[layer] + s
            v_out[layer] = value
            fields.append(value)
            west = turned[rows * layer : rows * (layer + 1), 0:1]
            east = turned[rows * layer : rows * (layer + 1), 1:2]
            if coupled:
                north, south = north_ref[layer : layer + 1], south_ref[layer : layer + 1]
                if layer == 0:
                    north = north + beside[0:1] * field[block_rows : block_rows + 1]
                    south = south + beside[1:2] * field[block_rows + 1 : block_rows + 2]
                    west = west + sides[layers, :, 0:1] * west_value
                    east = east + sides[layers, :, 1:2] * east_value
            else:
                near = ghosts[layer]
                place = 2 * layers + layer
                north, south = north_ref[place : place + 1] * near[0], south_ref[place : place + 1] * near[1]
                west, east = west * near[2], east * near[3]
            outside.append(
                (
                    (north + s_north) * has_north,
                    (south + s_south) * has_south,
                    (west + s_west) * has_west,
                    (east + s_east) * has_east,
                )
            )
        done(out.v)
        images = []
        for layer in range(layers):
            value, own_cond = fields[layer], cond[layer]
            north, south, west, east = outside[layer]
            plain = stencil(value, north, south, west, east)
            carried = stencil(
                value * own_cond,
                north * cond_north[layer : layer + 1],
                south * cond_south[layer : layer + 1],
                west * sides[layer, :, 0:1],
                east * sides[layer, :, 1:2],
            )
            image = diagonal_ref[layer] * value - 0.5 * (own_cond * plain + carried)
            if layer < layers - 1:
                image = image - leak[layer] * fields[layer + 1]
            if layer > 0:
                image = image - leak[layer - 1] * fields[layer - 1]
            image_out[layer] = image
            images.append(image)
        done(out.image)
        line, chunk = out.line, out.chunk
        totals = zone_totals(fields[0], get.zone_line[:, at_zones:at_sides], get.down[...], zones)
        if final:
            rhs_ref, v0_ref, v1_ref, w0_ref = get.rhs, get.v0, get.v1, get.w0

            def dot(left, right):
                total = left[0] * right[0]
                for layer in range(1, layers):
                    total = total + left[layer] * right[layer]
                return jnp.sum(jnp.sum(total, axis=0, keepdims=True), axis=1, keepdims=True)

            w1 = [surface] + [w_ref[layer] for layer in range(1, layers)]
            products = [
                dot(v0_ref, w0_ref), dot(v0_ref, w1), dot(v1_ref, w1), dot(fields, w0_ref), dot(fields, w1),
                dot(fields, images), dot(v0_ref, rhs_ref), dot(v1_ref, rhs_ref), dot(fields, rhs_ref),
            ]
            packed = jnp.zeros((1, 128), F32)
            for place, value in enumerate(products):
                packed = jnp.where(iota((1, 128), 1) == place, value, packed)
            line[:, :zones] = totals
            line[:, zones:] = packed
        else:
            depth = images[0]
            for layer in range(1, layers):
                depth = depth + images[layer]
            q_next = mm(depth, get.sine_cols)
            out.q_mixed[...] = q_next
            done(out.q_mixed)
            scaled = [images[layer] * inverse_ref[layer] for layer in range(layers)]
            for layer in range(layers):
                out.first[layer : layer + 1] = scaled[layer][0:1]
                out.last[layer : layer + 1] = scaled[layer][rows - 1 : rows]
            done(out.first, out.last)
            first, last, left, right = rings(q_next, get)
            west, east = side_lanes(scaled, (left, right))
            line[:, :cols] = first
            line[:, cols : 2 * cols] = last
            line[:, at_zones : at_zones + zones] = totals
            line[:, at_zones + zones : at_zones + zones + 128] = west
            line[:, at_zones + zones + 128 :] = east
        chunk[...] = jnp.broadcast_to(line[...][None], chunk.shape)
        done(out.chunk, out.line)

    tail_width = zones + 128
    shared = {}

    def step(number, received, q_mixed, w, north, south, more=()):
        ins = dict(received=received)
        if number > 0:
            ins |= dict(couple=couple, zone_map=zone_map, coarse=t.coarse)
        ins |= dict(row_chain=t.row_chain, answer=t.answer, q_mixed=q_mixed, w=w, down=t.down)
        if number > 0:
            ins |= dict(up_modes=t.up_modes)
        ins |= dict(waves=t.waves, own_columns=t.own_columns, around=t.around, wave_weight=t.wave_weight)
        ins |= dict(ends=t.ends, sine_rows=t.sine_rows, weight=t.weight, sine_cols=t.sine_cols)
        ins |= dict(north=north, south=south, conductivity=conductivity, leakance=leakance)
        ins |= dict(zone_line=started.line)
        outs = dict(v=area, image=area)
        if number > 0:
            ins |= dict(first_north=first_north, first_south=first_south) | shared
            outs |= dict(w=area)
        else:
            ins |= dict(partial=started.partial, couple=(couple, None))
            outs |= dict(diagonal=area, inverse=area, sides=(layers + 1, rows, 128), beside=(2, cols))
        ins |= dict(more)
        if number == 2:
            outs |= dict(line=(1, tail_width), chunk=(devices, 1, tail_width))
        else:
            outs |= dict(
                q_mixed=(rows, cols), first=(layers, cols), last=(layers, cols), line=(1, widths[1]), chunk=(devices, 1, widths[1])
            )
        return call(lambda get, out, done: step_body(number, get, out, done), ins, outs)

    one = step(0, received, started.q_mixed, rhs, halo_north, halo_south)
    shared.update(diagonal=one.diagonal, inverse=one.inverse, sides=one.sides, beside=one.beside)
    zone_map = (first_received, (slice(None), slice(None), slice(at_zones, at_sides)))
    received = exchange(one.chunk)
    halo_north, halo_south = neighbours(one.first, one.last)
    two = step(1, received, one.q_mixed, one.image, halo_north, halo_south)
    received = exchange(two.chunk)
    halo_north, halo_south = neighbours(two.first, two.last)
    more = dict(rhs=rhs, v0=one.v, v1=two.v, w0=two.w)
    three = step(2, received, two.q_mixed, two.image, halo_north, halo_south, more)
    received = exchange(three.chunk)

    def finish_body(get, out, done):
        sums = jnp.sum(get.received[:, 0, :], axis=0, keepdims=True)
        totals = sums[:, :zones]
        reply = mm_f32(jnp.broadcast_to(totals, (8, zones)), get.couple[...])
        zone_line = get.zone_line[:, at_zones:at_sides]
        index = jnp.broadcast_to(zone_line, (8, blocks)).astype(jnp.int32)
        found = lookup(reply[0:1], index)[0:1]
        field, _ = field_rows([(found, i) for i in range(block_rows)], get.down[...], block_rows, block_cols)
        coupled = spread_rows8(field, rows)
        a00, a01, a11, a02, a12, a22, h0, h1, h2 = [sums[:, zones + i : zones + i + 1] for i in range(9)]
        a22 = a22 + jnp.sum(totals * reply[0:1], axis=1, keepdims=True)
        l10, l20 = a01 / a00, a02 / a00
        d1 = a11 - l10 * a01
        l21 = (a12 - l10 * a02) / d1
        d2 = a22 - l20 * a02 - l21 * (a12 - l10 * a02)
        y1 = h1 - l10 * h0
        y2 = h2 - l20 * h0 - l21 * y1
        c2 = y2 / d2
        c1 = y1 / d1 - l21 * c2
        c0 = h0 / a00 - l10 * c1 - l20 * c2
        v0, v1, v2, w0, w1, w2 = get.v0, get.v1, get.v2, get.w0, get.w1, get.w2
        rhs_ref = get.rhs
        for layer in range(layers):
            last = w2[layer] + coupled if layer == 0 else w2[layer]
            out.solution[layer] = c0 * v0[layer] + c1 * v1[layer] + c2 * v2[layer]
            out.residual[layer] = rhs_ref[layer] - c0 * w0[layer] - c1 * w1[layer] - c2 * last
        done(out.solution, out.residual)

    ended = call(
        finish_body,
        dict(received=received, couple=couple, zone_line=started.line, down=t.down)
        | dict(rhs=rhs, v0=one.v, v1=two.v, v2=three.v, w0=two.w, w1=three.w, w2=three.image),
        dict(solution=area, residual=area),
    )
    return ended.solution, ended.residual


def solution(mesh):
    placed = (
        P(None, "slab", "grp"),
        P(None, "slab", "grp"),
        P(None, "slab", "grp"),
        P(None, "slab", "grp"),
        P("slab", "grp"),
        P("slab", "grp"),
        P(),
        P(),
        P(),
        P(),
    )
    return jax.shard_map(
        shards,
        mesh=mesh,
        in_specs=placed,
        out_specs=(P(None, "slab", "grp"), P(None, "slab", "grp")),
        check_vma=False,
    )
```

```python
import math
from types import SimpleNamespace

import jax
import jax.numpy as jnp
import numpy as np
from jax import lax
from jax.experimental import pallas as pl
from jax.experimental.pallas import tpu as pltpu
from jax.sharding import PartitionSpec as P

COUPLE = 4.0
PRECOND_T = 2.0
PRECOND_SHIFT = 3.0
HIGHEST = lax.Precision.HIGHEST
BOTH = ("slab", "grp")
VMEM_LIMIT = 64 * 1024 * 1024
F32, BF16 = jnp.float32, jnp.bfloat16


def sine_basis(count):
    index = np.arange(1, count + 1)
    basis = math.sqrt(2.0 / (count + 1)) * np.sin(np.pi * np.outer(index, index) / (count + 1))
    return basis, 4.0 * np.sin(np.pi * index / (2.0 * (count + 1))) ** 2


def fourier_basis(count):
    cells = np.arange(count)[:, None]
    waves = np.concatenate([np.arange(count // 2 + 1), np.arange(1, count // 2)])[None, :]
    turned = 2.0 * np.pi * ((cells * waves) % count) / count
    is_sine = np.arange(count)[None, :] > count // 2
    basis = np.where(is_sine, np.sin(turned), np.cos(turned)) * math.sqrt(2.0 / count)
    basis[:, 0] /= math.sqrt(2.0)
    basis[:, count // 2] /= math.sqrt(2.0)
    return basis, 4.0 * np.sin(np.pi * waves[0] / count) ** 2


def chain_tables(cross, total, block):
    half = (PRECOND_SHIFT / PRECOND_T + cross) / 2.0 + 1.0
    decay = 1.0 / (half + np.sqrt(half * half - 1.0))
    scale = 1.0 / ((1.0 - decay**total) * PRECOND_T * (1.0 / decay - decay))

    def green(distance):
        distance = distance % total
        return PRECOND_T * scale * (decay**distance + decay ** (total - distance))

    count = total // block
    tables = np.zeros((4, count, len(cross)))
    for back in range(count):
        tables[0, back] = green(block * back)
        tables[1, back] = green(block * (back - 1) - 1) + (1.0 if back == 1 % count else 0.0)
        tables[2, back] = green(block * (back + 1) + 1) + (1.0 if back == count - 1 else 0.0)
        tables[3, back] = green(block * back)
    return tables


def grid_tables(slabs, groups, rows, cols):
    rows_total, cols_total = slabs * rows, groups * cols
    sine_rows, cross_rows = sine_basis(rows)
    sine_cols, cross_cols = sine_basis(cols)
    waves, cross_waves = fourier_basis(rows_total)
    weight = 1.0 / (PRECOND_SHIFT + PRECOND_T * (cross_rows[:, None] + cross_cols[None, :]))
    wave_weight = 1.0 / (PRECOND_SHIFT + PRECOND_T * (cross_waves[:, None] + cross_cols[None, :]))
    first, last = sine_cols[0], sine_cols[-1]
    answer = np.zeros((cols, 128))
    for end, row in enumerate((0, rows - 1)):
        inside = PRECOND_T * np.einsum("ri,ij,i->jr", sine_rows, weight, sine_rows[:, row])
        answer[:, 64 * end : 64 * end + rows] = first[:, None] * inside
        answer[:, 64 * end + rows : 64 * end + 2 * rows] = last[:, None] * inside
    spread_rows = np.repeat(np.eye(rows // 8), 8, axis=0)
    spread_cols = np.repeat(np.eye(cols // 8), 8, axis=0)
    mode_rows, mode_cols = sine_rows @ spread_rows, sine_cols @ spread_cols
    mixed = np.einsum("ri,ij,ib->rbj", sine_rows, weight, mode_rows)
    coarse = np.zeros((rows // 8, cols // 8, 128))
    coarse[:, :, :rows] = np.einsum("rbj,j,jc->bcr", mixed, first, mode_cols)
    coarse[:, :, rows : 2 * rows] = np.einsum("rbj,j,jc->bcr", mixed, last, mode_cols)
    column_chain = chain_tables(cross_waves, cols_total, cols)
    tile = max(8, groups)
    own_columns = np.zeros((groups, 4, tile, rows_total))
    for group in range(groups):
        for other in range(groups):
            own_columns[group, :, other] = column_chain[:, (group - other) % groups]
    around = np.zeros((slabs, 8, rows_total))
    for slab in range(slabs):
        around[slab, 0] = waves[(rows * slab - 1) % rows_total]
        around[slab, 1] = waves[(rows * slab + rows) % rows_total]
    ends = np.zeros((8, cols))
    ends[0], ends[1] = first, last
    blocks = (rows // 8) * (cols // 8)
    down = np.tile(spread_cols, (1, rows // 8))
    exact = dict(
        weight=weight,
        row_chain=chain_tables(cross_cols, rows_total, rows).reshape(4 * slabs, cols),
        own_columns=own_columns.reshape(groups, 4 * tile, rows_total),
        around=around,
        ends=ends,
        coarse_rows=np.concatenate([mixed[0], mixed[-1]]),
    )
    split = dict(
        sine_rows=sine_rows,
        sine_cols=sine_cols,
        answer=answer,
        coarse=coarse.reshape(blocks, 128),
        waves=waves,
        wave_weight=wave_weight,
        up_modes=np.tile(mode_cols.T, (128 // (cols // 8), 1)),
    )
    tables = {name: np.asarray(table, np.float32) for name, table in exact.items()}
    for name, table in split.items():
        high = table.astype(jnp.bfloat16)
        tables[name] = np.stack([high, (table - high.astype(np.float64)).astype(jnp.bfloat16)])
    tables["down"] = down.astype(jnp.bfloat16)
    tables["place"] = np.tile(np.eye(cols // 8), (1, rows // 8)).astype(jnp.bfloat16)
    return tables


def terms(value, count):
    parts = []
    for _ in range(count):
        part = value.astype(BF16).astype(F32)
        parts.append(part)
        value = value - part
    return parts


DIMS = (((1,), (0,)), ((), ()))
DIMS_T = (((1,), (1,)), ((), ()))


def product(left, right, dims):
    return lax.dot_general(left, right, dims, preferred_element_type=F32)


def mm(value, table, dims=DIMS):
    rows = value.shape[0]
    high, low = terms(value, 2)
    both = product(jnp.concatenate([high, low], axis=0).astype(BF16), table[0], dims)
    return both[:rows] + both[rows:] + product(high.astype(BF16), table[1], dims)


def mm_left(table, value, dims=DIMS):
    rows = table[0].shape[0]
    high, low = terms(value, 2)
    both = product(jnp.concatenate([table[0], table[1]], axis=0), high.astype(BF16), dims)
    return both[:rows] + both[rows:] + product(table[0], low.astype(BF16), dims)


def mm_exact(value, table, dims=DIMS):
    rows = value.shape[0]
    every = product(jnp.concatenate(terms(value, 3), axis=0).astype(BF16), table, dims)
    return every[:rows] + every[rows : 2 * rows] + every[2 * rows :]


def mm_f32(left, right, dims=DIMS):
    return lax.dot_general(left, right, dims, precision=HIGHEST, preferred_element_type=F32)


def iota(shape, dim):
    return lax.broadcasted_iota(jnp.int32, shape, dim)


def lookup(values, index):
    rows, lanes = index.shape
    zones = values.shape[1]
    within, which = index & 127, index >> 7
    pieces = []
    for start in range(0, lanes, 128):
        part = jnp.zeros((rows, 128), F32)
        for half in range(zones // 128):
            table = jnp.broadcast_to(values[:, 128 * half : 128 * (half + 1)], (rows, 128))
            found = jnp.take_along_axis(table, within[:, start : start + 128], axis=1)
            part = jnp.where(which[:, start : start + 128] == half, found, part)
        pieces.append(part)
    return jnp.concatenate(pieces, axis=1) if len(pieces) > 1 else pieces[0]


def rings(q_mixed, t):
    sine_rows = t.sine_rows
    inside = mm_left(sine_rows, mm_left(sine_rows, q_mixed) * t.weight[...])
    rows = inside.shape[0]
    ends = t.ends
    left = jnp.sum(inside * ends[0:1], axis=1, keepdims=True)
    right = jnp.sum(inside * ends[1:2], axis=1, keepdims=True)
    return inside[0:1], inside[rows - 1 : rows], left, right


def side_lanes(parts, last=None):
    rows, cols = parts[0].shape
    lane = iota((rows, 128), 1)
    tall = [jnp.where(lane == 127, p[:, cols - 128 :], p[:, :128]) for p in parts]
    if last is not None:
        tall.append(jnp.where(lane == 127, last[1], last[0]))
    while len(tall) < 4:
        tall.append(jnp.zeros((rows, 128), F32))
    turned = jnp.concatenate(tall, axis=0).T
    return turned[0:1], turned[127:128]


def stencil(values, before, after, left, right):
    rows, cols = values.shape
    row, col = iota(values.shape, 0), iota(values.shape, 1)
    up = jnp.where(row == 0, before, pltpu.roll(values, 1, 0))
    down = jnp.where(row == rows - 1, after, pltpu.roll(values, rows - 1, 0))
    west = jnp.where(col == 0, left, pltpu.roll(values, 1, 1))
    east = jnp.where(col == cols - 1, right, pltpu.roll(values, cols - 1, 1))
    return (up + down) + (west + east)


def to_line(spread, block_cols):
    own = iota(spread.shape, 1) // block_cols == iota(spread.shape, 0)
    return jnp.sum(jnp.where(own, spread, 0.0), axis=0, keepdims=True)


def zone_totals(surface, hot, down):
    rows, cols = surface.shape
    sums = [jnp.sum(surface[8 * i : 8 * i + 8], axis=0, keepdims=True) for i in range(rows // 8)]
    sums = jnp.concatenate(sums + [jnp.zeros((8 - rows // 8, cols), F32)], axis=0)
    line = to_line(mm_exact(sums, down), cols // 8)
    line = jnp.broadcast_to(line, (8, line.shape[1]))
    return mm_exact(line, hot, DIMS_T)[0:1]


def field_rows(lines, down, block_cols):
    row, place = iota((8, lines[0][0].shape[1]), 0), iota((8, lines[0][0].shape[1]), 1) // block_cols
    picked = jnp.zeros(row.shape, F32)
    for index, (line, wanted) in enumerate(lines):
        picked = jnp.where((row == index) & (place == wanted), line, picked)
    return mm_exact(picked, down, DIMS_T)


def spread_rows8(lines, rows):
    return jnp.concatenate(
        [jnp.broadcast_to(lines[i : i + 1], (8, lines.shape[1])) for i in range(rows // 8)], axis=0
    )


def smooth(first_rows, last_rows, edges, q_mixed, slab, group, groups, t):
    devices = first_rows.shape[0]
    slabs = devices // groups
    rows, cols = q_mixed.shape
    before = jnp.zeros_like(first_rows)
    after = jnp.zeros_like(first_rows)
    chain = t.row_chain
    for back in range(slabs):
        turned_first = pltpu.roll(first_rows, groups * back, 0) if back else first_rows
        turned_last = pltpu.roll(last_rows, groups * back, 0) if back else last_rows
        line = [chain[slabs * kind + back : slabs * kind + back + 1] for kind in range(4)]
        before = before + (line[0] * turned_first + line[1] * turned_last)
        after = after + (line[2] * turned_first + line[3] * turned_last)
    mine = iota(before.shape, 0) == slab * groups + group
    own_before = jnp.sum(jnp.where(mine, before, 0.0), axis=0, keepdims=True)
    own_after = jnp.sum(jnp.where(mine, after, 0.0), axis=0, keepdims=True)
    answer = t.answer
    moved = mm(jnp.concatenate([before, after], axis=0), answer)
    lane = iota(edges.shape, 1)
    edges = edges + jnp.where(lane < 64, moved[:devices] + pltpu.roll(moved[devices:], 64, 1), 0.0)
    tile, per = max(8, groups), 128 // rows
    lane = iota(edges.shape, 1) // rows
    lines = []
    for side in range(2):
        joined = jnp.zeros_like(edges)
        for i in range(per):
            moved = pltpu.roll(edges, rows * (i - side) % 128, 1) if i != side else edges
            moved = pltpu.roll(moved, devices - groups * i, 0) if i else moved
            joined = jnp.where(lane == i, moved, joined)
        step = per * groups
        lines.append(jnp.concatenate([joined[step * p : step * p + tile] for p in range(slabs // per)], axis=1))
    waves = t.waves
    waved = mm(jnp.concatenate(lines, axis=0), waves)
    count = waved.shape[1]
    firsts, lasts = waved[:tile], waved[tile:]
    chain = t.own_columns
    table = [chain[tile * kind : tile * (kind + 1)] for kind in range(4)]
    left = jnp.sum(table[0] * firsts + table[1] * lasts, axis=0, keepdims=True)
    right = jnp.sum(table[2] * firsts + table[3] * lasts, axis=0, keepdims=True)
    row = iota((8, count), 0)
    sides = jnp.where(row == 0, left, jnp.where(row == 1, right, 0.0))
    own_rows = pl.ds(pl.multiple_of(slab * rows, rows), rows)
    columns = mm_left([waves[0, own_rows, :], waves[1, own_rows, :]], sides, DIMS_T)
    left_col, right_col = columns[:, 0:1], columns[:, 1:2]
    around = t.around
    north, south = around[0:1], around[1:2]
    four = jnp.where(
        row == 0,
        north * left,
        jnp.where(row == 1, north * right, jnp.where(row == 2, south * left, jnp.where(row == 3, south * right, 0.0))),
    )
    four = mm(four, t.wave_weight)
    ends = t.ends
    first, last = ends[0:1], ends[1:2]
    north_row = own_before + PRECOND_T * (first * four[0:1] + last * four[1:2])
    south_row = own_after + PRECOND_T * (first * four[2:3] + last * four[3:4])
    place = iota((rows, cols), 0)
    loaded = q_mixed + PRECOND_T * (
        jnp.where(place == 0, north_row, 0.0)
        + jnp.where(place == rows - 1, south_row, 0.0)
        + left_col * first
        + right_col * last
    )
    sine_rows = t.sine_rows
    inside = mm_left(sine_rows, mm_left(sine_rows, loaded) * t.weight[...])
    pad = jnp.zeros((6, cols), F32)
    whole = mm(jnp.concatenate([inside, north_row, south_row, pad], axis=0), t.sine_cols)
    return whole[:rows], whole[rows : rows + 1], whole[rows + 1 : rows + 2], left_col, right_col


class Operands:
    def __init__(self, copies, buffers):
        self._copies, self._buffers = copies, buffers

    def __getattr__(self, name):
        if name in self._copies:
            self._copies.pop(name).wait()
        return self._buffers[name]


def call(body, ins, outs):
    names, results = list(ins), list(outs)
    pairs = [value if isinstance(value, tuple) else (value, ()) for value in ins.values()]
    arrays = [array for array, _ in pairs]
    copied = [place for place, (_, part) in enumerate(pairs) if part is not None]

    def shape_of(array, part):
        if isinstance(part, str):
            return array.shape[1:]
        return tuple(len(range(*cut.indices(size))) for cut, size in zip(part, array.shape)) + array.shape[len(part) :]

    def kernel(*refs):
        given, refs = refs[: len(names)], refs[len(names) :]
        made, refs = refs[: len(results)], refs[len(results) :]
        held, refs = refs[: len(copied)], refs[len(copied) :]
        built, (in_sems, out_sems) = refs[: len(results)], refs[len(results) :]
        copies = {}
        for slot, place in enumerate(copied):
            part = pairs[place][1]
            origin = given[place].at[lax.axis_index(part) if isinstance(part, str) else part] if part else given[place]
            copies[names[place]] = pltpu.make_async_copy(origin, held[slot], in_sems.at[slot])
            copies[names[place]].start()
        sent = []

        def done(*buffers):
            for buffer in buffers:
                place = [other is buffer for other in built].index(True)
                sent.append(pltpu.make_async_copy(buffer, made[place], out_sems.at[place]))
                sent[-1].start()

        get = Operands(copies, {names[place]: buffer for place, buffer in zip(copied, held)})
        body(get, SimpleNamespace(**dict(zip(results, built))), done)
        for place in copied:
            getattr(get, names[place])
        assert len(sent) == len(results)
        for copy in sent:
            copy.wait()

    kinds = [value if isinstance(value[-1], type(F32)) else (value, F32) for value in outs.values()]
    buffers = [pltpu.VMEM(shape_of(*pairs[place]), arrays[place].dtype) for place in copied]
    made = pl.pallas_call(
        kernel,
        out_shape=[jax.ShapeDtypeStruct(*kind) for kind in kinds],
        in_specs=[pl.BlockSpec(memory_space=pl.ANY)] * len(names),
        out_specs=[pl.BlockSpec(memory_space=pl.ANY)] * len(results),
        scratch_shapes=buffers
        + [pltpu.VMEM(*kind) for kind in kinds]
        + [pltpu.SemaphoreType.DMA((len(copied),)), pltpu.SemaphoreType.DMA((len(results),))],
        compiler_params=pltpu.CompilerParams(vmem_limit_bytes=VMEM_LIMIT),
    )(*arrays)
    return SimpleNamespace(**dict(zip(results, made)))


def shards(
    source,
    conductivity,
    leakance,
    storage,
    et_rate,
    zone_of_block,
    zone_recharge,
    zone_weight,
    pair_zones,
    pair_weight,
):
    slabs, groups = lax.axis_size("slab"), lax.axis_size("grp")
    layers, rows, cols = source.shape
    devices = slabs * groups
    zones = zone_weight.shape[0]
    tables = {name: jnp.asarray(table) for name, table in grid_tables(slabs, groups, rows, cols).items()}
    t = SimpleNamespace(**tables)
    t.own_columns, t.around = (t.own_columns, "grp"), (t.around, "slab")
    block_rows, block_cols = rows // 8, cols // 8
    blocks = block_rows * block_cols
    at_zones = 2 * cols
    at_sides = at_zones + blocks
    widths = (at_sides + 5 * 128, at_zones + zones + 2 * 128)
    area = (layers, rows, cols)

    def neighbours(near, far):
        across = [(i, i + 1) for i in range(1, slabs - 1, 2)]
        return (
            lax.ppermute(near, "slab", [(i, i ^ 1) for i in range(slabs)]),
            lax.ppermute(far, "slab", across + [(j, i) for i, j in across]),
        )

    def choose(near, far):
        odd = lax.axis_index("slab") % 2 == 1
        return jnp.where(odd, near, far), jnp.where(odd, far, near)

    def exchange(chunk):
        return lax.all_to_all(chunk, BOTH, split_axis=0, concat_axis=0, tiled=True)

    def start_body(get, out, done):
        ids = get.zone_of_block[...].astype(F32)
        ids = jnp.concatenate([ids, jnp.zeros((8 - block_rows, block_cols), F32)], axis=0)
        zone_line = to_line(mm_exact(ids, get.place[...]), block_cols)
        index = jnp.broadcast_to(zone_line, (8, blocks)).astype(jnp.int32)
        found = lookup(get.zone_recharge[...], index)[0:1]
        field = field_rows([(found, i) for i in range(block_rows)], get.down[...], block_cols)
        source_ref, rhs = get.source, out.rhs
        rhs[0] = source_ref[0] + spread_rows8(field, rows)
        for layer in range(1, layers):
            rhs[layer] = source_ref[layer]
        done(out.rhs)
        total = rhs[0]
        for layer in range(1, layers):
            total = total + rhs[layer]
        q_mixed = mm(total, get.sine_cols)
        out.q_mixed[...] = q_mixed
        done(out.q_mixed)
        cond, store, leak = get.conductivity, get.storage, get.leakance
        partial, edge_rows = out.partial, [[], []]
        for layer in range(layers):
            own = cond[layer]
            diagonal = store[layer] + 0.5 * (4.0 * own + stencil(own, 0.0, 0.0, 0.0, 0.0))
            if layer < layers - 1:
                diagonal = diagonal + leak[layer]
            if layer > 0:
                diagonal = diagonal + leak[layer - 1]
            if layer == 0:
                diagonal = diagonal + get.et_rate[...]
            partial[layer] = diagonal
            for end, row in enumerate((0, rows - 1)):
                edge_rows[end] += [own[row : row + 1], diagonal[row : row + 1], rhs[layer, row : row + 1]]
        first, last = [
            jnp.concatenate([rows_of[place] for kind in range(3) for place in range(kind, 3 * layers, 3)], axis=0)
            for rows_of in edge_rows
        ]
        out.near[...], out.far[...] = choose(first, last)
        done(out.partial, out.near, out.far)
        first, last, left, right = rings(q_mixed, get)
        line, chunk = out.line, out.chunk
        line[:, :cols] = first
        line[:, cols : 2 * cols] = last
        line[:, at_zones:at_sides] = zone_line
        west, east = side_lanes([rhs[layer] for layer in range(layers)], (left, right))
        line[:, at_sides : at_sides + 128] = west
        line[:, at_sides + 128 : at_sides + 256] = east
        west, east = side_lanes(
            [cond[layer] for layer in range(layers)], (partial[0, :, 0:1], partial[0, :, cols - 1 : cols])
        )
        line[:, at_sides + 256 : at_sides + 384] = west
        line[:, at_sides + 384 : at_sides + 512] = east
        west, east = side_lanes([partial[layer] for layer in range(1, layers)])
        line[:, at_sides + 512 :] = jnp.where(iota((1, 128), 1) < 64, west, pltpu.roll(east, 64, 1))
        chunk[...] = jnp.broadcast_to(line[...][None], chunk.shape)
        done(out.chunk, out.line)

    started = call(
        start_body,
        dict(
            zone_of_block=zone_of_block,
            zone_recharge=zone_recharge[None],
            place=t.place,
            down=t.down,
            source=source,
            sine_cols=t.sine_cols,
            conductivity=conductivity,
            storage=storage,
            leakance=leakance,
            et_rate=et_rate,
            sine_rows=t.sine_rows,
            weight=t.weight,
            ends=t.ends,
        ),
        dict(
            rhs=area,
            q_mixed=(rows, cols),
            partial=area,
            near=(3 * layers, cols),
            far=(3 * layers, cols),
            line=(1, widths[0]),
            chunk=(devices, 1, widths[0]),
        ),
    )
    rhs = started.rhs
    received = first_received = exchange(started.chunk)
    near, far = first_near, first_far = neighbours(started.near, started.far)

    def couple_body(get, out, done):
        ids, weights = get.pair_zones, get.pair_weight
        place = iota((zones, ids.shape[1]), 0)
        table = (place == ids[0:1]).astype(F32) - (place == ids[1:2]).astype(F32)
        matrix = mm_f32(table * weights[...], table, DIMS_T)
        own = iota((zones, zones), 0) == iota((zones, zones), 1)
        matrix = matrix + jnp.where(own, get.zone_weight[...], 0.0)
        out.couple[...] = (COUPLE * zones / (slabs * rows * groups * cols)) * matrix
        line = get.line[:, at_zones:at_sides].astype(jnp.int32)
        out.hot[...] = (iota((zones, blocks), 0) == line).astype(F32).astype(BF16)
        done(out.couple, out.hot)

    coupling = call(
        couple_body,
        dict(pair_zones=pair_zones.T, pair_weight=pair_weight[None], zone_weight=zone_weight[None])
        | dict(line=started.line),
        dict(couple=(zones, zones), hot=((zones, blocks), BF16)),
    )
    couple, hot = coupling.couple, coupling.hot

    def step_body(number, get, out, done):
        coupled, final = number > 0, number == 2
        slab, group = lax.axis_index("slab"), lax.axis_index("grp")
        own = slab * groups + group
        has_north = (slab > 0).astype(F32)
        has_south = (slab < slabs - 1).astype(F32)
        has_west = (group > 0).astype(F32)
        has_east = (group < groups - 1).astype(F32)
        recv = get.received

        def of(shift, start):
            return recv[pl.ds(jnp.clip(own + shift, 0, devices - 1), 1), 0, start : start + 128]

        first_rows, last_rows = recv[:, 0, :cols], recv[:, 0, cols : 2 * cols]
        sides_at = at_sides if not coupled else at_zones + zones
        lane = iota((devices, 128), 1)
        edges = jnp.where(
            lane < rows,
            pltpu.roll(recv[:, 0, sides_at : sides_at + 128], rows, 1),
            pltpu.roll(recv[:, 0, sides_at + 128 : sides_at + 256], 2 * rows, 1),
        )
        edges = jnp.where(lane < 2 * rows, edges, 0.0)
        q_in = get.q_mixed[...]
        w_ref = get.w
        surface = w_ref[0]
        if coupled:
            totals = jnp.sum(recv[:, 0, at_zones : at_zones + zones], axis=0, keepdims=True)
            reply = mm_f32(jnp.broadcast_to(totals, (8, zones)), get.couple[...])[0:1]
            every = lookup(reply, get.zone_map[:, 0, :].astype(jnp.int32))
            edges = edges + mm(every, get.coarse)
            share = 128 // block_cols
            inner = iota((devices, 128), 1) // block_cols
            slabs_of = [
                jnp.where(inner == i % share, every[:, 128 * (i // share) : 128 * (i // share + 1)], 0.0)
                for i in range(block_rows)
            ]
            modes_of = mm(jnp.concatenate(slabs_of, axis=0), get.up_modes)
            device = iota(first_rows.shape, 0)
            modes = []
            for i in range(block_rows):
                part = modes_of[devices * i : devices * (i + 1)]
                first_rows = first_rows + get.coarse_rows[i : i + 1] * part
                last_rows = last_rows + get.coarse_rows[block_rows + i : block_rows + i + 1] * part
                modes.append(jnp.sum(jnp.where(device == own, part, 0.0), axis=0, keepdims=True))
            modes = jnp.concatenate(modes, axis=0)
            device = iota(every.shape, 0)
            line_of = lambda shift: jnp.sum(
                jnp.where(device == own + shift, every, 0.0), axis=0, keepdims=True
            )
            mine = line_of(0)
            wanted = [(mine, i) for i in range(block_rows)]
            wanted += [(line_of(-groups), block_rows - 1), (line_of(groups), 0)]
            field = field_rows(wanted, get.down[...], block_cols)
            q_in = q_in + spread_rows8(modes, rows)
            surface = surface + spread_rows8(field, rows)
            column = iota((rows, blocks), 1)
            base = block_cols * (iota((rows, blocks), 0) // 8)
            west_value = jnp.sum(
                jnp.where(column == base + block_cols - 1, line_of(-1), 0.0), axis=1, keepdims=True
            )
            east_value = jnp.sum(jnp.where(column == base, line_of(1), 0.0), axis=1, keepdims=True)
        if final:
            out.w[0] = surface
            for layer in range(1, layers):
                out.w[layer] = w_ref[layer]
            done(out.w)
        elif coupled:
            out.w[0] = surface
            for layer in range(1, layers):
                out.w[layer] = w_ref[layer]
            done(out.w)
        s, s_north, s_south, s_west, s_east = smooth(
            first_rows, last_rows, edges, q_in, slab, group, groups, get
        )
        cond, leak = get.conductivity, get.leakance
        north_ref, south_ref = choose(get.near[...], get.far[...])
        row, col = iota((rows, cols), 0), iota((rows, cols), 1)
        if coupled:
            cond_north, cond_south = choose(get.first_near[...], get.first_far[...])
            sides = get.sides
            lanes = [of(-1, sides_at + 128), of(1, sides_at)]
            diagonal_ref, inverse_ref = get.diagonal, get.inverse
            beside = get.beside
        else:
            cond_north, cond_south = north_ref, south_ref
            lanes = [of(-1, sides_at + 128), of(1, sides_at)]
            lanes += [of(-1, sides_at + 384) * has_west, of(1, sides_at + 256) * has_east]
            lanes += [of(-1, sides_at + 512), of(1, sides_at + 512)]
            diagonal_ref, inverse_ref, sides, beside = out.diagonal, out.inverse, out.sides, out.beside
        turned = jnp.concatenate(lanes + [jnp.zeros((128 - len(lanes), 128), F32)], axis=0).T
        if not coupled:
            corner = [
                of(-groups - 1, sides_at + 384) * (has_north * has_west),
                of(-groups + 1, sides_at + 256) * (has_north * has_east),
                of(groups - 1, sides_at + 384) * (has_south * has_west),
                of(groups + 1, sides_at + 256) * (has_south * has_east),
            ]
            ghosts = []
            partial = get.partial
            line_col, line_row = iota((1, cols), 1), iota((rows, 1), 0)
            for layer in range(layers):
                c_north, c_south = north_ref[layer : layer + 1], south_ref[layer : layer + 1]
                c_west = turned[rows * layer : rows * (layer + 1), 2:3]
                c_east = turned[rows * layer : rows * (layer + 1), 3:4]
                both = jnp.where(lane[:rows] == 0, c_west, jnp.where(lane[:rows] == 1, c_east, 0.0))
                sides[layer] = both
                diagonal = partial[layer] + 0.5 * (
                    jnp.where(row == 0, c_north, 0.0)
                    + jnp.where(row == rows - 1, c_south, 0.0)
                    + jnp.where(col == 0, c_west, 0.0)
                    + jnp.where(col == cols - 1, c_east, 0.0)
                )
                diagonal_ref[layer] = diagonal
                inverse_ref[layer] = 1.0 / diagonal
                start, end = rows * layer, rows * layer + rows - 1
                nw, ne = corner[0][:, end : end + 1], corner[1][:, end : end + 1]
                sw, se = corner[2][:, start : start + 1], corner[3][:, start : start + 1]
                own_cond = cond[layer]
                d_north = north_ref[layers + layer : layers + layer + 1] + 0.5 * (
                    own_cond[0:1] + jnp.where(line_col == 0, nw, jnp.where(line_col == cols - 1, ne, 0.0))
                )
                d_south = south_ref[layers + layer : layers + layer + 1] + 0.5 * (
                    own_cond[rows - 1 : rows]
                    + jnp.where(line_col == 0, sw, jnp.where(line_col == cols - 1, se, 0.0))
                )
                if layer == 0:
                    west, east = turned[3 * rows : 4 * rows, 2:3], turned[3 * rows : 4 * rows, 3:4]
                else:
                    west = turned[64 + rows * (layer - 1) : 64 + rows * layer, 4:5]
                    east = turned[rows * (layer - 1) : rows * layer, 5:6]
                d_west = west + 0.5 * (
                    own_cond[:, 0:1] + jnp.where(line_row == 0, nw, jnp.where(line_row == rows - 1, sw, 0.0))
                )
                d_east = east + 0.5 * (
                    own_cond[:, cols - 1 : cols]
                    + jnp.where(line_row == 0, ne, jnp.where(line_row == rows - 1, se, 0.0))
                )
                ghosts.append((1.0 / d_north, 1.0 / d_south, 1.0 / d_west, 1.0 / d_east))
            sides[layers] = jnp.where(lane[:rows] == 0, ghosts[0][2], jnp.where(lane[:rows] == 1, ghosts[0][3], 0.0))
            beside[0:1] = ghosts[0][0]
            beside[1:2] = ghosts[0][1]
            done(out.diagonal, out.inverse, out.sides, out.beside)
        v_out, image_out = out.v, out.image
        fields, outside = [], []
        for layer in range(layers):
            value = (surface if layer == 0 else w_ref[layer]) * inverse_ref[layer] + s
            v_out[layer] = value
            fields.append(value)
            west = turned[rows * layer : rows * (layer + 1), 0:1]
            east = turned[rows * layer : rows * (layer + 1), 1:2]
            if coupled:
                north, south = north_ref[layer : layer + 1], south_ref[layer : layer + 1]
                if layer == 0:
                    north = north + beside[0:1] * field[block_rows : block_rows + 1]
                    south = south + beside[1:2] * field[block_rows + 1 : block_rows + 2]
                    west = west + sides[layers, :, 0:1] * west_value
                    east = east + sides[layers, :, 1:2] * east_value
            else:
                near = ghosts[layer]
                place = 2 * layers + layer
                north, south = north_ref[place : place + 1] * near[0], south_ref[place : place + 1] * near[1]
                west, east = west * near[2], east * near[3]
            outside.append(
                (
                    (north + s_north) * has_north,
                    (south + s_south) * has_south,
                    (west + s_west) * has_west,
                    (east + s_east) * has_east,
                )
            )
        done(out.v)
        images = []
        for layer in range(layers):
            value, own_cond = fields[layer], cond[layer]
            north, south, west, east = outside[layer]
            plain = stencil(value, north, south, west, east)
            carried = stencil(
                value * own_cond,
                north * cond_north[layer : layer + 1],
                south * cond_south[layer : layer + 1],
                west * sides[layer, :, 0:1],
                east * sides[layer, :, 1:2],
            )
            image = diagonal_ref[layer] * value - 0.5 * (own_cond * plain + carried)
            if layer < layers - 1:
                image = image - leak[layer] * fields[layer + 1]
            if layer > 0:
                image = image - leak[layer - 1] * fields[layer - 1]
            image_out[layer] = image
            images.append(image)
        done(out.image)
        line, chunk = out.line, out.chunk
        totals = zone_totals(fields[0], get.hot[...], get.down[...])
        if final:
            rhs_ref, v0_ref, v1_ref, w0_ref = get.rhs, get.v0, get.v1, get.w0

            def dot(left, right):
                total = left[0] * right[0]
                for layer in range(1, layers):
                    total = total + left[layer] * right[layer]
                return jnp.sum(jnp.sum(total, axis=0, keepdims=True), axis=1, keepdims=True)

            w1 = [surface] + [w_ref[layer] for layer in range(1, layers)]
            products = [
                dot(v0_ref, w0_ref), dot(v0_ref, w1), dot(v1_ref, w1), dot(fields, w0_ref), dot(fields, w1),
                dot(fields, images), dot(v0_ref, rhs_ref), dot(v1_ref, rhs_ref), dot(fields, rhs_ref),
            ]
            packed = jnp.zeros((1, 128), F32)
            for place, value in enumerate(products):
                packed = jnp.where(iota((1, 128), 1) == place, value, packed)
            line[:, :zones] = totals
            line[:, zones:] = packed
        else:
            depth = images[0]
            for layer in range(1, layers):
                depth = depth + images[layer]
            q_next = mm(depth, get.sine_cols)
            out.q_mixed[...] = q_next
            done(out.q_mixed)
            scaled = [images[layer] * inverse_ref[layer] for layer in range(layers)]
            out.near[...], out.far[...] = choose(
                jnp.concatenate([part[0:1] for part in scaled], axis=0),
                jnp.concatenate([part[rows - 1 : rows] for part in scaled], axis=0),
            )
            done(out.near, out.far)
            first, last, left, right = rings(q_next, get)
            west, east = side_lanes(scaled, (left, right))
            line[:, :cols] = first
            line[:, cols : 2 * cols] = last
            line[:, at_zones : at_zones + zones] = totals
            line[:, at_zones + zones : at_zones + zones + 128] = west
            line[:, at_zones + zones + 128 :] = east
        chunk[...] = jnp.broadcast_to(line[...][None], chunk.shape)
        done(out.chunk, out.line)

    tail_width = zones + 128
    shared = {}

    def step(number, received, q_mixed, w, near, far, more=()):
        ins = dict(received=received)
        if number > 0:
            ins |= dict(couple=couple, zone_map=zone_map, coarse=t.coarse, up_modes=t.up_modes, coarse_rows=t.coarse_rows)
        ins |= dict(row_chain=t.row_chain, answer=t.answer, q_mixed=q_mixed, w=w, down=t.down)
        ins |= dict(waves=t.waves, own_columns=t.own_columns, around=t.around, wave_weight=t.wave_weight)
        ins |= dict(ends=t.ends, sine_rows=t.sine_rows, weight=t.weight, sine_cols=t.sine_cols)
        ins |= dict(near=near, far=far, conductivity=conductivity, leakance=leakance)
        ins |= dict(hot=hot)
        outs = dict(v=area, image=area)
        if number > 0:
            ins |= dict(first_near=first_near, first_far=first_far) | shared
            outs |= dict(w=area)
        else:
            ins |= dict(partial=started.partial, couple=(couple, None))
            outs |= dict(diagonal=area, inverse=area, sides=(layers + 1, rows, 128), beside=(2, cols))
        ins |= dict(more)
        if number == 2:
            outs |= dict(line=(1, tail_width), chunk=(devices, 1, tail_width))
        else:
            outs |= dict(
                q_mixed=(rows, cols), near=(layers, cols), far=(layers, cols), line=(1, widths[1]), chunk=(devices, 1, widths[1])
            )
        return call(lambda get, out, done: step_body(number, get, out, done), ins, outs)

    one = step(0, received, started.q_mixed, rhs, near, far)
    shared.update(diagonal=one.diagonal, inverse=one.inverse, sides=one.sides, beside=one.beside)
    zone_map = (first_received, (slice(None), slice(None), slice(at_zones, at_sides)))
    received = exchange(one.chunk)
    near, far = neighbours(one.near, one.far)
    two = step(1, received, one.q_mixed, one.image, near, far)
    received = exchange(two.chunk)
    near, far = neighbours(two.near, two.far)
    more = dict(rhs=rhs, v0=one.v, v1=two.v, w0=two.w)
    three = step(2, received, two.q_mixed, two.image, near, far, more)
    received = exchange(three.chunk)

    def finish_body(get, out, done):
        sums = jnp.sum(get.received[:, 0, :], axis=0, keepdims=True)
        totals = sums[:, :zones]
        reply = mm_f32(jnp.broadcast_to(totals, (8, zones)), get.couple[...])
        zone_line = get.zone_line[:, at_zones:at_sides]
        index = jnp.broadcast_to(zone_line, (8, blocks)).astype(jnp.int32)
        found = lookup(reply[0:1], index)[0:1]
        field = field_rows([(found, i) for i in range(block_rows)], get.down[...], block_cols)
        coupled = spread_rows8(field, rows)
        a00, a01, a11, a02, a12, a22, h0, h1, h2 = [sums[:, zones + i : zones + i + 1] for i in range(9)]
        a22 = a22 + jnp.sum(totals * reply[0:1], axis=1, keepdims=True)
        l10, l20 = a01 / a00, a02 / a00
        d1 = a11 - l10 * a01
        l21 = (a12 - l10 * a02) / d1
        d2 = a22 - l20 * a02 - l21 * (a12 - l10 * a02)
        y1 = h1 - l10 * h0
        y2 = h2 - l20 * h0 - l21 * y1
        c2 = y2 / d2
        c1 = y1 / d1 - l21 * c2
        c0 = h0 / a00 - l10 * c1 - l20 * c2
        v0, v1, v2, w0, w1, w2 = get.v0, get.v1, get.v2, get.w0, get.w1, get.w2
        rhs_ref = get.rhs
        for layer in range(layers):
            last = w2[layer] + coupled if layer == 0 else w2[layer]
            out.solution[layer] = c0 * v0[layer] + c1 * v1[layer] + c2 * v2[layer]
            out.residual[layer] = rhs_ref[layer] - c0 * w0[layer] - c1 * w1[layer] - c2 * last
        done(out.solution, out.residual)

    ended = call(
        finish_body,
        dict(received=received, couple=couple, zone_line=started.line, down=t.down)
        | dict(rhs=rhs, v0=one.v, v1=two.v, v2=three.v, w0=two.w, w1=three.w, w2=three.image),
        dict(solution=area, residual=area),
    )
    return ended.solution, ended.residual


def solution(mesh):
    placed = (
        P(None, "slab", "grp"),
        P(None, "slab", "grp"),
        P(None, "slab", "grp"),
        P(None, "slab", "grp"),
        P("slab", "grp"),
        P("slab", "grp"),
        P(),
        P(),
        P(),
        P(),
    )
    return jax.shard_map(
        shards,
        mesh=mesh,
        in_specs=placed,
        out_specs=(P(None, "slab", "grp"), P(None, "slab", "grp")),
        check_vma=False,
    )
```

```python
import math
from types import SimpleNamespace

import jax
import jax.numpy as jnp
import numpy as np
from jax import lax
from jax.experimental import pallas as pl
from jax.experimental.pallas import tpu as pltpu
from jax.sharding import PartitionSpec as P

COUPLE = 4.0
PRECOND_T = 2.0
PRECOND_SHIFT = 3.0
HIGHEST = lax.Precision.HIGHEST
BOTH = ("slab", "grp")
VMEM_LIMIT = 24 * 1024 * 1024
F32, BF16 = jnp.float32, jnp.bfloat16


def sine_basis(count):
    index = np.arange(1, count + 1)
    basis = math.sqrt(2.0 / (count + 1)) * np.sin(np.pi * np.outer(index, index) / (count + 1))
    return basis, 4.0 * np.sin(np.pi * index / (2.0 * (count + 1))) ** 2


def fourier_basis(count):
    cells = np.arange(count)[:, None]
    waves = np.concatenate([np.arange(count // 2 + 1), np.arange(1, count // 2)])[None, :]
    turned = 2.0 * np.pi * ((cells * waves) % count) / count
    is_sine = np.arange(count)[None, :] > count // 2
    basis = np.where(is_sine, np.sin(turned), np.cos(turned)) * math.sqrt(2.0 / count)
    basis[:, 0] /= math.sqrt(2.0)
    basis[:, count // 2] /= math.sqrt(2.0)
    return basis, 4.0 * np.sin(np.pi * waves[0] / count) ** 2


def chain_tables(cross, total, block):
    half = (PRECOND_SHIFT / PRECOND_T + cross) / 2.0 + 1.0
    decay = 1.0 / (half + np.sqrt(half * half - 1.0))
    scale = 1.0 / ((1.0 - decay**total) * PRECOND_T * (1.0 / decay - decay))

    def green(distance):
        distance = distance % total
        return PRECOND_T * scale * (decay**distance + decay ** (total - distance))

    count = total // block
    tables = np.zeros((4, count, len(cross)))
    for back in range(count):
        tables[0, back] = green(block * back)
        tables[1, back] = green(block * (back - 1) - 1) + (1.0 if back == 1 % count else 0.0)
        tables[2, back] = green(block * (back + 1) + 1) + (1.0 if back == count - 1 else 0.0)
        tables[3, back] = green(block * back)
    return tables


def grid_tables(slabs, groups, rows, cols):
    rows_total, cols_total = slabs * rows, groups * cols
    sine_rows, cross_rows = sine_basis(rows)
    sine_cols, cross_cols = sine_basis(cols)
    waves, cross_waves = fourier_basis(rows_total)
    weight = 1.0 / (PRECOND_SHIFT + PRECOND_T * (cross_rows[:, None] + cross_cols[None, :]))
    wave_weight = 1.0 / (PRECOND_SHIFT + PRECOND_T * (cross_waves[:, None] + cross_cols[None, :]))
    first, last = sine_cols[0], sine_cols[-1]
    answer = np.zeros((cols, 128))
    for end, row in enumerate((0, rows - 1)):
        inside = PRECOND_T * np.einsum("ri,ij,i->jr", sine_rows, weight, sine_rows[:, row])
        answer[:, 64 * end : 64 * end + rows] = first[:, None] * inside
        answer[:, 64 * end + rows : 64 * end + 2 * rows] = last[:, None] * inside
    spread_rows = np.repeat(np.eye(rows // 8), 8, axis=0)
    spread_cols = np.repeat(np.eye(cols // 8), 8, axis=0)
    mode_rows, mode_cols = sine_rows @ spread_rows, sine_cols @ spread_cols
    mixed = np.einsum("ri,ij,ib->rbj", sine_rows, weight, mode_rows)
    coarse = np.zeros((rows // 8, cols // 8, 128))
    coarse[:, :, :rows] = np.einsum("rbj,j,jc->bcr", mixed, first, mode_cols)
    coarse[:, :, rows : 2 * rows] = np.einsum("rbj,j,jc->bcr", mixed, last, mode_cols)
    column_chain = chain_tables(cross_waves, cols_total, cols)
    tile = max(8, groups)
    own_columns = np.zeros((groups, 4, tile, rows_total))
    for group in range(groups):
        for other in range(groups):
            own_columns[group, :, other] = column_chain[:, (group - other) % groups]
    around = np.zeros((slabs, 8, rows_total))
    for slab in range(slabs):
        around[slab, 0] = waves[(rows * slab - 1) % rows_total]
        around[slab, 1] = waves[(rows * slab + rows) % rows_total]
    ends = np.zeros((8, cols))
    ends[0], ends[1] = first, last
    blocks = (rows // 8) * (cols // 8)
    down = np.tile(spread_cols, (1, rows // 8))
    exact = dict(
        weight=weight,
        row_chain=chain_tables(cross_cols, rows_total, rows).reshape(4 * slabs, cols),
        own_columns=own_columns.reshape(groups, 4 * tile, rows_total),
        around=around,
        ends=ends,
        coarse_rows=np.concatenate([mixed[0], mixed[-1]]),
    )
    split = dict(
        sine_rows=sine_rows,
        sine_cols=sine_cols,
        answer=answer,
        coarse=coarse.reshape(blocks, 128),
        waves=waves,
        wave_weight=wave_weight,
        up_modes=np.tile(mode_cols.T, (128 // (cols // 8), 1)),
    )
    tables = {name: np.asarray(table, np.float32) for name, table in exact.items()}
    for name, table in split.items():
        high = table.astype(jnp.bfloat16)
        tables[name] = np.stack([high, (table - high.astype(np.float64)).astype(jnp.bfloat16)])
    tables["down"] = down.astype(jnp.bfloat16)
    tables["place"] = np.tile(np.eye(cols // 8), (1, rows // 8)).astype(jnp.bfloat16)
    return tables


def terms(value, count):
    parts = []
    for _ in range(count):
        part = value.astype(BF16).astype(F32)
        parts.append(part)
        value = value - part
    return parts


DIMS = (((1,), (0,)), ((), ()))
DIMS_T = (((1,), (1,)), ((), ()))


def product(left, right, dims):
    return lax.dot_general(left, right, dims, preferred_element_type=F32)


def mm(value, table, dims=DIMS):
    rows = value.shape[0]
    high, low = terms(value, 2)
    both = product(jnp.concatenate([high, low], axis=0).astype(BF16), table[0], dims)
    return both[:rows] + both[rows:] + product(high.astype(BF16), table[1], dims)


def mm_left(table, value, dims=DIMS):
    rows = table[0].shape[0]
    high, low = terms(value, 2)
    both = product(jnp.concatenate([table[0], table[1]], axis=0), high.astype(BF16), dims)
    return both[:rows] + both[rows:] + product(table[0], low.astype(BF16), dims)


def mm_exact(value, table, dims=DIMS):
    rows = value.shape[0]
    every = product(jnp.concatenate(terms(value, 3), axis=0).astype(BF16), table, dims)
    return every[:rows] + every[rows : 2 * rows] + every[2 * rows :]


def mm_f32(left, right, dims=DIMS):
    return lax.dot_general(left, right, dims, precision=HIGHEST, preferred_element_type=F32)


def iota(shape, dim):
    return lax.broadcasted_iota(jnp.int32, shape, dim)


def lookup(values, index):
    rows, lanes = index.shape
    zones = values.shape[1]
    within, which = index & 127, index >> 7
    pieces = []
    for start in range(0, lanes, 128):
        part = jnp.zeros((rows, 128), F32)
        for half in range(zones // 128):
            table = jnp.broadcast_to(values[:, 128 * half : 128 * (half + 1)], (rows, 128))
            found = jnp.take_along_axis(table, within[:, start : start + 128], axis=1)
            part = jnp.where(which[:, start : start + 128] == half, found, part)
        pieces.append(part)
    return jnp.concatenate(pieces, axis=1) if len(pieces) > 1 else pieces[0]


def rings(q_mixed, t):
    sine_rows = t.sine_rows
    inside = mm_left(sine_rows, mm_left(sine_rows, q_mixed) * t.weight[...])
    rows = inside.shape[0]
    ends = t.ends
    left = jnp.sum(inside * ends[0:1], axis=1, keepdims=True)
    right = jnp.sum(inside * ends[1:2], axis=1, keepdims=True)
    return inside[0:1], inside[rows - 1 : rows], left, right


def side_lanes(parts, last=None):
    rows, cols = parts[0].shape
    lane = iota((rows, 128), 1)
    tall = [jnp.where(lane == 127, p[:, cols - 128 :], p[:, :128]) for p in parts]
    if last is not None:
        tall.append(jnp.where(lane == 127, last[1], last[0]))
    while len(tall) < 4:
        tall.append(jnp.zeros((rows, 128), F32))
    turned = jnp.concatenate(tall, axis=0).T
    return turned[0:1], turned[127:128]


def stencil(values, before, after, left, right):
    rows, cols = values.shape
    row, col = iota(values.shape, 0), iota(values.shape, 1)
    up = jnp.where(row == 0, before, pltpu.roll(values, 1, 0))
    down = jnp.where(row == rows - 1, after, pltpu.roll(values, rows - 1, 0))
    west = jnp.where(col == 0, left, pltpu.roll(values, 1, 1))
    east = jnp.where(col == cols - 1, right, pltpu.roll(values, cols - 1, 1))
    return (up + down) + (west + east)


def to_line(spread, block_cols):
    own = iota(spread.shape, 1) // block_cols == iota(spread.shape, 0)
    return jnp.sum(jnp.where(own, spread, 0.0), axis=0, keepdims=True)


def zone_totals(surface, hot, down):
    rows, cols = surface.shape
    sums = [jnp.sum(surface[8 * i : 8 * i + 8], axis=0, keepdims=True) for i in range(rows // 8)]
    sums = jnp.concatenate(sums + [jnp.zeros((8 - rows // 8, cols), F32)], axis=0)
    line = to_line(mm_exact(sums, down), cols // 8)
    line = jnp.broadcast_to(line, (8, line.shape[1]))
    return mm_exact(line, hot, DIMS_T)[0:1]


def field_rows(lines, down, block_cols):
    row, place = iota((8, lines[0][0].shape[1]), 0), iota((8, lines[0][0].shape[1]), 1) // block_cols
    picked = jnp.zeros(row.shape, F32)
    for index, (line, wanted) in enumerate(lines):
        picked = jnp.where((row == index) & (place == wanted), line, picked)
    return mm_exact(picked, down, DIMS_T)


def spread_rows8(lines, rows):
    return jnp.concatenate(
        [jnp.broadcast_to(lines[i : i + 1], (8, lines.shape[1])) for i in range(rows // 8)], axis=0
    )


def smooth(first_rows, last_rows, edges, q_mixed, slab, group, groups, t):
    devices = first_rows.shape[0]
    slabs = devices // groups
    rows, cols = q_mixed.shape
    before = jnp.zeros_like(first_rows)
    after = jnp.zeros_like(first_rows)
    chain = t.row_chain
    for back in range(slabs):
        turned_first = pltpu.roll(first_rows, groups * back, 0) if back else first_rows
        turned_last = pltpu.roll(last_rows, groups * back, 0) if back else last_rows
        line = [chain[slabs * kind + back : slabs * kind + back + 1] for kind in range(4)]
        before = before + (line[0] * turned_first + line[1] * turned_last)
        after = after + (line[2] * turned_first + line[3] * turned_last)
    mine = iota(before.shape, 0) == slab * groups + group
    own_before = jnp.sum(jnp.where(mine, before, 0.0), axis=0, keepdims=True)
    own_after = jnp.sum(jnp.where(mine, after, 0.0), axis=0, keepdims=True)
    answer = t.answer
    moved = mm(jnp.concatenate([before, after], axis=0), answer)
    lane = iota(edges.shape, 1)
    edges = edges + jnp.where(lane < 64, moved[:devices] + pltpu.roll(moved[devices:], 64, 1), 0.0)
    tile, per = max(8, groups), 128 // rows
    lane = iota(edges.shape, 1) // rows
    lines = []
    for side in range(2):
        joined = jnp.zeros_like(edges)
        for i in range(per):
            moved = pltpu.roll(edges, rows * (i - side) % 128, 1) if i != side else edges
            moved = pltpu.roll(moved, devices - groups * i, 0) if i else moved
            joined = jnp.where(lane == i, moved, joined)
        step = per * groups
        lines.append(jnp.concatenate([joined[step * p : step * p + tile] for p in range(slabs // per)], axis=1))
    waves = t.waves
    waved = mm(jnp.concatenate(lines, axis=0), waves)
    count = waved.shape[1]
    firsts, lasts = waved[:tile], waved[tile:]
    chain = t.own_columns
    table = [chain[tile * kind : tile * (kind + 1)] for kind in range(4)]
    left = jnp.sum(table[0] * firsts + table[1] * lasts, axis=0, keepdims=True)
    right = jnp.sum(table[2] * firsts + table[3] * lasts, axis=0, keepdims=True)
    row = iota((8, count), 0)
    sides = jnp.where(row == 0, left, jnp.where(row == 1, right, 0.0))
    own_rows = pl.ds(pl.multiple_of(slab * rows, rows), rows)
    columns = mm_left([waves[0, own_rows, :], waves[1, own_rows, :]], sides, DIMS_T)
    left_col, right_col = columns[:, 0:1], columns[:, 1:2]
    around = t.around
    north, south = around[0:1], around[1:2]
    four = jnp.where(
        row == 0,
        north * left,
        jnp.where(row == 1, north * right, jnp.where(row == 2, south * left, jnp.where(row == 3, south * right, 0.0))),
    )
    four = mm(four, t.wave_weight)
    ends = t.ends
    first, last = ends[0:1], ends[1:2]
    north_row = own_before + PRECOND_T * (first * four[0:1] + last * four[1:2])
    south_row = own_after + PRECOND_T * (first * four[2:3] + last * four[3:4])
    place = iota((rows, cols), 0)
    loaded = q_mixed + PRECOND_T * (
        jnp.where(place == 0, north_row, 0.0)
        + jnp.where(place == rows - 1, south_row, 0.0)
        + left_col * first
        + right_col * last
    )
    sine_rows = t.sine_rows
    inside = mm_left(sine_rows, mm_left(sine_rows, loaded) * t.weight[...])
    pad = jnp.zeros((6, cols), F32)
    whole = mm(jnp.concatenate([inside, north_row, south_row, pad], axis=0), t.sine_cols)
    return whole[:rows], whole[rows : rows + 1], whole[rows + 1 : rows + 2], left_col, right_col


class Operands:
    def __init__(self, copies, buffers):
        self._copies, self._buffers = copies, buffers

    def __getattr__(self, name):
        if name in self._copies:
            self._copies.pop(name).wait()
        return self._buffers[name]


class Held:
    def __init__(self, array):
        self.array = array


def call(body, ins, outs, keep=()):
    names, results = list(ins), list(outs) + list(keep)
    arrays, parts, copied = [], [], []
    for place, value in enumerate(ins.values()):
        held = isinstance(value, Held)
        array, part = (value.array, None) if held else value if isinstance(value, tuple) else (value, ())
        arrays.append(pltpu.with_memory_space_constraint(array, pltpu.VMEM if held else pltpu.HBM))
        parts.append(part)
        if part is not None:
            copied.append(place)
    kinds, sent = [], []
    for place, value in enumerate(outs.values()):
        if isinstance(value, Held):
            kinds.append((value.array, F32))
        else:
            kinds.append(value if isinstance(value[-1], type(F32)) else (value, F32))
            sent.append(place)
    spaces = [
        [pl.BlockSpec(memory_space=pltpu.VMEM if isinstance(value, Held) else pltpu.HBM) for value in side.values()]
        for side in (ins, outs)
    ]
    spaces[1] += [pl.BlockSpec(memory_space=pltpu.VMEM)] * len(keep)

    def shape_of(array, part):
        if isinstance(part, str):
            return array.shape[1:]
        return tuple(len(range(*cut.indices(size))) for cut, size in zip(part, array.shape)) + array.shape[len(part) :]

    def kernel(*refs):
        given, refs = refs[: len(names)], refs[len(names) :]
        made, refs = refs[: len(results)], refs[len(results) :]
        in_sems, out_sems = refs[-2:]
        copies, buffers = {}, dict(zip(names, given))
        for slot, place in enumerate(copied):
            part = parts[place]
            origin = given[place].at[lax.axis_index(part) if isinstance(part, str) else part] if part else given[place]
            name = names[place]
            buffers[name] = made[results.index(name, len(outs))] if name in keep else refs[slot]
            copies[name] = pltpu.make_async_copy(origin, buffers[name], in_sems.at[slot])
            copies[name].start()
        built = list(made)
        for slot, place in enumerate(sent):
            built[place] = refs[len(copied) + slot]
        going = []

        def done(*which):
            for buffer in which:
                for slot, place in enumerate(sent):
                    if built[place] is buffer:
                        going.append(pltpu.make_async_copy(buffer, made[place], out_sems.at[slot]))
                        going[-1].start()

        get = Operands(copies, buffers)
        body(get, SimpleNamespace(**dict(zip(results, built))), done)
        for place in copied:
            getattr(get, names[place])
        assert len(going) == len(sent)
        for copy in going:
            copy.wait()

    shapes = [(shape_of(arrays[place], parts[place]), arrays[place].dtype) for place in copied]
    kept = [shapes[copied.index(names.index(name))] for name in keep]
    scratch = [
        pltpu.VMEM(*((8, 128), F32) if names[place] in keep else shape) for place, shape in zip(copied, shapes)
    ]
    scratch += [pltpu.VMEM(*kinds[place]) for place in sent]
    scratch += [pltpu.SemaphoreType.DMA((max(1, len(some)),)) for some in (copied, sent)]
    made = pl.pallas_call(
        kernel,
        out_shape=[
            pltpu.VMEM(*kind) if isinstance(value, Held) else pltpu.HBM(*kind)
            for kind, value in zip(kinds, outs.values())
        ]
        + [pltpu.VMEM(*shape) for shape in kept],
        in_specs=spaces[0],
        out_specs=spaces[1],
        scratch_shapes=scratch,
        compiler_params=pltpu.CompilerParams(vmem_limit_bytes=VMEM_LIMIT),
    )(*arrays)
    return SimpleNamespace(**dict(zip(results, made)))


def shards(
    source,
    conductivity,
    leakance,
    storage,
    et_rate,
    zone_of_block,
    zone_recharge,
    zone_weight,
    pair_zones,
    pair_weight,
):
    slabs, groups = lax.axis_size("slab"), lax.axis_size("grp")
    layers, rows, cols = source.shape
    devices = slabs * groups
    zones = zone_weight.shape[0]
    tables = {name: jnp.asarray(table) for name, table in grid_tables(slabs, groups, rows, cols).items()}
    t = SimpleNamespace(**tables)
    t.own_columns, t.around = (t.own_columns, "grp"), (t.around, "slab")
    block_rows, block_cols = rows // 8, cols // 8
    blocks = block_rows * block_cols
    at_zones = 2 * cols
    at_sides = at_zones + blocks
    widths = (at_sides + 5 * 128, at_zones + zones + 2 * 128)
    area = (layers, rows, cols)

    def neighbours(near, far):
        across = [(i, i + 1) for i in range(1, slabs - 1, 2)]
        return (
            lax.ppermute(near, "slab", [(i, i ^ 1) for i in range(slabs)]),
            lax.ppermute(far, "slab", across + [(j, i) for i, j in across]),
        )

    def choose(near, far):
        odd = lax.axis_index("slab") % 2 == 1
        return jnp.where(odd, near, far), jnp.where(odd, far, near)

    def exchange(chunk):
        return lax.all_to_all(chunk, BOTH, split_axis=0, concat_axis=0, tiled=True)

    def start_body(get, out, done):
        ids = get.zone_of_block[...].astype(F32)
        ids = jnp.concatenate([ids, jnp.zeros((8 - block_rows, block_cols), F32)], axis=0)
        zone_line = to_line(mm_exact(ids, get.place[...]), block_cols)
        index = jnp.broadcast_to(zone_line, (8, blocks)).astype(jnp.int32)
        found = lookup(get.zone_recharge[...], index)[0:1]
        field = field_rows([(found, i) for i in range(block_rows)], get.down[...], block_cols)
        source_ref, rhs = get.source, out.rhs
        rhs[0] = source_ref[0] + spread_rows8(field, rows)
        for layer in range(1, layers):
            rhs[layer] = source_ref[layer]
        done(out.rhs)
        total = rhs[0]
        for layer in range(1, layers):
            total = total + rhs[layer]
        q_mixed = mm(total, get.sine_cols)
        out.q_mixed[...] = q_mixed
        done(out.q_mixed)
        cond, store, leak = get.conductivity, get.storage, get.leakance
        partial, edge_rows = out.partial, [[], []]
        for layer in range(layers):
            own = cond[layer]
            diagonal = store[layer] + 0.5 * (4.0 * own + stencil(own, 0.0, 0.0, 0.0, 0.0))
            if layer < layers - 1:
                diagonal = diagonal + leak[layer]
            if layer > 0:
                diagonal = diagonal + leak[layer - 1]
            if layer == 0:
                diagonal = diagonal + get.et_rate[...]
            partial[layer] = diagonal
            for end, row in enumerate((0, rows - 1)):
                edge_rows[end] += [own[row : row + 1], diagonal[row : row + 1], rhs[layer, row : row + 1]]
        first, last = [
            jnp.concatenate([rows_of[place] for kind in range(3) for place in range(kind, 3 * layers, 3)], axis=0)
            for rows_of in edge_rows
        ]
        out.near[...], out.far[...] = choose(first, last)
        done(out.partial, out.near, out.far)
        first, last, left, right = rings(q_mixed, get)
        sides = side_lanes([rhs[layer] for layer in range(layers)], (left, right))
        sides += side_lanes(
            [cond[layer] for layer in range(layers)], (partial[0, :, 0:1], partial[0, :, cols - 1 : cols])
        )
        west, east = side_lanes([partial[layer] for layer in range(1, layers)])
        both = jnp.where(iota((1, 128), 1) < 64, west, pltpu.roll(east, 64, 1))
        line = jnp.concatenate([first, last, zone_line, *sides, both], axis=1)
        out.chunk[...] = jnp.broadcast_to(line[None], out.chunk.shape)
        out.zone_line[...] = zone_line
        done(out.chunk)

    started = call(
        start_body,
        dict(
            zone_of_block=zone_of_block,
            zone_recharge=zone_recharge[None],
            place=t.place,
            down=t.down,
            source=source,
            sine_cols=t.sine_cols,
            conductivity=conductivity,
            storage=storage,
            leakance=leakance,
            et_rate=et_rate,
            sine_rows=t.sine_rows,
            weight=t.weight,
            ends=t.ends,
        ),
        dict(
            rhs=Held(area),
            q_mixed=Held((rows, cols)),
            partial=area,
            near=(3 * layers, cols),
            far=(3 * layers, cols),
            zone_line=Held((1, blocks)),
            chunk=(devices, 1, widths[0]),
        ),
    )
    rhs = started.rhs
    received = exchange(started.chunk)
    near, far = neighbours(started.near, started.far)

    def couple_body(get, out, done):
        ids, weights = get.pair_zones, get.pair_weight
        place = iota((zones, ids.shape[1]), 0)
        table = (place == ids[0:1]).astype(F32) - (place == ids[1:2]).astype(F32)
        matrix = mm_f32(table * weights[...], table, DIMS_T)
        own = iota((zones, zones), 0) == iota((zones, zones), 1)
        matrix = matrix + jnp.where(own, get.zone_weight[...], 0.0)
        out.couple[...] = (COUPLE * zones / (slabs * rows * groups * cols)) * matrix
        line = get.zone_line[...].astype(jnp.int32)
        out.hot[...] = (iota((zones, blocks), 0) == line).astype(F32).astype(BF16)
        done(out.couple, out.hot)

    coupling = call(
        couple_body,
        dict(pair_zones=pair_zones.T, pair_weight=pair_weight[None], zone_weight=zone_weight[None])
        | dict(zone_line=Held(started.zone_line)),
        dict(couple=(zones, zones), hot=((zones, blocks), BF16)),
    )
    couple, hot = coupling.couple, coupling.hot

    def step_body(number, get, out, done):
        coupled, final = number > 0, number == 2
        slab, group = lax.axis_index("slab"), lax.axis_index("grp")
        own = slab * groups + group
        has_north = (slab > 0).astype(F32)
        has_south = (slab < slabs - 1).astype(F32)
        has_west = (group > 0).astype(F32)
        has_east = (group < groups - 1).astype(F32)
        recv = get.received

        def of(shift, start):
            return recv[pl.ds(jnp.clip(own + shift, 0, devices - 1), 1), 0, start : start + 128]

        first_rows, last_rows = recv[:, 0, :cols], recv[:, 0, cols : 2 * cols]
        sides_at = at_sides if not coupled else at_zones + zones
        lane = iota((devices, 128), 1)
        edges = jnp.where(
            lane < rows,
            pltpu.roll(recv[:, 0, sides_at : sides_at + 128], rows, 1),
            pltpu.roll(recv[:, 0, sides_at + 128 : sides_at + 256], 2 * rows, 1),
        )
        edges = jnp.where(lane < 2 * rows, edges, 0.0)
        q_in = get.q_mixed[...]
        w_ref = get.w
        surface = w_ref[0]
        if coupled:
            totals = jnp.sum(recv[:, 0, at_zones : at_zones + zones], axis=0, keepdims=True)
            reply = mm_f32(jnp.broadcast_to(totals, (8, zones)), get.couple[...])[0:1]
            every = lookup(reply, get.zone_map[...].astype(jnp.int32))
            edges = edges + mm(every, get.coarse)
            share = 128 // block_cols
            inner = iota((devices, 128), 1) // block_cols
            slabs_of = [
                jnp.where(inner == i % share, every[:, 128 * (i // share) : 128 * (i // share + 1)], 0.0)
                for i in range(block_rows)
            ]
            modes_of = mm(jnp.concatenate(slabs_of, axis=0), get.up_modes)
            device = iota(first_rows.shape, 0)
            modes = []
            for i in range(block_rows):
                part = modes_of[devices * i : devices * (i + 1)]
                first_rows = first_rows + get.coarse_rows[i : i + 1] * part
                last_rows = last_rows + get.coarse_rows[block_rows + i : block_rows + i + 1] * part
                modes.append(jnp.sum(jnp.where(device == own, part, 0.0), axis=0, keepdims=True))
            modes = jnp.concatenate(modes, axis=0)
            device = iota(every.shape, 0)
            line_of = lambda shift: jnp.sum(
                jnp.where(device == own + shift, every, 0.0), axis=0, keepdims=True
            )
            mine = line_of(0)
            wanted = [(mine, i) for i in range(block_rows)]
            wanted += [(line_of(-groups), block_rows - 1), (line_of(groups), 0)]
            field = field_rows(wanted, get.down[...], block_cols)
            q_in = q_in + spread_rows8(modes, rows)
            surface = surface + spread_rows8(field, rows)
            column = iota((rows, blocks), 1)
            base = block_cols * (iota((rows, blocks), 0) // 8)
            west_value = jnp.sum(
                jnp.where(column == base + block_cols - 1, line_of(-1), 0.0), axis=1, keepdims=True
            )
            east_value = jnp.sum(jnp.where(column == base, line_of(1), 0.0), axis=1, keepdims=True)
        if final:
            out.w[0] = surface
            for layer in range(1, layers):
                out.w[layer] = w_ref[layer]
            done(out.w)
        elif coupled:
            out.w[0] = surface
            for layer in range(1, layers):
                out.w[layer] = w_ref[layer]
            done(out.w)
        s, s_north, s_south, s_west, s_east = smooth(
            first_rows, last_rows, edges, q_in, slab, group, groups, get
        )
        cond, leak = get.conductivity, get.leakance
        north_ref, south_ref = choose(get.near[...], get.far[...])
        row, col = iota((rows, cols), 0), iota((rows, cols), 1)
        if coupled:
            cond_north, cond_south = get.cond_north, get.cond_south
            sides = get.sides
            lanes = [of(-1, sides_at + 128), of(1, sides_at)]
            diagonal_ref, inverse_ref = get.diagonal, get.inverse
            beside = get.beside
        else:
            cond_north, cond_south = north_ref, south_ref
            lanes = [of(-1, sides_at + 128), of(1, sides_at)]
            lanes += [of(-1, sides_at + 384) * has_west, of(1, sides_at + 256) * has_east]
            lanes += [of(-1, sides_at + 512), of(1, sides_at + 512)]
            diagonal_ref, inverse_ref, sides, beside = out.diagonal, out.inverse, out.sides, out.beside
        turned = jnp.concatenate(lanes + [jnp.zeros((128 - len(lanes), 128), F32)], axis=0).T
        if not coupled:
            corner = [
                of(-groups - 1, sides_at + 384) * (has_north * has_west),
                of(-groups + 1, sides_at + 256) * (has_north * has_east),
                of(groups - 1, sides_at + 384) * (has_south * has_west),
                of(groups + 1, sides_at + 256) * (has_south * has_east),
            ]
            ghosts = []
            partial = get.partial
            line_col, line_row = iota((1, cols), 1), iota((rows, 1), 0)
            for layer in range(layers):
                c_north, c_south = north_ref[layer : layer + 1], south_ref[layer : layer + 1]
                c_west = turned[rows * layer : rows * (layer + 1), 2:3]
                c_east = turned[rows * layer : rows * (layer + 1), 3:4]
                both = jnp.where(lane[:rows] == 0, c_west, jnp.where(lane[:rows] == 1, c_east, 0.0))
                sides[layer] = both
                diagonal = partial[layer] + 0.5 * (
                    jnp.where(row == 0, c_north, 0.0)
                    + jnp.where(row == rows - 1, c_south, 0.0)
                    + jnp.where(col == 0, c_west, 0.0)
                    + jnp.where(col == cols - 1, c_east, 0.0)
                )
                diagonal_ref[layer] = diagonal
                inverse_ref[layer] = 1.0 / diagonal
                start, end = rows * layer, rows * layer + rows - 1
                nw, ne = corner[0][:, end : end + 1], corner[1][:, end : end + 1]
                sw, se = corner[2][:, start : start + 1], corner[3][:, start : start + 1]
                own_cond = cond[layer]
                d_north = north_ref[layers + layer : layers + layer + 1] + 0.5 * (
                    own_cond[0:1] + jnp.where(line_col == 0, nw, jnp.where(line_col == cols - 1, ne, 0.0))
                )
                d_south = south_ref[layers + layer : layers + layer + 1] + 0.5 * (
                    own_cond[rows - 1 : rows]
                    + jnp.where(line_col == 0, sw, jnp.where(line_col == cols - 1, se, 0.0))
                )
                if layer == 0:
                    west, east = turned[3 * rows : 4 * rows, 2:3], turned[3 * rows : 4 * rows, 3:4]
                else:
                    west = turned[64 + rows * (layer - 1) : 64 + rows * layer, 4:5]
                    east = turned[rows * (layer - 1) : rows * layer, 5:6]
                d_west = west + 0.5 * (
                    own_cond[:, 0:1] + jnp.where(line_row == 0, nw, jnp.where(line_row == rows - 1, sw, 0.0))
                )
                d_east = east + 0.5 * (
                    own_cond[:, cols - 1 : cols]
                    + jnp.where(line_row == 0, ne, jnp.where(line_row == rows - 1, se, 0.0))
                )
                ghosts.append((1.0 / d_north, 1.0 / d_south, 1.0 / d_west, 1.0 / d_east))
            sides[layers] = jnp.where(lane[:rows] == 0, ghosts[0][2], jnp.where(lane[:rows] == 1, ghosts[0][3], 0.0))
            beside[0:1] = ghosts[0][0]
            beside[1:2] = ghosts[0][1]
            out.cond_north[...], out.cond_south[...] = north_ref[:layers], south_ref[:layers]
            out.zone_map[...] = recv[:, 0, at_zones:at_sides]
            done(out.diagonal, out.inverse, out.sides, out.beside, out.cond_north, out.cond_south, out.zone_map)
        v_out, image_out = out.v, out.image
        fields, outside = [], []
        for layer in range(layers):
            value = (surface if layer == 0 else w_ref[layer]) * inverse_ref[layer] + s
            v_out[layer] = value
            fields.append(value)
            west = turned[rows * layer : rows * (layer + 1), 0:1]
            east = turned[rows * layer : rows * (layer + 1), 1:2]
            if coupled:
                north, south = north_ref[layer : layer + 1], south_ref[layer : layer + 1]
                if layer == 0:
                    north = north + beside[0:1] * field[block_rows : block_rows + 1]
                    south = south + beside[1:2] * field[block_rows + 1 : block_rows + 2]
                    west = west + sides[layers, :, 0:1] * west_value
                    east = east + sides[layers, :, 1:2] * east_value
            else:
                near = ghosts[layer]
                place = 2 * layers + layer
                north, south = north_ref[place : place + 1] * near[0], south_ref[place : place + 1] * near[1]
                west, east = west * near[2], east * near[3]
            outside.append(
                (
                    (north + s_north) * has_north,
                    (south + s_south) * has_south,
                    (west + s_west) * has_west,
                    (east + s_east) * has_east,
                )
            )
        done(out.v)
        images = []
        for layer in range(layers):
            value, own_cond = fields[layer], cond[layer]
            north, south, west, east = outside[layer]
            plain = stencil(value, north, south, west, east)
            carried = stencil(
                value * own_cond,
                north * cond_north[layer : layer + 1],
                south * cond_south[layer : layer + 1],
                west * sides[layer, :, 0:1],
                east * sides[layer, :, 1:2],
            )
            image = diagonal_ref[layer] * value - 0.5 * (own_cond * plain + carried)
            if layer < layers - 1:
                image = image - leak[layer] * fields[layer + 1]
            if layer > 0:
                image = image - leak[layer - 1] * fields[layer - 1]
            image_out[layer] = image
            images.append(image)
        done(out.image)
        totals = zone_totals(fields[0], get.hot[...], get.down[...])
        if final:
            rhs_ref, v0_ref, v1_ref, w0_ref = get.rhs, get.v0, get.v1, get.w0

            def dot(left, right):
                total = left[0] * right[0]
                for layer in range(1, layers):
                    total = total + left[layer] * right[layer]
                return jnp.sum(jnp.sum(total, axis=0, keepdims=True), axis=1, keepdims=True)

            w1 = [surface] + [w_ref[layer] for layer in range(1, layers)]
            products = [
                dot(v0_ref, w0_ref), dot(v0_ref, w1), dot(v1_ref, w1), dot(fields, w0_ref), dot(fields, w1),
                dot(fields, images), dot(v0_ref, rhs_ref), dot(v1_ref, rhs_ref), dot(fields, rhs_ref),
            ]
            packed = jnp.zeros((1, 128), F32)
            for place, value in enumerate(products):
                packed = jnp.where(iota((1, 128), 1) == place, value, packed)
            line = jnp.concatenate([totals, packed], axis=1)
        else:
            depth = images[0]
            for layer in range(1, layers):
                depth = depth + images[layer]
            q_next = mm(depth, get.sine_cols)
            out.q_mixed[...] = q_next
            done(out.q_mixed)
            scaled = [images[layer] * inverse_ref[layer] for layer in range(layers)]
            out.near[...], out.far[...] = choose(
                jnp.concatenate([part[0:1] for part in scaled], axis=0),
                jnp.concatenate([part[rows - 1 : rows] for part in scaled], axis=0),
            )
            done(out.near, out.far)
            first, last, left, right = rings(q_next, get)
            west, east = side_lanes(scaled, (left, right))
            line = jnp.concatenate([first, last, totals, west, east], axis=1)
        out.chunk[...] = jnp.broadcast_to(line[None], out.chunk.shape)
        done(out.chunk)

    tail_width = zones + 128
    shared = {}

    def step(number, received, near, far, more, keep=()):
        ins = dict(received=Held(received))
        if number > 0:
            ins |= dict(couple=couple, zone_map=one.zone_map, coarse=t.coarse, up_modes=t.up_modes)
            ins |= dict(coarse_rows=t.coarse_rows)
        ins |= dict(row_chain=t.row_chain, answer=t.answer, down=t.down, waves=t.waves, own_columns=t.own_columns)
        ins |= dict(around=t.around, wave_weight=t.wave_weight, ends=t.ends, sine_rows=t.sine_rows, weight=t.weight)
        ins |= dict(sine_cols=t.sine_cols, near=near, far=far, conductivity=conductivity, leakance=leakance, hot=hot)
        ins |= shared | more
        if number == 2:
            outs = dict(v=Held(area), w=Held(area), image=Held(area))
            outs |= dict(chunk=(devices, 1, tail_width))
        else:
            outs = dict(v=area, image=Held(area), q_mixed=Held((rows, cols)))
            outs |= dict(near=(layers, cols), far=(layers, cols))
            outs |= dict(chunk=(devices, 1, widths[1]))
        if number == 0:
            outs |= dict(diagonal=area, inverse=area, sides=(layers + 1, rows, 128), beside=(2, cols))
            outs |= dict(cond_north=(layers, cols), cond_south=(layers, cols), zone_map=(devices, blocks))
        elif number == 1:
            outs |= dict(w=area)
        return call(lambda get, out, done: step_body(number, get, out, done), ins, outs, keep)

    q_mixed = Held(started.q_mixed)
    one = step(0, received, near, far, dict(partial=started.partial, q_mixed=q_mixed, w=Held(rhs)))
    shared |= dict(diagonal=one.diagonal, inverse=one.inverse, sides=one.sides, beside=one.beside)
    shared |= dict(cond_north=one.cond_north, cond_south=one.cond_south)
    received = exchange(one.chunk)
    near, far = neighbours(one.near, one.far)
    two = step(1, received, near, far, dict(q_mixed=Held(one.q_mixed), w=Held(one.image)))
    received = exchange(two.chunk)
    near, far = neighbours(two.near, two.far)
    more = dict(rhs=Held(rhs), v0=one.v, v1=two.v, w0=two.w)
    after = dict(q_mixed=Held(two.q_mixed), w=Held(two.image)) | more
    last_needs = tuple(dict(v0=0, v1=0, w0=0, couple=0, down=0))
    three = step(2, received, near, far, after, last_needs)
    received = exchange(three.chunk)

    def finish_body(get, out, done):
        sums = jnp.sum(get.received[:, 0, :], axis=0, keepdims=True)
        totals = sums[:, :zones]
        reply = mm_f32(jnp.broadcast_to(totals, (8, zones)), get.couple[...])
        zone_line = get.zone_line[...]
        index = jnp.broadcast_to(zone_line, (8, blocks)).astype(jnp.int32)
        found = lookup(reply[0:1], index)[0:1]
        field = field_rows([(found, i) for i in range(block_rows)], get.down[...], block_cols)
        coupled = spread_rows8(field, rows)
        a00, a01, a11, a02, a12, a22, h0, h1, h2 = [sums[:, zones + i : zones + i + 1] for i in range(9)]
        a22 = a22 + jnp.sum(totals * reply[0:1], axis=1, keepdims=True)
        l10, l20 = a01 / a00, a02 / a00
        d1 = a11 - l10 * a01
        l21 = (a12 - l10 * a02) / d1
        d2 = a22 - l20 * a02 - l21 * (a12 - l10 * a02)
        y1 = h1 - l10 * h0
        y2 = h2 - l20 * h0 - l21 * y1
        c2 = y2 / d2
        c1 = y1 / d1 - l21 * c2
        c0 = h0 / a00 - l10 * c1 - l20 * c2
        v0, v1, v2, w0, w1, w2 = get.v0, get.v1, get.v2, get.w0, get.w1, get.w2
        rhs_ref = get.rhs
        for layer in range(layers):
            last = w2[layer] + coupled if layer == 0 else w2[layer]
            out.solution[layer] = c0 * v0[layer] + c1 * v1[layer] + c2 * v2[layer]
            out.residual[layer] = rhs_ref[layer] - c0 * w0[layer] - c1 * w1[layer] - c2 * last
        done(out.solution, out.residual)

    needs = {name: Held(getattr(three, name)) for name in last_needs}
    for name, array in dict(couple=couple, down=t.down, v0=one.v, v1=two.v, w0=two.w).items():
        needs.setdefault(name, array)
    ended = call(
        finish_body,
        dict(received=Held(received), zone_line=Held(started.zone_line), rhs=Held(rhs))
        | needs
        | dict(v2=Held(three.v), w1=Held(three.w), w2=Held(three.image)),
        dict(solution=area, residual=area),
    )
    return ended.solution, ended.residual


def solution(mesh):
    placed = (
        P(None, "slab", "grp"),
        P(None, "slab", "grp"),
        P(None, "slab", "grp"),
        P(None, "slab", "grp"),
        P("slab", "grp"),
        P("slab", "grp"),
        P(),
        P(),
        P(),
        P(),
    )
    return jax.shard_map(
        shards,
        mesh=mesh,
        in_specs=placed,
        out_specs=(P(None, "slab", "grp"), P(None, "slab", "grp")),
        check_vma=False,
    )
```

```python
import math
from types import SimpleNamespace

import jax
import jax.numpy as jnp
import numpy as np
from jax import lax
from jax.experimental import pallas as pl
from jax.experimental.pallas import tpu as pltpu
from jax.sharding import PartitionSpec as P

COUPLE = 4.0
PRECOND_T = 2.0
PRECOND_SHIFT = 3.0
HIGHEST = lax.Precision.HIGHEST
BOTH = ("slab", "grp")
VMEM_LIMIT = 24 * 1024 * 1024
F32, BF16 = jnp.float32, jnp.bfloat16


def sine_basis(count):
    index = np.arange(1, count + 1)
    basis = math.sqrt(2.0 / (count + 1)) * np.sin(np.pi * np.outer(index, index) / (count + 1))
    return basis, 4.0 * np.sin(np.pi * index / (2.0 * (count + 1))) ** 2


def fourier_basis(count):
    cells = np.arange(count)[:, None]
    waves = np.concatenate([np.arange(count // 2 + 1), np.arange(1, count // 2)])[None, :]
    turned = 2.0 * np.pi * ((cells * waves) % count) / count
    is_sine = np.arange(count)[None, :] > count // 2
    basis = np.where(is_sine, np.sin(turned), np.cos(turned)) * math.sqrt(2.0 / count)
    basis[:, 0] /= math.sqrt(2.0)
    basis[:, count // 2] /= math.sqrt(2.0)
    return basis, 4.0 * np.sin(np.pi * waves[0] / count) ** 2


def chain_tables(cross, total, block):
    half = (PRECOND_SHIFT / PRECOND_T + cross) / 2.0 + 1.0
    decay = 1.0 / (half + np.sqrt(half * half - 1.0))
    scale = 1.0 / ((1.0 - decay**total) * PRECOND_T * (1.0 / decay - decay))

    def green(distance):
        distance = distance % total
        return PRECOND_T * scale * (decay**distance + decay ** (total - distance))

    count = total // block
    tables = np.zeros((4, count, len(cross)))
    for back in range(count):
        tables[0, back] = green(block * back)
        tables[1, back] = green(block * (back - 1) - 1) + (1.0 if back == 1 % count else 0.0)
        tables[2, back] = green(block * (back + 1) + 1) + (1.0 if back == count - 1 else 0.0)
        tables[3, back] = green(block * back)
    return tables


def grid_tables(slabs, groups, rows, cols):
    rows_total, cols_total = slabs * rows, groups * cols
    sine_rows, cross_rows = sine_basis(rows)
    sine_cols, cross_cols = sine_basis(cols)
    waves, cross_waves = fourier_basis(rows_total)
    weight = 1.0 / (PRECOND_SHIFT + PRECOND_T * (cross_rows[:, None] + cross_cols[None, :]))
    wave_weight = 1.0 / (PRECOND_SHIFT + PRECOND_T * (cross_waves[:, None] + cross_cols[None, :]))
    first, last = sine_cols[0], sine_cols[-1]
    answer = np.zeros((cols, 128))
    for end, row in enumerate((0, rows - 1)):
        inside = PRECOND_T * np.einsum("ri,ij,i->jr", sine_rows, weight, sine_rows[:, row])
        answer[:, 64 * end : 64 * end + rows] = first[:, None] * inside
        answer[:, 64 * end + rows : 64 * end + 2 * rows] = last[:, None] * inside
    spread_rows = np.repeat(np.eye(rows // 8), 8, axis=0)
    spread_cols = np.repeat(np.eye(cols // 8), 8, axis=0)
    mode_rows, mode_cols = sine_rows @ spread_rows, sine_cols @ spread_cols
    mixed = np.einsum("ri,ij,ib->rbj", sine_rows, weight, mode_rows)
    coarse = np.zeros((rows // 8, cols // 8, 128))
    coarse[:, :, :rows] = np.einsum("rbj,j,jc->bcr", mixed, first, mode_cols)
    coarse[:, :, rows : 2 * rows] = np.einsum("rbj,j,jc->bcr", mixed, last, mode_cols)
    column_chain = chain_tables(cross_waves, cols_total, cols)
    tile = max(8, groups)
    own_columns = np.zeros((groups, 4, tile, rows_total))
    for group in range(groups):
        for other in range(groups):
            own_columns[group, :, other] = column_chain[:, (group - other) % groups]
    around = np.zeros((slabs, 8, rows_total))
    for slab in range(slabs):
        around[slab, 0] = waves[(rows * slab - 1) % rows_total]
        around[slab, 1] = waves[(rows * slab + rows) % rows_total]
    ends = np.zeros((8, cols))
    ends[0], ends[1] = first, last
    blocks = (rows // 8) * (cols // 8)
    down = np.tile(spread_cols, (1, rows // 8))
    exact = dict(
        weight=weight,
        row_chain=chain_tables(cross_cols, rows_total, rows).reshape(4 * slabs, cols),
        own_columns=own_columns.reshape(groups, 4 * tile, rows_total),
        around=around,
        ends=ends,
        coarse_rows=np.concatenate([mixed[0], mixed[-1]]),
    )
    split = dict(
        sine_rows=sine_rows,
        sine_cols=sine_cols,
        answer=answer,
        coarse=coarse.reshape(blocks, 128),
        waves=waves,
        wave_weight=wave_weight,
        up_modes=np.tile(mode_cols.T, (128 // (cols // 8), 1)),
    )
    tables = {name: np.asarray(table, np.float32) for name, table in exact.items()}
    for name, table in split.items():
        high = table.astype(jnp.bfloat16)
        tables[name] = np.stack([high, (table - high.astype(np.float64)).astype(jnp.bfloat16)])
    tables["down"] = down.astype(jnp.bfloat16)
    tables["place"] = np.tile(np.eye(cols // 8), (1, rows // 8)).astype(jnp.bfloat16)
    return tables


def terms(value, count):
    parts = []
    for _ in range(count):
        part = value.astype(BF16).astype(F32)
        parts.append(part)
        value = value - part
    return parts


DIMS = (((1,), (0,)), ((), ()))
DIMS_T = (((1,), (1,)), ((), ()))


def product(left, right, dims):
    return lax.dot_general(left, right, dims, preferred_element_type=F32)


def mm(value, table, dims=DIMS):
    rows = value.shape[0]
    high, low = terms(value, 2)
    both = product(jnp.concatenate([high, low], axis=0).astype(BF16), table[0], dims)
    return both[:rows] + both[rows:] + product(high.astype(BF16), table[1], dims)


def mm_left(table, value, dims=DIMS):
    rows = table[0].shape[0]
    high, low = terms(value, 2)
    both = product(jnp.concatenate([table[0], table[1]], axis=0), high.astype(BF16), dims)
    return both[:rows] + both[rows:] + product(table[0], low.astype(BF16), dims)


def mm_exact(value, table, dims=DIMS):
    rows = value.shape[0]
    every = product(jnp.concatenate(terms(value, 3), axis=0).astype(BF16), table, dims)
    return every[:rows] + every[rows : 2 * rows] + every[2 * rows :]


def mm_f32(left, right, dims=DIMS):
    return lax.dot_general(left, right, dims, precision=HIGHEST, preferred_element_type=F32)


def iota(shape, dim):
    return lax.broadcasted_iota(jnp.int32, shape, dim)


def lookup(values, index):
    rows, lanes = index.shape
    zones = values.shape[1]
    within, which = index & 127, index >> 7
    pieces = []
    for start in range(0, lanes, 128):
        part = jnp.zeros((rows, 128), F32)
        for half in range(zones // 128):
            table = jnp.broadcast_to(values[:, 128 * half : 128 * (half + 1)], (rows, 128))
            found = jnp.take_along_axis(table, within[:, start : start + 128], axis=1)
            part = jnp.where(which[:, start : start + 128] == half, found, part)
        pieces.append(part)
    return jnp.concatenate(pieces, axis=1) if len(pieces) > 1 else pieces[0]


def rings(q_mixed, t):
    sine_rows = t.sine_rows
    inside = mm_left(sine_rows, mm_left(sine_rows, q_mixed) * t.weight[...])
    rows = inside.shape[0]
    ends = t.ends
    left = jnp.sum(inside * ends[0:1], axis=1, keepdims=True)
    right = jnp.sum(inside * ends[1:2], axis=1, keepdims=True)
    return inside[0:1], inside[rows - 1 : rows], left, right


def side_lanes(parts, last=None):
    rows, cols = parts[0].shape
    lane = iota((rows, 128), 1)
    tall = [jnp.where(lane == 127, p[:, cols - 128 :], p[:, :128]) for p in parts]
    if last is not None:
        tall.append(jnp.where(lane == 127, last[1], last[0]))
    while len(tall) < 4:
        tall.append(jnp.zeros((rows, 128), F32))
    turned = jnp.concatenate(tall, axis=0).T
    return turned[0:1], turned[127:128]


def stencil(values, before, after, left, right):
    rows, cols = values.shape
    row, col = iota(values.shape, 0), iota(values.shape, 1)
    up = jnp.where(row == 0, before, pltpu.roll(values, 1, 0))
    down = jnp.where(row == rows - 1, after, pltpu.roll(values, rows - 1, 0))
    west = jnp.where(col == 0, left, pltpu.roll(values, 1, 1))
    east = jnp.where(col == cols - 1, right, pltpu.roll(values, cols - 1, 1))
    return (up + down) + (west + east)


def to_line(spread, block_cols):
    own = iota(spread.shape, 1) // block_cols == iota(spread.shape, 0)
    return jnp.sum(jnp.where(own, spread, 0.0), axis=0, keepdims=True)


def zone_totals(surface, hot, down):
    rows, cols = surface.shape
    sums = [jnp.sum(surface[8 * i : 8 * i + 8], axis=0, keepdims=True) for i in range(rows // 8)]
    sums = jnp.concatenate(sums + [jnp.zeros((8 - rows // 8, cols), F32)], axis=0)
    line = to_line(mm_exact(sums, down), cols // 8)
    line = jnp.broadcast_to(line, (8, line.shape[1]))
    return mm_exact(line, hot, DIMS_T)[0:1]


def field_rows(lines, down, block_cols):
    row, place = iota((8, lines[0][0].shape[1]), 0), iota((8, lines[0][0].shape[1]), 1) // block_cols
    picked = jnp.zeros(row.shape, F32)
    for index, (line, wanted) in enumerate(lines):
        picked = jnp.where((row == index) & (place == wanted), line, picked)
    return mm_exact(picked, down, DIMS_T)


def spread_rows8(lines, rows):
    return jnp.concatenate(
        [jnp.broadcast_to(lines[i : i + 1], (8, lines.shape[1])) for i in range(rows // 8)], axis=0
    )


def smooth(first_rows, last_rows, edges, q_mixed, slab, group, groups, t):
    devices = first_rows.shape[0]
    slabs = devices // groups
    rows, cols = q_mixed.shape
    before = jnp.zeros_like(first_rows)
    after = jnp.zeros_like(first_rows)
    chain = t.row_chain
    for back in range(slabs):
        turned_first = pltpu.roll(first_rows, groups * back, 0) if back else first_rows
        turned_last = pltpu.roll(last_rows, groups * back, 0) if back else last_rows
        line = [chain[slabs * kind + back : slabs * kind + back + 1] for kind in range(4)]
        before = before + (line[0] * turned_first + line[1] * turned_last)
        after = after + (line[2] * turned_first + line[3] * turned_last)
    mine = iota(before.shape, 0) == slab * groups + group
    own_before = jnp.sum(jnp.where(mine, before, 0.0), axis=0, keepdims=True)
    own_after = jnp.sum(jnp.where(mine, after, 0.0), axis=0, keepdims=True)
    answer = t.answer
    moved = mm(jnp.concatenate([before, after], axis=0), answer)
    lane = iota(edges.shape, 1)
    edges = edges + jnp.where(lane < 64, moved[:devices] + pltpu.roll(moved[devices:], 64, 1), 0.0)
    tile, per = max(8, groups), 128 // rows
    lane = iota(edges.shape, 1) // rows
    lines = []
    for side in range(2):
        joined = jnp.zeros_like(edges)
        for i in range(per):
            moved = pltpu.roll(edges, rows * (i - side) % 128, 1) if i != side else edges
            moved = pltpu.roll(moved, devices - groups * i, 0) if i else moved
            joined = jnp.where(lane == i, moved, joined)
        step = per * groups
        lines.append(jnp.concatenate([joined[step * p : step * p + tile] for p in range(slabs // per)], axis=1))
    waves = t.waves
    waved = mm(jnp.concatenate(lines, axis=0), waves)
    count = waved.shape[1]
    firsts, lasts = waved[:tile], waved[tile:]
    chain = t.own_columns
    table = [chain[tile * kind : tile * (kind + 1)] for kind in range(4)]
    left = jnp.sum(table[0] * firsts + table[1] * lasts, axis=0, keepdims=True)
    right = jnp.sum(table[2] * firsts + table[3] * lasts, axis=0, keepdims=True)
    row = iota((8, count), 0)
    sides = jnp.where(row == 0, left, jnp.where(row == 1, right, 0.0))
    own_rows = pl.ds(pl.multiple_of(slab * rows, rows), rows)
    columns = mm_left([waves[0, own_rows, :], waves[1, own_rows, :]], sides, DIMS_T)
    left_col, right_col = columns[:, 0:1], columns[:, 1:2]
    around = t.around
    north, south = around[0:1], around[1:2]
    four = jnp.where(
        row == 0,
        north * left,
        jnp.where(row == 1, north * right, jnp.where(row == 2, south * left, jnp.where(row == 3, south * right, 0.0))),
    )
    four = mm(four, t.wave_weight)
    ends = t.ends
    first, last = ends[0:1], ends[1:2]
    north_row = own_before + PRECOND_T * (first * four[0:1] + last * four[1:2])
    south_row = own_after + PRECOND_T * (first * four[2:3] + last * four[3:4])
    place = iota((rows, cols), 0)
    loaded = q_mixed + PRECOND_T * (
        jnp.where(place == 0, north_row, 0.0)
        + jnp.where(place == rows - 1, south_row, 0.0)
        + left_col * first
        + right_col * last
    )
    sine_rows = t.sine_rows
    inside = mm_left(sine_rows, mm_left(sine_rows, loaded) * t.weight[...])
    pad = jnp.zeros((6, cols), F32)
    whole = mm(jnp.concatenate([inside, north_row, south_row, pad], axis=0), t.sine_cols)
    return whole[:rows], whole[rows : rows + 1], whole[rows + 1 : rows + 2], left_col, right_col


class Operands:
    def __init__(self, copies, buffers, early):
        self._copies, self._buffers, self._early = copies, buffers, early

    def __getattr__(self, name):
        if name in self._copies:
            names = list(self._copies)
            for other in names if name not in names[: self._early] else names[: self._early]:
                self._copies.pop(other).wait()
            self._early = 0
        return self._buffers[name]


class Held:
    def __init__(self, array):
        self.array = array


def call(body, ins, outs, keep=(), early=0):
    names, results = list(ins), list(outs) + list(keep)
    arrays, parts, copied = [], [], []
    for place, value in enumerate(ins.values()):
        held = isinstance(value, Held)
        array, part = (value.array, None) if held else value if isinstance(value, tuple) else (value, ())
        arrays.append(pltpu.with_memory_space_constraint(array, pltpu.VMEM if held else pltpu.HBM))
        parts.append(part)
        if part is not None:
            copied.append(place)
    kinds, sent = [], []
    for place, value in enumerate(outs.values()):
        if isinstance(value, Held):
            kinds.append((value.array, F32))
        else:
            kinds.append(value if isinstance(value[-1], type(F32)) else (value, F32))
            sent.append(place)
    spaces = [
        [pl.BlockSpec(memory_space=pltpu.VMEM if isinstance(value, Held) else pltpu.HBM) for value in side.values()]
        for side in (ins, outs)
    ]
    spaces[1] += [pl.BlockSpec(memory_space=pltpu.VMEM)] * len(keep)

    def shape_of(array, part):
        if isinstance(part, str):
            return array.shape[1:]
        return tuple(len(range(*cut.indices(size))) for cut, size in zip(part, array.shape)) + array.shape[len(part) :]

    def kernel(*refs):
        given, refs = refs[: len(names)], refs[len(names) :]
        made, refs = refs[: len(results)], refs[len(results) :]
        in_sems, out_sems = refs[-2:]
        copies, buffers = {}, dict(zip(names, given))
        for slot, place in enumerate(copied):
            part = parts[place]
            origin = given[place].at[lax.axis_index(part) if isinstance(part, str) else part] if part else given[place]
            name = names[place]
            buffers[name] = made[results.index(name, len(outs))] if name in keep else refs[slot]
            copies[name] = pltpu.make_async_copy(origin, buffers[name], in_sems.at[slot])
            copies[name].start()
        built = list(made)
        for slot, place in enumerate(sent):
            built[place] = refs[len(copied) + slot]
        going = []

        def done(*which):
            for buffer in which:
                for slot, place in enumerate(sent):
                    if built[place] is buffer:
                        going.append(pltpu.make_async_copy(buffer, made[place], out_sems.at[slot]))
                        going[-1].start()

        get = Operands(copies, buffers, early)
        body(get, SimpleNamespace(**dict(zip(results, built))), done)
        for place in copied:
            getattr(get, names[place])
        assert len(going) == len(sent)
        for copy in going:
            copy.wait()

    shapes = [(shape_of(arrays[place], parts[place]), arrays[place].dtype) for place in copied]
    kept = [shapes[copied.index(names.index(name))] for name in keep]
    scratch = [
        pltpu.VMEM(*((8, 128), F32) if names[place] in keep else shape) for place, shape in zip(copied, shapes)
    ]
    scratch += [pltpu.VMEM(*kinds[place]) for place in sent]
    scratch += [pltpu.SemaphoreType.DMA((max(1, len(some)),)) for some in (copied, sent)]
    made = pl.pallas_call(
        kernel,
        out_shape=[
            pltpu.VMEM(*kind) if isinstance(value, Held) else pltpu.HBM(*kind)
            for kind, value in zip(kinds, outs.values())
        ]
        + [pltpu.VMEM(*shape) for shape in kept],
        in_specs=spaces[0],
        out_specs=spaces[1],
        scratch_shapes=scratch,
        compiler_params=pltpu.CompilerParams(vmem_limit_bytes=VMEM_LIMIT),
    )(*arrays)
    return SimpleNamespace(**dict(zip(results, made)))


def shards(
    source,
    conductivity,
    leakance,
    storage,
    et_rate,
    zone_of_block,
    zone_recharge,
    zone_weight,
    pair_zones,
    pair_weight,
):
    slabs, groups = lax.axis_size("slab"), lax.axis_size("grp")
    layers, rows, cols = source.shape
    devices = slabs * groups
    zones = zone_weight.shape[0]
    tables = {name: jnp.asarray(table) for name, table in grid_tables(slabs, groups, rows, cols).items()}
    t = SimpleNamespace(**tables)
    t.own_columns, t.around = (t.own_columns, "grp"), (t.around, "slab")
    block_rows, block_cols = rows // 8, cols // 8
    blocks = block_rows * block_cols
    at_zones = 2 * cols
    at_sides = at_zones + blocks
    widths = (at_sides + 5 * 128, at_zones + zones + 2 * 128)
    area = (layers, rows, cols)

    def neighbours(near, far):
        across = [(i, i + 1) for i in range(1, slabs - 1, 2)]
        return (
            lax.ppermute(near, "slab", [(i, i ^ 1) for i in range(slabs)]),
            lax.ppermute(far, "slab", across + [(j, i) for i, j in across]),
        )

    def choose(near, far):
        odd = lax.axis_index("slab") % 2 == 1
        return jnp.where(odd, near, far), jnp.where(odd, far, near)

    def exchange(chunk):
        return lax.all_to_all(chunk, BOTH, split_axis=0, concat_axis=0, tiled=True)

    def start_body(get, out, done):
        ids = get.zone_of_block[...].astype(F32)
        ids = jnp.concatenate([ids, jnp.zeros((8 - block_rows, block_cols), F32)], axis=0)
        zone_line = to_line(mm_exact(ids, get.place[...]), block_cols)
        index = jnp.broadcast_to(zone_line, (8, blocks)).astype(jnp.int32)
        found = lookup(get.zone_recharge[...], index)[0:1]
        field = field_rows([(found, i) for i in range(block_rows)], get.down[...], block_cols)
        source_ref, rhs = get.source, out.rhs
        rhs[0] = source_ref[0] + spread_rows8(field, rows)
        for layer in range(1, layers):
            rhs[layer] = source_ref[layer]
        done(out.rhs)
        total = rhs[0]
        for layer in range(1, layers):
            total = total + rhs[layer]
        q_mixed = mm(total, get.sine_cols)
        out.q_mixed[...] = q_mixed
        done(out.q_mixed)
        cond, store, leak = get.conductivity, get.storage, get.leakance
        partial, edge_rows = out.partial, [[], []]
        for layer in range(layers):
            own = cond[layer]
            diagonal = store[layer] + 0.5 * (4.0 * own + stencil(own, 0.0, 0.0, 0.0, 0.0))
            if layer < layers - 1:
                diagonal = diagonal + leak[layer]
            if layer > 0:
                diagonal = diagonal + leak[layer - 1]
            if layer == 0:
                diagonal = diagonal + get.et_rate[...]
            partial[layer] = diagonal
            for end, row in enumerate((0, rows - 1)):
                edge_rows[end] += [own[row : row + 1], diagonal[row : row + 1], rhs[layer, row : row + 1]]
        first, last = [
            jnp.concatenate([rows_of[place] for kind in range(3) for place in range(kind, 3 * layers, 3)], axis=0)
            for rows_of in edge_rows
        ]
        out.near[...], out.far[...] = choose(first, last)
        done(out.partial, out.near, out.far)
        first, last, left, right = rings(q_mixed, get)
        sides = side_lanes([rhs[layer] for layer in range(layers)], (left, right))
        sides += side_lanes(
            [cond[layer] for layer in range(layers)], (partial[0, :, 0:1], partial[0, :, cols - 1 : cols])
        )
        west, east = side_lanes([partial[layer] for layer in range(1, layers)])
        both = jnp.where(iota((1, 128), 1) < 64, west, pltpu.roll(east, 64, 1))
        line = jnp.concatenate([first, last, zone_line, *sides, both], axis=1)
        out.chunk[...] = jnp.broadcast_to(line[None], out.chunk.shape)
        out.zone_line[...] = zone_line
        done(out.chunk)

    started = call(
        start_body,
        dict(
            zone_of_block=zone_of_block,
            zone_recharge=zone_recharge[None],
            place=t.place,
            down=t.down,
            source=source,
            sine_cols=t.sine_cols,
            conductivity=conductivity,
            storage=storage,
            leakance=leakance,
            et_rate=et_rate,
            sine_rows=t.sine_rows,
            weight=t.weight,
            ends=t.ends,
        ),
        dict(
            rhs=Held(area),
            q_mixed=Held((rows, cols)),
            partial=area,
            near=(3 * layers, cols),
            far=(3 * layers, cols),
            zone_line=Held((1, blocks)),
            chunk=(devices, 1, widths[0]),
        ),
        early=4,
    )
    rhs = started.rhs
    received = exchange(started.chunk)
    near, far = neighbours(started.near, started.far)

    def couple_body(get, out, done):
        ids, weights = get.pair_zones, get.pair_weight
        place = iota((zones, ids.shape[1]), 0)
        table = (place == ids[0:1]).astype(F32) - (place == ids[1:2]).astype(F32)
        matrix = mm_f32(table * weights[...], table, DIMS_T)
        own = iota((zones, zones), 0) == iota((zones, zones), 1)
        matrix = matrix + jnp.where(own, get.zone_weight[...], 0.0)
        out.couple[...] = (COUPLE * zones / (slabs * rows * groups * cols)) * matrix
        line = get.zone_line[...].astype(jnp.int32)
        out.hot[...] = (iota((zones, blocks), 0) == line).astype(F32).astype(BF16)
        done(out.couple, out.hot)

    coupling = call(
        couple_body,
        dict(pair_zones=pair_zones.T, pair_weight=pair_weight[None], zone_weight=zone_weight[None])
        | dict(zone_line=Held(started.zone_line)),
        dict(couple=(zones, zones), hot=((zones, blocks), BF16)),
    )
    couple, hot = coupling.couple, coupling.hot

    def step_body(number, get, out, done):
        coupled, final = number > 0, number == 2
        slab, group = lax.axis_index("slab"), lax.axis_index("grp")
        own = slab * groups + group
        has_north = (slab > 0).astype(F32)
        has_south = (slab < slabs - 1).astype(F32)
        has_west = (group > 0).astype(F32)
        has_east = (group < groups - 1).astype(F32)
        recv = get.received

        def of(shift, start):
            return recv[pl.ds(jnp.clip(own + shift, 0, devices - 1), 1), 0, start : start + 128]

        first_rows, last_rows = recv[:, 0, :cols], recv[:, 0, cols : 2 * cols]
        sides_at = at_sides if not coupled else at_zones + zones
        lane = iota((devices, 128), 1)
        edges = jnp.where(
            lane < rows,
            pltpu.roll(recv[:, 0, sides_at : sides_at + 128], rows, 1),
            pltpu.roll(recv[:, 0, sides_at + 128 : sides_at + 256], 2 * rows, 1),
        )
        edges = jnp.where(lane < 2 * rows, edges, 0.0)
        q_in = get.q_mixed[...]
        w_ref = get.w
        surface = w_ref[0]
        if coupled:
            totals = jnp.sum(recv[:, 0, at_zones : at_zones + zones], axis=0, keepdims=True)
            reply = mm_f32(jnp.broadcast_to(totals, (8, zones)), get.couple[...])[0:1]
            every = lookup(reply, get.zone_map[...].astype(jnp.int32))
            edges = edges + mm(every, get.coarse)
            share = 128 // block_cols
            inner = iota((devices, 128), 1) // block_cols
            slabs_of = [
                jnp.where(inner == i % share, every[:, 128 * (i // share) : 128 * (i // share + 1)], 0.0)
                for i in range(block_rows)
            ]
            modes_of = mm(jnp.concatenate(slabs_of, axis=0), get.up_modes)
            device = iota(first_rows.shape, 0)
            modes = []
            for i in range(block_rows):
                part = modes_of[devices * i : devices * (i + 1)]
                first_rows = first_rows + get.coarse_rows[i : i + 1] * part
                last_rows = last_rows + get.coarse_rows[block_rows + i : block_rows + i + 1] * part
                modes.append(jnp.sum(jnp.where(device == own, part, 0.0), axis=0, keepdims=True))
            modes = jnp.concatenate(modes, axis=0)
            device = iota(every.shape, 0)
            line_of = lambda shift: jnp.sum(
                jnp.where(device == own + shift, every, 0.0), axis=0, keepdims=True
            )
            mine = line_of(0)
            wanted = [(mine, i) for i in range(block_rows)]
            wanted += [(line_of(-groups), block_rows - 1), (line_of(groups), 0)]
            field = field_rows(wanted, get.down[...], block_cols)
            q_in = q_in + spread_rows8(modes, rows)
            surface = surface + spread_rows8(field, rows)
            column = iota((rows, blocks), 1)
            base = block_cols * (iota((rows, blocks), 0) // 8)
            west_value = jnp.sum(
                jnp.where(column == base + block_cols - 1, line_of(-1), 0.0), axis=1, keepdims=True
            )
            east_value = jnp.sum(jnp.where(column == base, line_of(1), 0.0), axis=1, keepdims=True)
        if final:
            out.w[0] = surface
            for layer in range(1, layers):
                out.w[layer] = w_ref[layer]
            done(out.w)
        elif coupled:
            out.w[0] = surface
            for layer in range(1, layers):
                out.w[layer] = w_ref[layer]
            done(out.w)
        s, s_north, s_south, s_west, s_east = smooth(
            first_rows, last_rows, edges, q_in, slab, group, groups, get
        )
        cond, leak = get.conductivity, get.leakance
        north_ref, south_ref = choose(get.near[...], get.far[...])
        row, col = iota((rows, cols), 0), iota((rows, cols), 1)
        if coupled:
            cond_north, cond_south = get.cond_north, get.cond_south
            sides = get.sides
            lanes = [of(-1, sides_at + 128), of(1, sides_at)]
            diagonal_ref, inverse_ref = get.diagonal, get.inverse
            beside = get.beside
        else:
            cond_north, cond_south = north_ref, south_ref
            lanes = [of(-1, sides_at + 128), of(1, sides_at)]
            lanes += [of(-1, sides_at + 384) * has_west, of(1, sides_at + 256) * has_east]
            lanes += [of(-1, sides_at + 512), of(1, sides_at + 512)]
            diagonal_ref, inverse_ref, sides, beside = out.diagonal, out.inverse, out.sides, out.beside
        turned = jnp.concatenate(lanes + [jnp.zeros((128 - len(lanes), 128), F32)], axis=0).T
        if not coupled:
            corner = [
                of(-groups - 1, sides_at + 384) * (has_north * has_west),
                of(-groups + 1, sides_at + 256) * (has_north * has_east),
                of(groups - 1, sides_at + 384) * (has_south * has_west),
                of(groups + 1, sides_at + 256) * (has_south * has_east),
            ]
            ghosts = []
            partial = get.partial
            line_col, line_row = iota((1, cols), 1), iota((rows, 1), 0)
            for layer in range(layers):
                c_north, c_south = north_ref[layer : layer + 1], south_ref[layer : layer + 1]
                c_west = turned[rows * layer : rows * (layer + 1), 2:3]
                c_east = turned[rows * layer : rows * (layer + 1), 3:4]
                both = jnp.where(lane[:rows] == 0, c_west, jnp.where(lane[:rows] == 1, c_east, 0.0))
                sides[layer] = both
                diagonal = partial[layer] + 0.5 * (
                    jnp.where(row == 0, c_north, 0.0)
                    + jnp.where(row == rows - 1, c_south, 0.0)
                    + jnp.where(col == 0, c_west, 0.0)
                    + jnp.where(col == cols - 1, c_east, 0.0)
                )
                diagonal_ref[layer] = diagonal
                inverse_ref[layer] = 1.0 / diagonal
                start, end = rows * layer, rows * layer + rows - 1
                nw, ne = corner[0][:, end : end + 1], corner[1][:, end : end + 1]
                sw, se = corner[2][:, start : start + 1], corner[3][:, start : start + 1]
                own_cond = cond[layer]
                d_north = north_ref[layers + layer : layers + layer + 1] + 0.5 * (
                    own_cond[0:1] + jnp.where(line_col == 0, nw, jnp.where(line_col == cols - 1, ne, 0.0))
                )
                d_south = south_ref[layers + layer : layers + layer + 1] + 0.5 * (
                    own_cond[rows - 1 : rows]
                    + jnp.where(line_col == 0, sw, jnp.where(line_col == cols - 1, se, 0.0))
                )
                if layer == 0:
                    west, east = turned[3 * rows : 4 * rows, 2:3], turned[3 * rows : 4 * rows, 3:4]
                else:
                    west = turned[64 + rows * (layer - 1) : 64 + rows * layer, 4:5]
                    east = turned[rows * (layer - 1) : rows * layer, 5:6]
                d_west = west + 0.5 * (
                    own_cond[:, 0:1] + jnp.where(line_row == 0, nw, jnp.where(line_row == rows - 1, sw, 0.0))
                )
                d_east = east + 0.5 * (
                    own_cond[:, cols - 1 : cols]
                    + jnp.where(line_row == 0, ne, jnp.where(line_row == rows - 1, se, 0.0))
                )
                ghosts.append((1.0 / d_north, 1.0 / d_south, 1.0 / d_west, 1.0 / d_east))
            sides[layers] = jnp.where(lane[:rows] == 0, ghosts[0][2], jnp.where(lane[:rows] == 1, ghosts[0][3], 0.0))
            beside[0:1] = ghosts[0][0]
            beside[1:2] = ghosts[0][1]
            out.cond_north[...], out.cond_south[...] = north_ref[:layers], south_ref[:layers]
            out.zone_map[...] = recv[:, 0, at_zones:at_sides]
            done(out.diagonal, out.inverse, out.sides, out.beside, out.cond_north, out.cond_south, out.zone_map)
        v_out, image_out = out.v, out.image
        fields, outside = [], []
        for layer in range(layers):
            value = (surface if layer == 0 else w_ref[layer]) * inverse_ref[layer] + s
            v_out[layer] = value
            fields.append(value)
            west = turned[rows * layer : rows * (layer + 1), 0:1]
            east = turned[rows * layer : rows * (layer + 1), 1:2]
            if coupled:
                north, south = north_ref[layer : layer + 1], south_ref[layer : layer + 1]
                if layer == 0:
                    north = north + beside[0:1] * field[block_rows : block_rows + 1]
                    south = south + beside[1:2] * field[block_rows + 1 : block_rows + 2]
                    west = west + sides[layers, :, 0:1] * west_value
                    east = east + sides[layers, :, 1:2] * east_value
            else:
                near = ghosts[layer]
                place = 2 * layers + layer
                north, south = north_ref[place : place + 1] * near[0], south_ref[place : place + 1] * near[1]
                west, east = west * near[2], east * near[3]
            outside.append(
                (
                    (north + s_north) * has_north,
                    (south + s_south) * has_south,
                    (west + s_west) * has_west,
                    (east + s_east) * has_east,
                )
            )
        done(out.v)
        images = []
        for layer in range(layers):
            value, own_cond = fields[layer], cond[layer]
            north, south, west, east = outside[layer]
            plain = stencil(value, north, south, west, east)
            carried = stencil(
                value * own_cond,
                north * cond_north[layer : layer + 1],
                south * cond_south[layer : layer + 1],
                west * sides[layer, :, 0:1],
                east * sides[layer, :, 1:2],
            )
            image = diagonal_ref[layer] * value - 0.5 * (own_cond * plain + carried)
            if layer < layers - 1:
                image = image - leak[layer] * fields[layer + 1]
            if layer > 0:
                image = image - leak[layer - 1] * fields[layer - 1]
            image_out[layer] = image
            images.append(image)
        done(out.image)
        totals = zone_totals(fields[0], get.hot[...], get.down[...])
        if final:
            rhs_ref, v0_ref, v1_ref, w0_ref = get.rhs, get.v0, get.v1, get.w0

            def dot(left, right):
                total = left[0] * right[0]
                for layer in range(1, layers):
                    total = total + left[layer] * right[layer]
                return jnp.sum(jnp.sum(total, axis=0, keepdims=True), axis=1, keepdims=True)

            w1 = [surface] + [w_ref[layer] for layer in range(1, layers)]
            products = [
                dot(v0_ref, w0_ref), dot(v0_ref, w1), dot(v1_ref, w1), dot(fields, w0_ref), dot(fields, w1),
                dot(fields, images), dot(v0_ref, rhs_ref), dot(v1_ref, rhs_ref), dot(fields, rhs_ref),
            ]
            packed = jnp.zeros((1, 128), F32)
            for place, value in enumerate(products):
                packed = jnp.where(iota((1, 128), 1) == place, value, packed)
            line = jnp.concatenate([totals, packed], axis=1)
        else:
            depth = images[0]
            for layer in range(1, layers):
                depth = depth + images[layer]
            q_next = mm(depth, get.sine_cols)
            out.q_mixed[...] = q_next
            done(out.q_mixed)
            scaled = [images[layer] * inverse_ref[layer] for layer in range(layers)]
            out.near[...], out.far[...] = choose(
                jnp.concatenate([part[0:1] for part in scaled], axis=0),
                jnp.concatenate([part[rows - 1 : rows] for part in scaled], axis=0),
            )
            done(out.near, out.far)
            first, last, left, right = rings(q_next, get)
            west, east = side_lanes(scaled, (left, right))
            line = jnp.concatenate([first, last, totals, west, east], axis=1)
        out.chunk[...] = jnp.broadcast_to(line[None], out.chunk.shape)
        done(out.chunk)

    tail_width = zones + 128
    shared = {}

    def step(number, received, near, far, more, keep=()):
        ins = dict(received=Held(received))
        if number > 0:
            ins |= dict(couple=couple, zone_map=one.zone_map, coarse=t.coarse, up_modes=t.up_modes)
            ins |= dict(coarse_rows=t.coarse_rows)
        ins |= dict(row_chain=t.row_chain, answer=t.answer, down=t.down, waves=t.waves, own_columns=t.own_columns)
        ins |= dict(around=t.around, wave_weight=t.wave_weight, ends=t.ends, sine_rows=t.sine_rows, weight=t.weight)
        ins |= dict(sine_cols=t.sine_cols, near=near, far=far, conductivity=conductivity, leakance=leakance, hot=hot)
        ins |= shared | more
        ins |= {name: Held(getattr(one, name)) for name in steady} if number else {}
        if number == 2:
            outs = dict(v=Held(area), w=Held(area), image=Held(area))
            outs |= dict(chunk=(devices, 1, tail_width))
        else:
            outs = dict(v=area, image=Held(area), q_mixed=Held((rows, cols)))
            outs |= dict(near=(layers, cols), far=(layers, cols))
            outs |= dict(chunk=(devices, 1, widths[1]))
        if number == 0:
            outs |= dict(diagonal=area, inverse=area, sides=(layers + 1, rows, 128), beside=(2, cols))
            outs |= dict(cond_north=(layers, cols), cond_south=(layers, cols), zone_map=(devices, blocks))
        elif number == 1:
            outs |= dict(w=area)
        return call(lambda get, out, done: step_body(number, get, out, done), ins, outs, keep, early=5)

    q_mixed = Held(started.q_mixed)
    steady = tuple(dict(sine_cols=0, wave_weight=0))
    one = step(0, received, near, far, dict(partial=started.partial, q_mixed=q_mixed, w=Held(rhs)), steady)
    shared |= dict(diagonal=one.diagonal, inverse=one.inverse, sides=one.sides, beside=one.beside)
    shared |= dict(cond_north=one.cond_north, cond_south=one.cond_south)
    received = exchange(one.chunk)
    near, far = neighbours(one.near, one.far)
    two = step(1, received, near, far, dict(q_mixed=Held(one.q_mixed), w=Held(one.image)))
    received = exchange(two.chunk)
    near, far = neighbours(two.near, two.far)
    more = dict(rhs=Held(rhs), v0=one.v, v1=two.v, w0=two.w)
    after = dict(q_mixed=Held(two.q_mixed), w=Held(two.image)) | more
    last_needs = tuple(dict(v0=0, v1=0, w0=0, couple=0, down=0))
    three = step(2, received, near, far, after, last_needs)
    received = exchange(three.chunk)

    def finish_body(get, out, done):
        sums = jnp.sum(get.received[:, 0, :], axis=0, keepdims=True)
        totals = sums[:, :zones]
        reply = mm_f32(jnp.broadcast_to(totals, (8, zones)), get.couple[...])
        zone_line = get.zone_line[...]
        index = jnp.broadcast_to(zone_line, (8, blocks)).astype(jnp.int32)
        found = lookup(reply[0:1], index)[0:1]
        field = field_rows([(found, i) for i in range(block_rows)], get.down[...], block_cols)
        coupled = spread_rows8(field, rows)
        a00, a01, a11, a02, a12, a22, h0, h1, h2 = [sums[:, zones + i : zones + i + 1] for i in range(9)]
        a22 = a22 + jnp.sum(totals * reply[0:1], axis=1, keepdims=True)
        l10, l20 = a01 / a00, a02 / a00
        d1 = a11 - l10 * a01
        l21 = (a12 - l10 * a02) / d1
        d2 = a22 - l20 * a02 - l21 * (a12 - l10 * a02)
        y1 = h1 - l10 * h0
        y2 = h2 - l20 * h0 - l21 * y1
        c2 = y2 / d2
        c1 = y1 / d1 - l21 * c2
        c0 = h0 / a00 - l10 * c1 - l20 * c2
        v0, v1, v2, w0, w1, w2 = get.v0, get.v1, get.v2, get.w0, get.w1, get.w2
        rhs_ref = get.rhs
        for layer in range(layers):
            last = w2[layer] + coupled if layer == 0 else w2[layer]
            out.solution[layer] = c0 * v0[layer] + c1 * v1[layer] + c2 * v2[layer]
            out.residual[layer] = rhs_ref[layer] - c0 * w0[layer] - c1 * w1[layer] - c2 * last
        done(out.solution, out.residual)

    needs = {name: Held(getattr(three, name)) for name in last_needs}
    for name, array in dict(couple=couple, down=t.down, v0=one.v, v1=two.v, w0=two.w).items():
        needs.setdefault(name, array)
    ended = call(
        finish_body,
        dict(received=Held(received), zone_line=Held(started.zone_line), rhs=Held(rhs))
        | needs
        | dict(v2=Held(three.v), w1=Held(three.w), w2=Held(three.image)),
        dict(solution=area, residual=area),
    )
    return ended.solution, ended.residual


def solution(mesh):
    placed = (
        P(None, "slab", "grp"),
        P(None, "slab", "grp"),
        P(None, "slab", "grp"),
        P(None, "slab", "grp"),
        P("slab", "grp"),
        P("slab", "grp"),
        P(),
        P(),
        P(),
        P(),
    )
    return jax.shard_map(
        shards,
        mesh=mesh,
        in_specs=placed,
        out_specs=(P(None, "slab", "grp"), P(None, "slab", "grp")),
        check_vma=False,
    )
```

```python
import math
from types import SimpleNamespace

import jax
import jax.numpy as jnp
import numpy as np
from jax import lax
from jax.experimental import pallas as pl
from jax.experimental.pallas import tpu as pltpu
from jax.sharding import PartitionSpec as P

COUPLE = 4.0
PRECOND_T = 2.0
PRECOND_SHIFT = 3.0
HIGHEST = lax.Precision.HIGHEST
BOTH = ("slab", "grp")
VMEM_LIMIT = 24 * 1024 * 1024
F32, BF16 = jnp.float32, jnp.bfloat16


def sine_basis(count):
    index = np.arange(1, count + 1)
    basis = math.sqrt(2.0 / (count + 1)) * np.sin(np.pi * np.outer(index, index) / (count + 1))
    return basis, 4.0 * np.sin(np.pi * index / (2.0 * (count + 1))) ** 2


def fourier_basis(count):
    cells = np.arange(count)[:, None]
    waves = np.concatenate([np.arange(count // 2 + 1), np.arange(1, count // 2)])[None, :]
    turned = 2.0 * np.pi * ((cells * waves) % count) / count
    is_sine = np.arange(count)[None, :] > count // 2
    basis = np.where(is_sine, np.sin(turned), np.cos(turned)) * math.sqrt(2.0 / count)
    basis[:, 0] /= math.sqrt(2.0)
    basis[:, count // 2] /= math.sqrt(2.0)
    return basis, 4.0 * np.sin(np.pi * waves[0] / count) ** 2


def chain_tables(cross, total, block):
    half = (PRECOND_SHIFT / PRECOND_T + cross) / 2.0 + 1.0
    decay = 1.0 / (half + np.sqrt(half * half - 1.0))
    scale = 1.0 / ((1.0 - decay**total) * PRECOND_T * (1.0 / decay - decay))

    def green(distance):
        distance = distance % total
        return PRECOND_T * scale * (decay**distance + decay ** (total - distance))

    count = total // block
    tables = np.zeros((4, count, len(cross)))
    for back in range(count):
        tables[0, back] = green(block * back)
        tables[1, back] = green(block * (back - 1) - 1) + (1.0 if back == 1 % count else 0.0)
        tables[2, back] = green(block * (back + 1) + 1) + (1.0 if back == count - 1 else 0.0)
        tables[3, back] = green(block * back)
    return tables


def grid_tables(slabs, groups, rows, cols):
    rows_total, cols_total = slabs * rows, groups * cols
    sine_rows, cross_rows = sine_basis(rows)
    sine_cols, cross_cols = sine_basis(cols)
    waves, cross_waves = fourier_basis(rows_total)
    weight = 1.0 / (PRECOND_SHIFT + PRECOND_T * (cross_rows[:, None] + cross_cols[None, :]))
    wave_weight = 1.0 / (PRECOND_SHIFT + PRECOND_T * (cross_waves[:, None] + cross_cols[None, :]))
    first, last = sine_cols[0], sine_cols[-1]
    answer = np.zeros((cols, 128))
    for end, row in enumerate((0, rows - 1)):
        inside = PRECOND_T * np.einsum("ri,ij,i->jr", sine_rows, weight, sine_rows[:, row])
        answer[:, 64 * end : 64 * end + rows] = first[:, None] * inside
        answer[:, 64 * end + rows : 64 * end + 2 * rows] = last[:, None] * inside
    spread_rows = np.repeat(np.eye(rows // 8), 8, axis=0)
    spread_cols = np.repeat(np.eye(cols // 8), 8, axis=0)
    mode_rows, mode_cols = sine_rows @ spread_rows, sine_cols @ spread_cols
    mixed = np.einsum("ri,ij,ib->rbj", sine_rows, weight, mode_rows)
    coarse = np.zeros((rows // 8, cols // 8, 128))
    coarse[:, :, :rows] = np.einsum("rbj,j,jc->bcr", mixed, first, mode_cols)
    coarse[:, :, rows : 2 * rows] = np.einsum("rbj,j,jc->bcr", mixed, last, mode_cols)
    column_chain = chain_tables(cross_waves, cols_total, cols)
    tile = max(8, groups)
    own_columns = np.zeros((groups, 4, tile, rows_total))
    for group in range(groups):
        for other in range(groups):
            own_columns[group, :, other] = column_chain[:, (group - other) % groups]
    around = np.zeros((slabs, 8, rows_total))
    for slab in range(slabs):
        around[slab, 0] = waves[(rows * slab - 1) % rows_total]
        around[slab, 1] = waves[(rows * slab + rows) % rows_total]
    ends = np.zeros((8, cols))
    ends[0], ends[1] = first, last
    blocks = (rows // 8) * (cols // 8)
    down = np.tile(spread_cols, (1, rows // 8))
    exact = dict(
        weight=weight,
        row_chain=chain_tables(cross_cols, rows_total, rows).reshape(4 * slabs, cols),
        own_columns=own_columns.reshape(groups, 4 * tile, rows_total),
        around=around,
        ends=ends,
        coarse_rows=np.concatenate([mixed[0], mixed[-1]]),
    )
    split = dict(
        sine_rows=sine_rows,
        sine_cols=sine_cols,
        answer=answer,
        coarse=coarse.reshape(blocks, 128),
        waves=waves,
        wave_weight=wave_weight,
        up_modes=np.tile(mode_cols.T, (128 // (cols // 8), 1)),
    )
    tables = {name: np.asarray(table, np.float32) for name, table in exact.items()}
    for name, table in split.items():
        high = table.astype(jnp.bfloat16)
        tables[name] = np.stack([high, (table - high.astype(np.float64)).astype(jnp.bfloat16)])
    tables["down"] = down.astype(jnp.bfloat16)
    tables["place"] = np.tile(np.eye(cols // 8), (1, rows // 8)).astype(jnp.bfloat16)
    return tables


def terms(value, count):
    parts = []
    for _ in range(count):
        part = value.astype(BF16).astype(F32)
        parts.append(part)
        value = value - part
    return parts


DIMS = (((1,), (0,)), ((), ()))
DIMS_T = (((1,), (1,)), ((), ()))


def product(left, right, dims):
    return lax.dot_general(left, right, dims, preferred_element_type=F32)


def mm(value, table, dims=DIMS):
    rows = value.shape[0]
    high, low = terms(value, 2)
    both = product(jnp.concatenate([high, low], axis=0).astype(BF16), table[0], dims)
    return both[:rows] + both[rows:] + product(high.astype(BF16), table[1], dims)


def mm_left(table, value, dims=DIMS):
    rows = table[0].shape[0]
    high, low = terms(value, 2)
    both = product(jnp.concatenate([table[0], table[1]], axis=0), high.astype(BF16), dims)
    return both[:rows] + both[rows:] + product(table[0], low.astype(BF16), dims)


def mm_exact(value, table, dims=DIMS):
    rows = value.shape[0]
    every = product(jnp.concatenate(terms(value, 3), axis=0).astype(BF16), table, dims)
    return every[:rows] + every[rows : 2 * rows] + every[2 * rows :]


def mm_f32(left, right, dims=DIMS):
    return lax.dot_general(left, right, dims, precision=HIGHEST, preferred_element_type=F32)


def iota(shape, dim):
    return lax.broadcasted_iota(jnp.int32, shape, dim)


def lookup(values, index):
    rows, lanes = index.shape
    zones = values.shape[1]
    within, which = index & 127, index >> 7
    pieces = []
    for start in range(0, lanes, 128):
        part = jnp.zeros((rows, 128), F32)
        for half in range(zones // 128):
            table = jnp.broadcast_to(values[:, 128 * half : 128 * (half + 1)], (rows, 128))
            found = jnp.take_along_axis(table, within[:, start : start + 128], axis=1)
            part = jnp.where(which[:, start : start + 128] == half, found, part)
        pieces.append(part)
    return jnp.concatenate(pieces, axis=1) if len(pieces) > 1 else pieces[0]


def rings(q_mixed, t):
    sine_rows = t.sine_rows
    inside = mm_left(sine_rows, mm_left(sine_rows, q_mixed) * t.weight[...])
    rows = inside.shape[0]
    ends = t.ends
    left = jnp.sum(inside * ends[0:1], axis=1, keepdims=True)
    right = jnp.sum(inside * ends[1:2], axis=1, keepdims=True)
    return inside[0:1], inside[rows - 1 : rows], left, right


def side_lanes(parts, last=None):
    rows, cols = parts[0].shape
    lane = iota((rows, 128), 1)
    tall = [jnp.where(lane == 127, p[:, cols - 128 :], p[:, :128]) for p in parts]
    if last is not None:
        tall.append(jnp.where(lane == 127, last[1], last[0]))
    while len(tall) < 4:
        tall.append(jnp.zeros((rows, 128), F32))
    turned = jnp.concatenate(tall, axis=0).T
    return turned[0:1], turned[127:128]


def stencil(values, before, after, left, right):
    rows, cols = values.shape
    row, col = iota(values.shape, 0), iota(values.shape, 1)
    up = jnp.where(row == 0, before, pltpu.roll(values, 1, 0))
    down = jnp.where(row == rows - 1, after, pltpu.roll(values, rows - 1, 0))
    west = jnp.where(col == 0, left, pltpu.roll(values, 1, 1))
    east = jnp.where(col == cols - 1, right, pltpu.roll(values, cols - 1, 1))
    return (up + down) + (west + east)


def to_line(spread, block_cols):
    own = iota(spread.shape, 1) // block_cols == iota(spread.shape, 0)
    return jnp.sum(jnp.where(own, spread, 0.0), axis=0, keepdims=True)


def zone_totals(surface, hot, down):
    rows, cols = surface.shape
    sums = [jnp.sum(surface[8 * i : 8 * i + 8], axis=0, keepdims=True) for i in range(rows // 8)]
    sums = jnp.concatenate(sums + [jnp.zeros((8 - rows // 8, cols), F32)], axis=0)
    line = to_line(mm_exact(sums, down), cols // 8)
    line = jnp.broadcast_to(line, (8, line.shape[1]))
    return mm_exact(line, hot, DIMS_T)[0:1]


def field_rows(lines, down, block_cols):
    row, place = iota((8, lines[0][0].shape[1]), 0), iota((8, lines[0][0].shape[1]), 1) // block_cols
    picked = jnp.zeros(row.shape, F32)
    for index, (line, wanted) in enumerate(lines):
        picked = jnp.where((row == index) & (place == wanted), line, picked)
    return mm_exact(picked, down, DIMS_T)


def spread_rows8(lines, rows):
    return jnp.concatenate(
        [jnp.broadcast_to(lines[i : i + 1], (8, lines.shape[1])) for i in range(rows // 8)], axis=0
    )


def smooth(first_rows, last_rows, edges, q_mixed, slab, group, groups, t):
    devices = first_rows.shape[0]
    slabs = devices // groups
    rows, cols = q_mixed.shape
    before = jnp.zeros_like(first_rows)
    after = jnp.zeros_like(first_rows)
    chain = t.row_chain
    for back in range(slabs):
        turned_first = pltpu.roll(first_rows, groups * back, 0) if back else first_rows
        turned_last = pltpu.roll(last_rows, groups * back, 0) if back else last_rows
        line = [chain[slabs * kind + back : slabs * kind + back + 1] for kind in range(4)]
        before = before + (line[0] * turned_first + line[1] * turned_last)
        after = after + (line[2] * turned_first + line[3] * turned_last)
    mine = iota(before.shape, 0) == slab * groups + group
    own_before = jnp.sum(jnp.where(mine, before, 0.0), axis=0, keepdims=True)
    own_after = jnp.sum(jnp.where(mine, after, 0.0), axis=0, keepdims=True)
    answer = t.answer
    moved = mm(jnp.concatenate([before, after], axis=0), answer)
    lane = iota(edges.shape, 1)
    edges = edges + jnp.where(lane < 64, moved[:devices] + pltpu.roll(moved[devices:], 64, 1), 0.0)
    tile, per = max(8, groups), 128 // rows
    lane = iota(edges.shape, 1) // rows
    lines = []
    for side in range(2):
        joined = jnp.zeros_like(edges)
        for i in range(per):
            moved = pltpu.roll(edges, rows * (i - side) % 128, 1) if i != side else edges
            moved = pltpu.roll(moved, devices - groups * i, 0) if i else moved
            joined = jnp.where(lane == i, moved, joined)
        step = per * groups
        lines.append(jnp.concatenate([joined[step * p : step * p + tile] for p in range(slabs // per)], axis=1))
    waves = t.waves
    waved = mm(jnp.concatenate(lines, axis=0), waves)
    count = waved.shape[1]
    firsts, lasts = waved[:tile], waved[tile:]
    chain = t.own_columns
    table = [chain[tile * kind : tile * (kind + 1)] for kind in range(4)]
    left = jnp.sum(table[0] * firsts + table[1] * lasts, axis=0, keepdims=True)
    right = jnp.sum(table[2] * firsts + table[3] * lasts, axis=0, keepdims=True)
    row = iota((8, count), 0)
    sides = jnp.where(row == 0, left, jnp.where(row == 1, right, 0.0))
    own_rows = pl.ds(pl.multiple_of(slab * rows, rows), rows)
    columns = mm_left([waves[0, own_rows, :], waves[1, own_rows, :]], sides, DIMS_T)
    left_col, right_col = columns[:, 0:1], columns[:, 1:2]
    around = t.around
    north, south = around[0:1], around[1:2]
    four = jnp.where(
        row == 0,
        north * left,
        jnp.where(row == 1, north * right, jnp.where(row == 2, south * left, jnp.where(row == 3, south * right, 0.0))),
    )
    four = mm(four, t.wave_weight)
    ends = t.ends
    first, last = ends[0:1], ends[1:2]
    north_row = own_before + PRECOND_T * (first * four[0:1] + last * four[1:2])
    south_row = own_after + PRECOND_T * (first * four[2:3] + last * four[3:4])
    place = iota((rows, cols), 0)
    loaded = q_mixed + PRECOND_T * (
        jnp.where(place == 0, north_row, 0.0)
        + jnp.where(place == rows - 1, south_row, 0.0)
        + left_col * first
        + right_col * last
    )
    sine_rows = t.sine_rows
    inside = mm_left(sine_rows, mm_left(sine_rows, loaded) * t.weight[...])
    pad = jnp.zeros((6, cols), F32)
    whole = mm(jnp.concatenate([inside, north_row, south_row, pad], axis=0), t.sine_cols)
    return whole[:rows], whole[rows : rows + 1], whole[rows + 1 : rows + 2], left_col, right_col


class Operands:
    def __init__(self, copies, buffers, early):
        self._copies, self._buffers, self._early = copies, buffers, early

    def __getattr__(self, name):
        if name in self._copies:
            names = list(self._copies)
            for other in names if name not in names[: self._early] else names[: self._early]:
                self._copies.pop(other).wait()
            self._early = 0
        return self._buffers[name]


class Held:
    def __init__(self, array):
        self.array = array


def call(body, ins, outs, keep=(), early=0):
    names, results = list(ins), list(outs) + list(keep)
    arrays, parts, copied = [], [], []
    for place, value in enumerate(ins.values()):
        held = isinstance(value, Held)
        array, part = (value.array, None) if held else value if isinstance(value, tuple) else (value, ())
        arrays.append(pltpu.with_memory_space_constraint(array, pltpu.VMEM if held else pltpu.HBM))
        parts.append(part)
        if part is not None:
            copied.append(place)
    kinds, sent = [], []
    for place, value in enumerate(outs.values()):
        if isinstance(value, Held):
            kinds.append((value.array, F32))
        else:
            kinds.append(value if isinstance(value[-1], type(F32)) else (value, F32))
            sent.append(place)
    spaces = [
        [pl.BlockSpec(memory_space=pltpu.VMEM if isinstance(value, Held) else pltpu.HBM) for value in side.values()]
        for side in (ins, outs)
    ]
    spaces[1] += [pl.BlockSpec(memory_space=pltpu.VMEM)] * len(keep)

    def shape_of(array, part):
        if isinstance(part, str):
            return array.shape[1:]
        return tuple(len(range(*cut.indices(size))) for cut, size in zip(part, array.shape)) + array.shape[len(part) :]

    def kernel(*refs):
        given, refs = refs[: len(names)], refs[len(names) :]
        made, refs = refs[: len(results)], refs[len(results) :]
        in_sems, out_sems = refs[-2:]
        copies, buffers = {}, dict(zip(names, given))
        for slot, place in enumerate(copied):
            part = parts[place]
            origin = given[place].at[lax.axis_index(part) if isinstance(part, str) else part] if part else given[place]
            name = names[place]
            buffers[name] = made[results.index(name, len(outs))] if name in keep else refs[slot]
            copies[name] = pltpu.make_async_copy(origin, buffers[name], in_sems.at[slot])
            copies[name].start()
        built = list(made)
        for slot, place in enumerate(sent):
            built[place] = refs[len(copied) + slot]
        going = []

        def done(*which):
            for buffer in which:
                for slot, place in enumerate(sent):
                    if built[place] is buffer:
                        going.append(pltpu.make_async_copy(buffer, made[place], out_sems.at[slot]))
                        going[-1].start()

        get = Operands(copies, buffers, early)
        body(get, SimpleNamespace(**dict(zip(results, built))), done)
        for place in copied:
            getattr(get, names[place])
        assert len(going) == len(sent)
        for copy in going:
            copy.wait()

    shapes = [(shape_of(arrays[place], parts[place]), arrays[place].dtype) for place in copied]
    kept = [shapes[copied.index(names.index(name))] for name in keep]
    scratch = [
        pltpu.VMEM(*((8, 128), F32) if names[place] in keep else shape) for place, shape in zip(copied, shapes)
    ]
    scratch += [pltpu.VMEM(*kinds[place]) for place in sent]
    scratch += [pltpu.SemaphoreType.DMA((max(1, len(some)),)) for some in (copied, sent)]
    made = pl.pallas_call(
        kernel,
        out_shape=[
            pltpu.VMEM(*kind) if isinstance(value, Held) else pltpu.HBM(*kind)
            for kind, value in zip(kinds, outs.values())
        ]
        + [pltpu.VMEM(*shape) for shape in kept],
        in_specs=spaces[0],
        out_specs=spaces[1],
        scratch_shapes=scratch,
        compiler_params=pltpu.CompilerParams(vmem_limit_bytes=VMEM_LIMIT),
    )(*arrays)
    return SimpleNamespace(**dict(zip(results, made)))


def shards(
    source,
    conductivity,
    leakance,
    storage,
    et_rate,
    zone_of_block,
    zone_recharge,
    zone_weight,
    pair_zones,
    pair_weight,
):
    slabs, groups = lax.axis_size("slab"), lax.axis_size("grp")
    layers, rows, cols = source.shape
    devices = slabs * groups
    zones = zone_weight.shape[0]
    tables = {name: jnp.asarray(table) for name, table in grid_tables(slabs, groups, rows, cols).items()}
    t = SimpleNamespace(**tables)
    t.own_columns, t.around = (t.own_columns, "grp"), (t.around, "slab")
    block_rows, block_cols = rows // 8, cols // 8
    blocks = block_rows * block_cols
    at_zones = 2 * cols
    at_sides = at_zones + blocks
    widths = (at_sides + 5 * 128, at_zones + zones + 2 * 128)
    area = (layers, rows, cols)

    def neighbours(near, far):
        across = [(i, i + 1) for i in range(1, slabs - 1, 2)]
        return (
            lax.ppermute(near, "slab", [(i, i ^ 1) for i in range(slabs)]),
            lax.ppermute(far, "slab", across + [(j, i) for i, j in across]),
        )

    def choose(near, far):
        odd = lax.axis_index("slab") % 2 == 1
        return jnp.where(odd, near, far), jnp.where(odd, far, near)

    def exchange(chunk):
        return lax.all_to_all(chunk, BOTH, split_axis=0, concat_axis=0, tiled=True)

    def start_body(get, out, done):
        ids = get.zone_of_block[...].astype(F32)
        ids = jnp.concatenate([ids, jnp.zeros((8 - block_rows, block_cols), F32)], axis=0)
        zone_line = to_line(mm_exact(ids, get.place[...]), block_cols)
        index = jnp.broadcast_to(zone_line, (8, blocks)).astype(jnp.int32)
        found = lookup(get.zone_recharge[...], index)[0:1]
        field = field_rows([(found, i) for i in range(block_rows)], get.down[...], block_cols)
        source_ref, rhs = get.source, out.rhs
        rhs[0] = source_ref[0] + spread_rows8(field, rows)
        for layer in range(1, layers):
            rhs[layer] = source_ref[layer]
        done(out.rhs)
        total = rhs[0]
        for layer in range(1, layers):
            total = total + rhs[layer]
        q_mixed = mm(total, get.sine_cols)
        out.q_mixed[...] = q_mixed
        done(out.q_mixed)
        cond, store, leak = get.conductivity, get.storage, get.leakance
        partial, edge_rows = out.partial, [[], []]
        for layer in range(layers):
            own = cond[layer]
            diagonal = store[layer] + 0.5 * (4.0 * own + stencil(own, 0.0, 0.0, 0.0, 0.0))
            if layer < layers - 1:
                diagonal = diagonal + leak[layer]
            if layer > 0:
                diagonal = diagonal + leak[layer - 1]
            if layer == 0:
                diagonal = diagonal + get.et_rate[...]
            partial[layer] = diagonal
            for end, row in enumerate((0, rows - 1)):
                edge_rows[end] += [own[row : row + 1], diagonal[row : row + 1], rhs[layer, row : row + 1]]
        first, last = [
            jnp.concatenate([rows_of[place] for kind in range(3) for place in range(kind, 3 * layers, 3)], axis=0)
            for rows_of in edge_rows
        ]
        out.near[...], out.far[...] = choose(first, last)
        done(out.partial, out.near, out.far)
        first, last, left, right = rings(q_mixed, get)
        sides = side_lanes([rhs[layer] for layer in range(layers)], (left, right))
        sides += side_lanes(
            [cond[layer] for layer in range(layers)], (partial[0, :, 0:1], partial[0, :, cols - 1 : cols])
        )
        west, east = side_lanes([partial[layer] for layer in range(1, layers)])
        both = jnp.where(iota((1, 128), 1) < 64, west, pltpu.roll(east, 64, 1))
        line = jnp.concatenate([first, last, zone_line, *sides, both], axis=1)
        out.chunk[...] = jnp.broadcast_to(line[None], out.chunk.shape)
        out.zone_line[...] = zone_line
        done(out.chunk)

    started = call(
        start_body,
        dict(
            zone_of_block=zone_of_block,
            zone_recharge=zone_recharge[None],
            place=t.place,
            down=t.down,
            source=source,
            sine_cols=t.sine_cols,
            conductivity=conductivity,
            storage=storage,
            leakance=leakance,
            et_rate=et_rate,
            sine_rows=t.sine_rows,
            weight=t.weight,
            ends=t.ends,
        ),
        dict(
            rhs=Held(area),
            q_mixed=Held((rows, cols)),
            partial=area,
            near=Held((3 * layers, cols)),
            far=Held((3 * layers, cols)),
            zone_line=Held((1, blocks)),
            chunk=(devices, 1, widths[0]),
        ),
        early=4,
    )
    rhs = started.rhs
    received = exchange(started.chunk)
    near, far = neighbours(started.near, started.far)

    def couple_body(get, out, done):
        ids, weights = get.pair_zones, get.pair_weight
        place = iota((zones, ids.shape[1]), 0)
        table = (place == ids[0:1]).astype(F32) - (place == ids[1:2]).astype(F32)
        matrix = mm_f32(table * weights[...], table, DIMS_T)
        own = iota((zones, zones), 0) == iota((zones, zones), 1)
        matrix = matrix + jnp.where(own, get.zone_weight[...], 0.0)
        out.couple[...] = (COUPLE * zones / (slabs * rows * groups * cols)) * matrix
        line = get.zone_line[...].astype(jnp.int32)
        out.hot[...] = (iota((zones, blocks), 0) == line).astype(F32).astype(BF16)
        done(out.couple, out.hot)

    coupling = call(
        couple_body,
        dict(pair_zones=pair_zones.T, pair_weight=pair_weight[None], zone_weight=zone_weight[None])
        | dict(zone_line=Held(started.zone_line)),
        dict(couple=(zones, zones), hot=((zones, blocks), BF16)),
    )
    couple, hot = coupling.couple, coupling.hot

    def step_body(number, get, out, done):
        coupled, final = number > 0, number == 2
        slab, group = lax.axis_index("slab"), lax.axis_index("grp")
        own = slab * groups + group
        has_north = (slab > 0).astype(F32)
        has_south = (slab < slabs - 1).astype(F32)
        has_west = (group > 0).astype(F32)
        has_east = (group < groups - 1).astype(F32)
        recv = get.received

        def of(shift, start):
            return recv[pl.ds(jnp.clip(own + shift, 0, devices - 1), 1), 0, start : start + 128]

        first_rows, last_rows = recv[:, 0, :cols], recv[:, 0, cols : 2 * cols]
        sides_at = at_sides if not coupled else at_zones + zones
        lane = iota((devices, 128), 1)
        edges = jnp.where(
            lane < rows,
            pltpu.roll(recv[:, 0, sides_at : sides_at + 128], rows, 1),
            pltpu.roll(recv[:, 0, sides_at + 128 : sides_at + 256], 2 * rows, 1),
        )
        edges = jnp.where(lane < 2 * rows, edges, 0.0)
        q_in = get.q_mixed[...]
        w_ref = get.w
        surface = w_ref[0]
        if coupled:
            totals = jnp.sum(recv[:, 0, at_zones : at_zones + zones], axis=0, keepdims=True)
            reply = mm_f32(jnp.broadcast_to(totals, (8, zones)), get.couple[...])[0:1]
            every = lookup(reply, get.zone_map[...].astype(jnp.int32))
            edges = edges + mm(every, get.coarse)
            share = 128 // block_cols
            inner = iota((devices, 128), 1) // block_cols
            slabs_of = [
                jnp.where(inner == i % share, every[:, 128 * (i // share) : 128 * (i // share + 1)], 0.0)
                for i in range(block_rows)
            ]
            modes_of = mm(jnp.concatenate(slabs_of, axis=0), get.up_modes)
            device = iota(first_rows.shape, 0)
            modes = []
            for i in range(block_rows):
                part = modes_of[devices * i : devices * (i + 1)]
                first_rows = first_rows + get.coarse_rows[i : i + 1] * part
                last_rows = last_rows + get.coarse_rows[block_rows + i : block_rows + i + 1] * part
                modes.append(jnp.sum(jnp.where(device == own, part, 0.0), axis=0, keepdims=True))
            modes = jnp.concatenate(modes, axis=0)
            device = iota(every.shape, 0)
            line_of = lambda shift: jnp.sum(
                jnp.where(device == own + shift, every, 0.0), axis=0, keepdims=True
            )
            mine = line_of(0)
            wanted = [(mine, i) for i in range(block_rows)]
            wanted += [(line_of(-groups), block_rows - 1), (line_of(groups), 0)]
            field = field_rows(wanted, get.down[...], block_cols)
            q_in = q_in + spread_rows8(modes, rows)
            surface = surface + spread_rows8(field, rows)
            column = iota((rows, blocks), 1)
            base = block_cols * (iota((rows, blocks), 0) // 8)
            west_value = jnp.sum(
                jnp.where(column == base + block_cols - 1, line_of(-1), 0.0), axis=1, keepdims=True
            )
            east_value = jnp.sum(jnp.where(column == base, line_of(1), 0.0), axis=1, keepdims=True)
        if final:
            out.w[0] = surface
            for layer in range(1, layers):
                out.w[layer] = w_ref[layer]
            done(out.w)
        elif coupled:
            out.w[0] = surface
            for layer in range(1, layers):
                out.w[layer] = w_ref[layer]
            done(out.w)
        s, s_north, s_south, s_west, s_east = smooth(
            first_rows, last_rows, edges, q_in, slab, group, groups, get
        )
        cond, leak = get.conductivity, get.leakance
        north_ref, south_ref = choose(get.near[...], get.far[...])
        row, col = iota((rows, cols), 0), iota((rows, cols), 1)
        if coupled:
            cond_north, cond_south = get.cond_north, get.cond_south
            sides = get.sides
            lanes = [of(-1, sides_at + 128), of(1, sides_at)]
            diagonal_ref, inverse_ref = get.diagonal, get.inverse
            beside = get.beside
        else:
            cond_north, cond_south = north_ref, south_ref
            lanes = [of(-1, sides_at + 128), of(1, sides_at)]
            lanes += [of(-1, sides_at + 384) * has_west, of(1, sides_at + 256) * has_east]
            lanes += [of(-1, sides_at + 512), of(1, sides_at + 512)]
            diagonal_ref, inverse_ref, sides, beside = out.diagonal, out.inverse, out.sides, out.beside
        turned = jnp.concatenate(lanes + [jnp.zeros((128 - len(lanes), 128), F32)], axis=0).T
        if not coupled:
            corner = [
                of(-groups - 1, sides_at + 384) * (has_north * has_west),
                of(-groups + 1, sides_at + 256) * (has_north * has_east),
                of(groups - 1, sides_at + 384) * (has_south * has_west),
                of(groups + 1, sides_at + 256) * (has_south * has_east),
            ]
            ghosts = []
            partial = get.partial
            line_col, line_row = iota((1, cols), 1), iota((rows, 1), 0)
            for layer in range(layers):
                c_north, c_south = north_ref[layer : layer + 1], south_ref[layer : layer + 1]
                c_west = turned[rows * layer : rows * (layer + 1), 2:3]
                c_east = turned[rows * layer : rows * (layer + 1), 3:4]
                both = jnp.where(lane[:rows] == 0, c_west, jnp.where(lane[:rows] == 1, c_east, 0.0))
                sides[layer] = both
                diagonal = partial[layer] + 0.5 * (
                    jnp.where(row == 0, c_north, 0.0)
                    + jnp.where(row == rows - 1, c_south, 0.0)
                    + jnp.where(col == 0, c_west, 0.0)
                    + jnp.where(col == cols - 1, c_east, 0.0)
                )
                diagonal_ref[layer] = diagonal
                inverse_ref[layer] = 1.0 / diagonal
                start, end = rows * layer, rows * layer + rows - 1
                nw, ne = corner[0][:, end : end + 1], corner[1][:, end : end + 1]
                sw, se = corner[2][:, start : start + 1], corner[3][:, start : start + 1]
                own_cond = cond[layer]
                d_north = north_ref[layers + layer : layers + layer + 1] + 0.5 * (
                    own_cond[0:1] + jnp.where(line_col == 0, nw, jnp.where(line_col == cols - 1, ne, 0.0))
                )
                d_south = south_ref[layers + layer : layers + layer + 1] + 0.5 * (
                    own_cond[rows - 1 : rows]
                    + jnp.where(line_col == 0, sw, jnp.where(line_col == cols - 1, se, 0.0))
                )
                if layer == 0:
                    west, east = turned[3 * rows : 4 * rows, 2:3], turned[3 * rows : 4 * rows, 3:4]
                else:
                    west = turned[64 + rows * (layer - 1) : 64 + rows * layer, 4:5]
                    east = turned[rows * (layer - 1) : rows * layer, 5:6]
                d_west = west + 0.5 * (
                    own_cond[:, 0:1] + jnp.where(line_row == 0, nw, jnp.where(line_row == rows - 1, sw, 0.0))
                )
                d_east = east + 0.5 * (
                    own_cond[:, cols - 1 : cols]
                    + jnp.where(line_row == 0, ne, jnp.where(line_row == rows - 1, se, 0.0))
                )
                ghosts.append((1.0 / d_north, 1.0 / d_south, 1.0 / d_west, 1.0 / d_east))
            sides[layers] = jnp.where(lane[:rows] == 0, ghosts[0][2], jnp.where(lane[:rows] == 1, ghosts[0][3], 0.0))
            beside[0:1] = ghosts[0][0]
            beside[1:2] = ghosts[0][1]
            out.cond_north[...], out.cond_south[...] = north_ref[:layers], south_ref[:layers]
            out.zone_map[...] = recv[:, 0, at_zones:at_sides]
            done(out.diagonal, out.inverse, out.sides, out.beside, out.cond_north, out.cond_south, out.zone_map)
        v_out, image_out = out.v, out.image
        fields, outside = [], []
        for layer in range(layers):
            value = (surface if layer == 0 else w_ref[layer]) * inverse_ref[layer] + s
            v_out[layer] = value
            fields.append(value)
            west = turned[rows * layer : rows * (layer + 1), 0:1]
            east = turned[rows * layer : rows * (layer + 1), 1:2]
            if coupled:
                north, south = north_ref[layer : layer + 1], south_ref[layer : layer + 1]
                if layer == 0:
                    north = north + beside[0:1] * field[block_rows : block_rows + 1]
                    south = south + beside[1:2] * field[block_rows + 1 : block_rows + 2]
                    west = west + sides[layers, :, 0:1] * west_value
                    east = east + sides[layers, :, 1:2] * east_value
            else:
                near = ghosts[layer]
                place = 2 * layers + layer
                north, south = north_ref[place : place + 1] * near[0], south_ref[place : place + 1] * near[1]
                west, east = west * near[2], east * near[3]
            outside.append(
                (
                    (north + s_north) * has_north,
                    (south + s_south) * has_south,
                    (west + s_west) * has_west,
                    (east + s_east) * has_east,
                )
            )
        done(out.v)
        images = []
        for layer in range(layers):
            value, own_cond = fields[layer], cond[layer]
            north, south, west, east = outside[layer]
            plain = stencil(value, north, south, west, east)
            carried = stencil(
                value * own_cond,
                north * cond_north[layer : layer + 1],
                south * cond_south[layer : layer + 1],
                west * sides[layer, :, 0:1],
                east * sides[layer, :, 1:2],
            )
            image = diagonal_ref[layer] * value - 0.5 * (own_cond * plain + carried)
            if layer < layers - 1:
                image = image - leak[layer] * fields[layer + 1]
            if layer > 0:
                image = image - leak[layer - 1] * fields[layer - 1]
            image_out[layer] = image
            images.append(image)
        done(out.image)
        totals = zone_totals(fields[0], get.hot[...], get.down[...])
        if final:
            rhs_ref, v0_ref, v1_ref, w0_ref = get.rhs, get.v0, get.v1, get.w0

            def dot(left, right):
                total = left[0] * right[0]
                for layer in range(1, layers):
                    total = total + left[layer] * right[layer]
                return jnp.sum(jnp.sum(total, axis=0, keepdims=True), axis=1, keepdims=True)

            w1 = [surface] + [w_ref[layer] for layer in range(1, layers)]
            products = [
                dot(v0_ref, w0_ref), dot(v0_ref, w1), dot(v1_ref, w1), dot(fields, w0_ref), dot(fields, w1),
                dot(fields, images), dot(v0_ref, rhs_ref), dot(v1_ref, rhs_ref), dot(fields, rhs_ref),
            ]
            packed = jnp.zeros((1, 128), F32)
            for place, value in enumerate(products):
                packed = jnp.where(iota((1, 128), 1) == place, value, packed)
            line = jnp.concatenate([totals, packed], axis=1)
        else:
            depth = images[0]
            for layer in range(1, layers):
                depth = depth + images[layer]
            q_next = mm(depth, get.sine_cols)
            out.q_mixed[...] = q_next
            done(out.q_mixed)
            scaled = [images[layer] * inverse_ref[layer] for layer in range(layers)]
            out.near[...], out.far[...] = choose(
                jnp.concatenate([part[0:1] for part in scaled], axis=0),
                jnp.concatenate([part[rows - 1 : rows] for part in scaled], axis=0),
            )
            done(out.near, out.far)
            first, last, left, right = rings(q_next, get)
            west, east = side_lanes(scaled, (left, right))
            line = jnp.concatenate([first, last, totals, west, east], axis=1)
        out.chunk[...] = jnp.broadcast_to(line[None], out.chunk.shape)
        done(out.chunk)

    tail_width = zones + 128
    shared = {}

    def step(number, received, near, far, more, keep=()):
        ins = dict(received=Held(received))
        if number > 0:
            ins |= dict(couple=couple, zone_map=one.zone_map, coarse=t.coarse, up_modes=t.up_modes)
            ins |= dict(coarse_rows=t.coarse_rows)
        ins |= dict(row_chain=t.row_chain, answer=t.answer, down=t.down, waves=t.waves, own_columns=t.own_columns)
        ins |= dict(around=t.around, wave_weight=t.wave_weight, ends=t.ends, sine_rows=t.sine_rows, weight=t.weight)
        ins |= dict(sine_cols=t.sine_cols, near=Held(near), far=Held(far), conductivity=conductivity, leakance=leakance, hot=hot)
        ins |= shared | more
        ins |= {name: Held(getattr(one, name)) for name in steady} if number else {}
        if number == 2:
            outs = dict(v=Held(area), w=Held(area), image=Held(area))
            outs |= dict(chunk=(devices, 1, tail_width))
        else:
            outs = dict(v=area, image=Held(area), q_mixed=Held((rows, cols)))
            outs |= dict(near=Held((layers, cols)), far=Held((layers, cols)))
            outs |= dict(chunk=(devices, 1, widths[1]))
        if number == 0:
            outs |= dict(diagonal=area, inverse=area, sides=(layers + 1, rows, 128), beside=(2, cols))
            outs |= dict(cond_north=(layers, cols), cond_south=(layers, cols), zone_map=(devices, blocks))
        elif number == 1:
            outs |= dict(w=area)
        return call(lambda get, out, done: step_body(number, get, out, done), ins, outs, keep, early=5)

    q_mixed = Held(started.q_mixed)
    steady = tuple(dict(sine_cols=0, wave_weight=0))
    one = step(0, received, near, far, dict(partial=started.partial, q_mixed=q_mixed, w=Held(rhs)), steady)
    shared |= dict(diagonal=one.diagonal, inverse=one.inverse, sides=one.sides, beside=one.beside)
    shared |= dict(cond_north=one.cond_north, cond_south=one.cond_south)
    received = exchange(one.chunk)
    near, far = neighbours(one.near, one.far)
    two = step(1, received, near, far, dict(q_mixed=Held(one.q_mixed), w=Held(one.image)))
    received = exchange(two.chunk)
    near, far = neighbours(two.near, two.far)
    more = dict(rhs=Held(rhs), v0=one.v, v1=two.v, w0=two.w)
    after = dict(q_mixed=Held(two.q_mixed), w=Held(two.image)) | more
    last_needs = tuple(dict(v0=0, v1=0, w0=0, couple=0, down=0))
    three = step(2, received, near, far, after, last_needs)
    received = exchange(three.chunk)

    def finish_body(get, out, done):
        sums = jnp.sum(get.received[:, 0, :], axis=0, keepdims=True)
        totals = sums[:, :zones]
        reply = mm_f32(jnp.broadcast_to(totals, (8, zones)), get.couple[...])
        zone_line = get.zone_line[...]
        index = jnp.broadcast_to(zone_line, (8, blocks)).astype(jnp.int32)
        found = lookup(reply[0:1], index)[0:1]
        field = field_rows([(found, i) for i in range(block_rows)], get.down[...], block_cols)
        coupled = spread_rows8(field, rows)
        a00, a01, a11, a02, a12, a22, h0, h1, h2 = [sums[:, zones + i : zones + i + 1] for i in range(9)]
        a22 = a22 + jnp.sum(totals * reply[0:1], axis=1, keepdims=True)
        l10, l20 = a01 / a00, a02 / a00
        d1 = a11 - l10 * a01
        l21 = (a12 - l10 * a02) / d1
        d2 = a22 - l20 * a02 - l21 * (a12 - l10 * a02)
        y1 = h1 - l10 * h0
        y2 = h2 - l20 * h0 - l21 * y1
        c2 = y2 / d2
        c1 = y1 / d1 - l21 * c2
        c0 = h0 / a00 - l10 * c1 - l20 * c2
        v0, v1, v2, w0, w1, w2 = get.v0, get.v1, get.v2, get.w0, get.w1, get.w2
        rhs_ref = get.rhs
        for layer in range(layers):
            last = w2[layer] + coupled if layer == 0 else w2[layer]
            out.solution[layer] = c0 * v0[layer] + c1 * v1[layer] + c2 * v2[layer]
            out.residual[layer] = rhs_ref[layer] - c0 * w0[layer] - c1 * w1[layer] - c2 * last
        done(out.solution, out.residual)

    needs = {name: Held(getattr(three, name)) for name in last_needs}
    for name, array in dict(couple=couple, down=t.down, v0=one.v, v1=two.v, w0=two.w).items():
        needs.setdefault(name, array)
    ended = call(
        finish_body,
        dict(received=Held(received), zone_line=Held(started.zone_line), rhs=Held(rhs))
        | needs
        | dict(v2=Held(three.v), w1=Held(three.w), w2=Held(three.image)),
        dict(solution=area, residual=area),
    )
    return ended.solution, ended.residual


def solution(mesh):
    placed = (
        P(None, "slab", "grp"),
        P(None, "slab", "grp"),
        P(None, "slab", "grp"),
        P(None, "slab", "grp"),
        P("slab", "grp"),
        P("slab", "grp"),
        P(),
        P(),
        P(),
        P(),
    )
    return jax.shard_map(
        shards,
        mesh=mesh,
        in_specs=placed,
        out_specs=(P(None, "slab", "grp"), P(None, "slab", "grp")),
        check_vma=False,
    )
```
